32 devices in a mesh: grp: 2 (over x), blk: 16 (over z, y, core).
Axes of the slice: x: 2, y: 2, z: 4, core: 2. Of those that a mesh axis runs over, the one named last changes fastest.
Arguments:
- theta: bfloat16 [32, 1024, 128], P(('grp', 'blk')), parts along dimension 0, may hold values from -6 to 6
- trial: bfloat16 [2048, 128], P('grp'), parts along dimension 0, may hold values from -0.5 to 0.5
- chol: bfloat16 [64, 128, 16384], P(('grp', 'blk')), parts along dimension 0, may hold values from -0.009765625 to 0.009765625
- fields: float32 [32, 128], P(('grp', 'blk')), parts along dimension 0, may hold values from -6 to 6
- tile_info: int32 [6, 32], P('grp'), parts along dimension 0, may hold values from 0 to 7, as said below
- tile_count: int32 [32], P('grp'), parts along dimension 0, may hold values from 0 to 2
- block_size: int32 [16], P('grp'), parts along dimension 0, may hold values from 96 to 128
Outputs:
- propagated: bfloat16 [32, 1024, 128], P(('grp', 'blk')), parts along dimension 0
- force_bias: float32 [32, 128], P(('grp', 'blk')), parts along dimension 0
The draws below stay inside these ranges and needn't reach their ends.
There are 2 independent parts, one for each index of `grp`. The reference program is written for one: setup_inputs(seed, part) draws one part's arguments, and reference() takes and returns one part's arrays. A program takes and returns all parts, laid end to end along the dimension named above; each array names one. Nothing has to cross between parts.
Inputs may be any that keep to these rules, and one draw needn't show every extreme that they name: `tile_info`: every pair of blocks (P, Q) with |P - Q| <= 1 and every vector range below 1 stand in exactly one live slot; live slots of an owner come first; unused slots hold zeros.
All inputs are finite; a program needn't handle non-finite values.
Results may differ from the reference program's by a relative error of at most 0.0045.
Values may be sent and summed in bfloat16 or wider, within the bound.
No kernel may reach another device: no remote copies, remote signals or barrier semaphores. Data moves between devices by JAX's collectives and lax.ppermute only.
A program may use at most 128 MiB of HBM per device.

```python
import jax
import jax.numpy as jnp
from jax import lax

BS = 128
NBLOCK = 8
NOCC = 128
GS = 128
TMAX = 2
NORB = 1024
NPAIR = 22
NSLAB = 1
NCHOL = 128
WALKERS = 16
N_BLK = 16


def tile_layout(key):
    layout_key = jax.random.fold_in(key, 11)
    slot_total = N_BLK * TMAX
    tile_total = NPAIR * NSLAB
    shuffled = jax.random.permutation(layout_key, slot_total).astype(jnp.int32).reshape(N_BLK, TMAX)
    live_slots = shuffled < tile_total
    ordering = jnp.argsort(jnp.where(live_slots, 0, 1).astype(jnp.int32), axis=1, stable=True)
    packed = jnp.take_along_axis(shuffled, ordering, axis=1)
    alive = jnp.take_along_axis(live_slots, ordering, axis=1)
    live_count = jnp.sum(alive.astype(jnp.int32), axis=1).astype(jnp.int32)
    alive_flat = alive.reshape(slot_total)
    tile_ids = jnp.where(alive_flat, packed.reshape(slot_total), 0)
    pair_ids = tile_ids % NPAIR
    slab_ids = tile_ids // NPAIR
    upper_off = pair_ids - NBLOCK
    lower_off = pair_ids - (2 * NBLOCK - 1)
    row_ids = jnp.where(pair_ids < NBLOCK, pair_ids, jnp.where(lower_off < 0, upper_off, lower_off + 1))
    col_ids = jnp.where(pair_ids < NBLOCK, pair_ids, jnp.where(lower_off < 0, upper_off + 1, lower_off))
    live_int = alive_flat.astype(jnp.int32)
    tile_table = jnp.stack([row_ids * live_int, col_ids * live_int, slab_ids * live_int]).astype(jnp.int32)
    return (tile_table, live_count)


def draw_tile_info(key, part):
    return tile_layout(key)[0]


def draw_tile_count(key, part):
    return tile_layout(key)[1]


def draw_block_size(key, part):
    size_key = jax.random.fold_in(key, 23)
    place_key = jax.random.fold_in(key, 29)
    sizes = jax.random.randint(size_key, (NBLOCK,), BS - BS // 4, BS).astype(jnp.int32)
    chosen = jax.random.randint(place_key, (), 0, NBLOCK).astype(jnp.int32)
    return jnp.where(jnp.arange(NBLOCK, dtype=jnp.int32) == chosen, BS, sizes).astype(jnp.int32)


def block_levels(key, dims, split, smallest, largest):
    loudness, own = 1.0, jax.random.fold_in(key, 6)
    for dim, blocks in split:
        draws = jnp.exp(jax.random.uniform(jax.random.fold_in(own, dim), (blocks,), jnp.float32, smallest / len(split), largest / len(split)))
        loudness = loudness * jnp.repeat(draws, dims[dim] // blocks).reshape([-1 if axis == dim else 1 for axis in range(len(dims))])
    return loudness


def centred(own_key, extent, width, limit, pieces=(), kind=jnp.bfloat16):
    level = block_levels(own_key, extent, pieces, -0.22, 0.18) if pieces else 1.0
    drawn = jax.random.normal(own_key, extent, jnp.float32) * width * level
    return jnp.minimum(jnp.maximum(drawn, -limit), limit).astype(kind)


def setup_inputs(seed: int = 0, part: int = 0) -> dict:
    key_list = jax.random.split(jax.random.key(seed), 8)
    own_keys = jax.random.split(jax.random.fold_in(key_list[7], part), 8)
    theta = centred(own_keys[0], (WALKERS, NORB, NOCC), 1.0, 6.0, ((0, 16),))
    trial = centred(own_keys[1], (NORB, NOCC), NOCC ** -0.5, 0.5)
    chol = centred(own_keys[2], (N_BLK * TMAX, GS, BS * BS), (NPAIR * BS * BS) ** -0.5, 0.009765625, ((0, 16),))
    fields = centred(own_keys[3], (WALKERS, NCHOL), 1.0, 6.0, ((0, 16),), jnp.float32)
    tile_info = draw_tile_info(jax.random.fold_in(jax.random.fold_in(key_list[7], part), 71), part)
    tile_count = draw_tile_count(jax.random.fold_in(jax.random.fold_in(key_list[7], part), 71), part)
    block_size = draw_block_size(jax.random.fold_in(jax.random.fold_in(key_list[7], part), 71), part)
    return {"theta": theta, "trial": trial, "chol": chol, "fields": fields, "tile_info": tile_info, "tile_count": tile_count, "block_size": block_size}


step_root = 0.25


def reference(theta, trial, chol, fields, tile_info, tile_count, block_size):
    walkers = theta.shape[0]
    slot_total = chol.shape[0]
    zero_index = jnp.zeros((), jnp.int32)
    rows_valid = (jnp.arange(BS, dtype=jnp.int32)[None, :] < block_size[:, None]).astype(jnp.float32)
    slot_ids = jnp.arange(slot_total, dtype=jnp.int32)
    slot_live = ((slot_ids % TMAX) < tile_count[slot_ids // TMAX]).astype(jnp.float32)
    theta_wide = theta.astype(jnp.float32)
    trial_wide = trial.astype(jnp.float32)

    def tile_parts(slot_index):
        row_block = tile_info[0, slot_index]
        col_block = tile_info[1, slot_index]
        slab_index = tile_info[2, slot_index]
        trial_rows = lax.dynamic_slice(trial_wide, (row_block * BS, zero_index), (BS, NOCC))
        theta_rows = lax.dynamic_slice(theta_wide, (zero_index, col_block * BS, zero_index), (walkers, BS, NOCC))
        valid_mask = rows_valid[row_block][:, None] * rows_valid[col_block][None, :] * slot_live[slot_index]
        cholesky_tile = chol[slot_index].astype(jnp.float32)
        return row_block, slab_index, trial_rows, theta_rows, valid_mask, cholesky_tile

    def bias_step(slot_index, bias_total):
        parts = tile_parts(slot_index)
        slab_index, trial_rows, theta_rows, valid_mask, cholesky_tile = parts[1], parts[2], parts[3], parts[4], parts[5]
        green_block = (jnp.einsum("pk,wqk->wpq", trial_rows, theta_rows) * valid_mask).astype(jnp.bfloat16)
        bias_term = jnp.einsum("wf,gf->wg", green_block.reshape(walkers, BS * BS).astype(jnp.float32), cholesky_tile)
        current = lax.dynamic_slice(bias_total, (zero_index, slab_index * GS), (walkers, GS))
        return lax.dynamic_update_slice(bias_total, current + bias_term, (zero_index, slab_index * GS))

    force_bias = lax.fori_loop(jnp.int32(0), jnp.int32(slot_total), bias_step,
                               jnp.zeros((walkers, fields.shape[1]), jnp.float32))
    shifted = (fields - force_bias).astype(jnp.bfloat16)
    shifted_wide = shifted.astype(jnp.float32)

    def update_step(slot_index, update):
        row_block, slab_index, trial_rows, theta_rows, valid_mask, cholesky_tile = tile_parts(slot_index)
        field_slab = lax.dynamic_slice(shifted_wide, (zero_index, slab_index * GS), (walkers, GS))
        operator_block = ((jnp.einsum("wg,gf->wf", field_slab, cholesky_tile) * step_root).reshape(walkers, BS, BS) * valid_mask).astype(jnp.bfloat16)
        contribution = jnp.einsum("wpq,wqk->wpk", operator_block.astype(jnp.float32), theta_rows)
        current = lax.dynamic_slice(update, (zero_index, row_block * BS, zero_index), (walkers, BS, NOCC))
        return lax.dynamic_update_slice(update, current + contribution, (zero_index, row_block * BS, zero_index))

    update = lax.fori_loop(jnp.int32(0), jnp.int32(slot_total), update_step, jnp.zeros(theta.shape, jnp.float32))
    propagated = (theta_wide + update).astype(jnp.bfloat16)
    return (propagated, force_bias)
```

```python
import functools

import jax
import jax.numpy as jnp
from jax import lax
from jax.experimental import pallas as pl
from jax.experimental.pallas import tpu as pltpu
from jax.sharding import PartitionSpec as P

STEP_ROOT = 0.25
PIECES = 8
F32 = jnp.float32
BF16 = jnp.bfloat16
LIMIT = 48 * 1024 * 1024
VMEM = pl.BlockSpec(memory_space=pltpu.VMEM)
SMEM = pl.BlockSpec(memory_space=pltpu.SMEM)
ANY = pl.BlockSpec(memory_space=pl.ANY)
NT = (((1,), (1,)), ((), ()))


def pick_kernel(info_ref, theta_ref, out_ref, sem):
    owners, walk, slots = out_ref.shape[:3]
    for o in range(owners):
        for j in range(slots):
            block = info_ref[1, o * slots + j]
            for w in range(walk):
                pltpu.make_async_copy(theta_ref.at[w, block], out_ref.at[o, w, j], sem).start()
    pltpu.make_async_copy(out_ref, out_ref, sem).wait()


def tile_pieces(chol_ref, tile_ref, sems, slot):
    width = chol_ref.shape[2] // PIECES
    return [
        pltpu.make_async_copy(
            chol_ref.at[slot, :, pl.ds(c * width, width)],
            tile_ref.at[slot, :, pl.ds(c * width, width)],
            sems.at[slot, c],
        )
        for c in range(PIECES)
    ]


def start_tiles(chol_ref, tile_ref, sems, live):
    for slot in range(chol_ref.shape[0]):

        @pl.when(slot < live)
        def _():
            for copy in tile_pieces(chol_ref, tile_ref, sems, slot):
                copy.start()


def block_mask(size_ref, row_block, col_block, bs):
    rows = lax.broadcasted_iota(jnp.int32, (bs, bs), 0) < size_ref[row_block]
    cols = lax.broadcasted_iota(jnp.int32, (bs, bs), 1) < size_ref[col_block]
    return rows & cols


def bias_kernel(
    spread, info_ref, count_ref, size_ref, recv_ref, trial_ref, fields_ref, chol_ref,
    out_ref, tile_ref, green_ref, bias_ref, sems,
):
    owners, walk, slots, bs, _ = recv_ref.shape
    walkers = owners * walk
    me = lax.axis_index("blk")
    live = count_ref[me]
    start_tiles(chol_ref, tile_ref, sems, live)
    bias_ref[...] = jnp.zeros_like(bias_ref)
    for slot in range(slots):

        @pl.when(slot < live)
        def _(slot=slot):
            row_block = info_ref[0, me * slots + slot]
            col_block = info_ref[1, me * slots + slot]
            trial_rows = trial_ref[pl.ds(pl.multiple_of(row_block * bs, bs), bs), :]
            mask = block_mask(size_ref, row_block, col_block, bs)

            def one(w, carry):
                block = recv_ref[w // walk, w % walk, slot]
                green = lax.dot_general(trial_rows, block, NT, preferred_element_type=F32)
                green_ref[pl.ds(w, bs, stride=walkers), :] = jnp.where(mask, green, 0.0)
                return carry

            lax.fori_loop(0, walkers, one, 0, unroll=min(walkers, 16))
            per = bs // PIECES
            for c, copy in enumerate(tile_pieces(chol_ref, tile_ref, sems, slot)):
                copy.wait()
                base = c * per * walkers
                left = jnp.concatenate(
                    [
                        green_ref[pl.ds(base + p * walkers, walkers), :].astype(BF16)
                        for p in range(per)
                    ],
                    axis=1,
                )
                right = tile_ref[slot, :, pl.ds(c * per * bs, per * bs)]
                bias_ref[slot] += lax.dot_general(left, right, NT, preferred_element_type=F32)

    if spread:
        total = sum(bias_ref[slot] for slot in range(slots))
        for o in range(owners):
            out_ref[o, :walkers, :] = total
            out_ref[o, pl.ds(walkers, 8), :] = jnp.broadcast_to(fields_ref[...], (8, fields_ref.shape[1]))
    else:
        out_ref[...] = bias_ref[...]


def operator_kernel(
    spread, info_ref, count_ref, size_ref, bias_ref, fields_ref, chol_ref,
    out_ref, own_ref, tile_ref, shifted_ref, oper_ref, sems,
):
    owners, walk, slots, bs, _ = out_ref.shape
    walkers = owners * walk
    gs = chol_ref.shape[1]
    me = lax.axis_index("blk")
    live = count_ref[me]
    start_tiles(chol_ref, tile_ref, sems, live)
    if spread:
        rows = walkers + 8
        bias = sum(bias_ref[pl.ds(o * rows, walkers), :] for o in range(owners))
        fields = bias_ref[pl.ds(walkers, owners, stride=rows), :]
        shifted_ref[...] = bias
        own_ref[...] = shifted_ref[pl.ds(me, 1), :]
    else:
        bias = bias_ref[...]
        fields = fields_ref[...]
        own_ref[...] = bias_ref[pl.ds(me * walk, walk), :]
    shifted_ref[...] = (fields - bias)
    for slot in range(slots):

        @pl.when(slot < live)
        def _(slot=slot):
            row_block = info_ref[0, me * slots + slot]
            col_block = info_ref[1, me * slots + slot]
            slab = info_ref[2, me * slots + slot]
            mask = block_mask(size_ref, row_block, col_block, bs)
            left = shifted_ref[:, pl.ds(pl.multiple_of(slab * gs, gs), gs)].astype(BF16)
            per = bs // PIECES
            for c, copy in enumerate(tile_pieces(chol_ref, tile_ref, sems, slot)):
                copy.wait()
                right = tile_ref[slot, :, pl.ds(c * per * bs, per * bs)]
                oper = jnp.dot(left, right, preferred_element_type=F32) * STEP_ROOT
                for p in range(per):
                    oper_ref[pl.ds(c * per + p, walkers, stride=bs), :] = oper[:, p * bs : (p + 1) * bs]

            def one(w, carry):
                block = oper_ref[pl.ds(pl.multiple_of(w * bs, bs), bs), :]
                out_ref[w // walk, w % walk, slot] = jnp.where(mask, block, 0.0).astype(BF16)
                return carry

            lax.fori_loop(0, walkers, one, 0, unroll=min(walkers, 16))

        @pl.when(slot >= live)
        def _(slot=slot):
            def one(w, carry):
                out_ref[w // walk, w % walk, slot] = jnp.zeros((bs, bs), BF16)
                return carry

            lax.fori_loop(0, walkers, one, 0, unroll=min(walkers, 16))


def update_kernel(info_ref, count_ref, theta_ref, oper_ref, out_ref, where_ref):
    owners, walk, slots, bs, _ = oper_ref.shape
    blocks = theta_ref.shape[1]
    slabs = where_ref.shape[0] // (3 * blocks)
    for o in range(owners):
        live = count_ref[o]
        for j in range(slots):

            @pl.when(j < live)
            def _(s=o * slots + j):
                row_block = info_ref[0, s]
                side = info_ref[1, s] - row_block + 1
                where_ref[(info_ref[2, s] * blocks + row_block) * 3 + side] = jnp.int32(s)

    for w in range(walk):
        for row_block in range(blocks):
            total = theta_ref[w, row_block].astype(F32)
            for col_block in range(max(row_block - 1, 0), min(row_block + 2, blocks)):
                for slab in range(slabs):
                    s = where_ref[(slab * blocks + row_block) * 3 + col_block - row_block + 1]
                    total += jnp.dot(
                        oper_ref[s // slots, w, s % slots], theta_ref[w, col_block],
                        preferred_element_type=F32,
                    )
            out_ref[w, row_block] = total.astype(BF16)


def per_device(theta, trial, chol, fields, tile_info, tile_count, block_size):
    owners = lax.axis_size("blk")
    walk, norb, nocc = theta.shape
    walkers = walk * owners
    slots, gs, _ = chol.shape
    nchol = fields.shape[1]
    blocks = block_size.shape[0]
    bs = norb // blocks
    slabs = nchol // gs
    spread = slabs == 1 and walk == 1
    params = pltpu.CompilerParams(vmem_limit_bytes=LIMIT)
    theta_blocks = theta.reshape(walk, blocks, bs, nocc)

    outgoing = pl.pallas_call(
        pick_kernel,
        out_shape=jax.ShapeDtypeStruct((owners, walk, slots, bs, nocc), BF16),
        in_specs=[SMEM, ANY],
        out_specs=ANY,
        scratch_shapes=[pltpu.SemaphoreType.DMA],
        name="pick",
    )(tile_info, theta_blocks)
    received = lax.all_to_all(outgoing, "blk", split_axis=0, concat_axis=0, tiled=True)

    part_shape = (owners, walkers + 8, gs) if spread else (slots, walkers, gs)
    part = pl.pallas_call(
        functools.partial(bias_kernel, spread),
        out_shape=jax.ShapeDtypeStruct(part_shape, F32),
        in_specs=[SMEM, SMEM, SMEM, VMEM, VMEM, VMEM, ANY],
        out_specs=VMEM,
        scratch_shapes=[
            pltpu.VMEM(chol.shape, BF16),
            pltpu.VMEM((bs * walkers, bs), F32),
            pltpu.VMEM((slots, walkers, gs), F32),
            pltpu.SemaphoreType.DMA((slots, PIECES)),
        ],
        compiler_params=params,
        name="bias",
    )(tile_info, tile_count, block_size, received, trial, fields, chol)

    if spread:
        bias_in = lax.all_to_all(part, "blk", split_axis=0, concat_axis=0, tiled=True)
        bias_in = bias_in.reshape(owners * (walkers + 8), gs)
        fields_in = fields
    else:
        me = lax.axis_index("blk")
        local = jnp.zeros((walkers, nchol), F32)
        for slot in range(slots):
            start = (0, tile_info[2, me * slots + slot] * gs)
            old = lax.dynamic_slice(local, start, (walkers, gs))
            local = lax.dynamic_update_slice(local, old + part[slot], start)
        bias_in = lax.psum(local, "blk")
        fields_in = lax.all_gather(fields, "blk", axis=0, tiled=True)

    operators, own_bias = pl.pallas_call(
        functools.partial(operator_kernel, spread),
        out_shape=(
            jax.ShapeDtypeStruct((owners, walk, slots, bs, bs), BF16),
            jax.ShapeDtypeStruct((walk, nchol), F32),
        ),
        in_specs=[SMEM, SMEM, SMEM, VMEM, VMEM, ANY],
        out_specs=(VMEM, VMEM),
        scratch_shapes=[
            pltpu.VMEM(chol.shape, BF16),
            pltpu.VMEM((walkers, nchol), F32),
            pltpu.VMEM((walkers * bs, bs), F32),
            pltpu.SemaphoreType.DMA((slots, PIECES)),
        ],
        compiler_params=params,
        name="operator",
    )(tile_info, tile_count, block_size, bias_in, fields_in, chol)
    arrived = lax.all_to_all(operators, "blk", split_axis=0, concat_axis=0, tiled=True)

    propagated = pl.pallas_call(
        update_kernel,
        out_shape=jax.ShapeDtypeStruct(theta_blocks.shape, BF16),
        in_specs=[SMEM, SMEM, VMEM, VMEM],
        out_specs=VMEM,
        scratch_shapes=[pltpu.SMEM((slabs * blocks * 3,), jnp.int32)],
        compiler_params=params,
        name="update",
    )(tile_info, tile_count, theta_blocks, arrived)
    return propagated.reshape(theta.shape), own_bias


def solution(mesh):
    placed = (
        P(("grp", "blk"), None, None),
        P("grp", None),
        P(("grp", "blk"), None, None),
        P(("grp", "blk"), None),
        P("grp", None),
        P("grp"),
        P("grp"),
    )
    return jax.shard_map(
        per_device,
        mesh=mesh,
        in_specs=placed,
        out_specs=(P(("grp", "blk"), None, None), P(("grp", "blk"), None)),
        check_vma=False,
    )
```

```python
import functools

import jax
import jax.numpy as jnp
from jax import lax
from jax.experimental import pallas as pl
from jax.experimental.pallas import tpu as pltpu
from jax.sharding import PartitionSpec as P

STEP_ROOT = 0.25
PIECES = 8
F32 = jnp.float32
BF16 = jnp.bfloat16
LIMIT = 24 * 1024 * 1024
VMEM = pl.BlockSpec(memory_space=pltpu.VMEM)
SMEM = pl.BlockSpec(memory_space=pltpu.SMEM)
HBM = pl.BlockSpec(memory_space=pltpu.HBM)
NT = (((1,), (1,)), ((), ()))


def pick_kernel(
    info_hbm, count_hbm, size_hbm, fields_hbm, theta_ref, trial_ref,
    out_ref, rows_ref, mask_ref, draws_ref, where_ref, info_ref, count_ref, size_ref, fields_ref, sems,
):
    owners, walk, slots, bs, _ = out_ref.shape
    blocks = theta_ref.shape[1]
    small = [
        pltpu.make_async_copy(source, target, sems.at[2 + n])
        for n, (source, target) in enumerate(
            [(info_hbm, info_ref), (count_hbm, count_ref), (size_hbm, size_ref), (fields_hbm, fields_ref)]
        )
    ]
    for copy in small:
        copy.start()
    small[0].wait()
    copies = []
    for o in range(owners):
        for j in range(slots):
            block = info_ref[1, o * slots + j]
            for w in range(walk):
                copies.append(pltpu.make_async_copy(theta_ref.at[w, block], out_ref.at[o, w, j], sems.at[0]))
    me = lax.axis_index("blk")
    for j in range(slots):
        block = info_ref[0, me * slots + j]
        copies.append(
            pltpu.make_async_copy(
                trial_ref.at[pl.ds(pl.multiple_of(block * bs, bs), bs), :], rows_ref.at[j], sems.at[1]
            )
        )
    for copy in copies:
        copy.start()
    for copy in small[1:]:
        copy.wait()
    live = count_ref[me]
    for j in range(slots):
        row_size = jnp.where(j < live, size_ref[info_ref[0, me * slots + j]], 0)
        col_size = size_ref[info_ref[1, me * slots + j]]
        rows = lax.broadcasted_iota(jnp.int32, (bs, bs), 0) < row_size
        cols = lax.broadcasted_iota(jnp.int32, (bs, bs), 1) < col_size
        mask_ref[j] = jnp.where(rows & cols, 1.0, 0.0)
    draws_ref[...] = jnp.broadcast_to(fields_ref[0:1, :], draws_ref.shape)
    for o in range(owners):
        for j in range(slots):

            @pl.when(j < count_ref[o])
            def _(s=o * slots + j):
                row_block = info_ref[0, s]
                side = info_ref[1, s] - row_block + 1
                where_ref[(info_ref[2, s] * blocks + row_block) * 3 + side] = jnp.int32(s)

    pltpu.make_async_copy(out_ref, out_ref, sems.at[0]).wait()
    pltpu.make_async_copy(rows_ref, rows_ref, sems.at[1]).wait()


def tile_pieces(chol_ref, tile_ref, sems, slot):
    width = chol_ref.shape[2] // PIECES
    return [
        pltpu.make_async_copy(
            chol_ref.at[slot, :, pl.ds(c * width, width)],
            tile_ref.at[slot, :, pl.ds(c * width, width)],
            sems.at[slot, c],
        )
        for c in range(PIECES)
    ]


def bias_kernel(
    spread, recv_ref, rows_ref, mask_ref, draws_ref, chol_ref, out_ref, tile_ref, green_ref, bias_ref, sems
):
    owners, walk, slots, bs, _ = recv_ref.shape
    walkers = owners * walk
    for slot in range(slots):
        for copy in tile_pieces(chol_ref, tile_ref, sems, slot):
            copy.start()
    for slot in range(slots):

        def one(w, carry, slot=slot):
            block = recv_ref[w // walk, w % walk, slot]
            green = lax.dot_general(rows_ref[slot], block, NT, preferred_element_type=F32)
            green_ref[slot, pl.ds(w, bs, stride=walkers), :] = green * mask_ref[slot]
            return carry

        lax.fori_loop(0, walkers, one, 0, unroll=min(walkers, 16))
    per = bs // PIECES
    for slot in range(slots):
        bias = jnp.zeros((walkers, chol_ref.shape[1]), F32)
        for c, copy in enumerate(tile_pieces(chol_ref, tile_ref, sems, slot)):
            copy.wait()
            base = c * per * walkers
            left = jnp.concatenate(
                [green_ref[slot, pl.ds(base + p * walkers, walkers), :].astype(BF16) for p in range(per)],
                axis=1,
            )
            right = tile_ref[slot, :, pl.ds(c * per * bs, per * bs)]
            bias += lax.dot_general(left, right, NT, preferred_element_type=F32)
        bias_ref[slot] = bias

    if spread:
        total = sum(bias_ref[slot] for slot in range(slots))
        for o in range(owners):
            out_ref[o, :walkers, :] = total
            out_ref[o, pl.ds(walkers, 8), :] = draws_ref[...]
    else:
        out_ref[...] = bias_ref[...]


def operator_kernel(spread, *refs):
    if spread:
        bias_ref, mask_ref, chol_ref, out_ref, own_ref, shifted_ref, oper_ref = refs
    else:
        info_ref, bias_ref, fields_ref, mask_ref, chol_ref, out_ref, own_ref, shifted_ref, oper_ref = refs
    owners, walk, slots, bs, _ = out_ref.shape
    walkers = owners * walk
    gs = chol_ref.shape[1]
    me = lax.axis_index("blk")
    if spread:
        rows = walkers + 8
        bias = sum(bias_ref[pl.ds(o * rows, walkers), :] for o in range(owners))
        fields = bias_ref[pl.ds(walkers, owners, stride=rows), :]
        shifted_ref[...] = bias
        own_ref[...] = shifted_ref[pl.ds(me, 1), :]
    else:
        bias = bias_ref[...]
        fields = fields_ref[...]
        own_ref[...] = bias_ref[pl.ds(me * walk, walk), :]
    shifted_ref[...] = fields - bias
    for slot in range(slots):
        slab = 0 if spread else pl.multiple_of(info_ref[2, me * slots + slot] * gs, gs)
        left = shifted_ref[:, pl.ds(slab, gs)].astype(BF16)
        per = bs // PIECES
        for c in range(PIECES):
            right = chol_ref[slot, :, pl.ds(c * per * bs, per * bs)]
            oper = jnp.dot(left, right, preferred_element_type=F32) * STEP_ROOT
            for p in range(per):
                oper_ref[pl.ds(c * per + p, walkers, stride=bs), :] = oper[:, p * bs : (p + 1) * bs]

        def one(w, carry, slot=slot):
            block = oper_ref[pl.ds(pl.multiple_of(w * bs, bs), bs), :]
            out_ref[w // walk, w % walk, slot] = (block * mask_ref[slot]).astype(BF16)
            return carry

        lax.fori_loop(0, walkers, one, 0, unroll=min(walkers, 16))


def update_kernel(where_ref, theta_ref, oper_ref, out_ref):
    owners, walk, slots, bs, _ = oper_ref.shape
    blocks = theta_ref.shape[1]
    slabs = where_ref.shape[0] // (3 * blocks)
    for w in range(walk):
        for row_block in range(blocks):
            total = theta_ref[w, row_block].astype(F32)
            for col_block in range(max(row_block - 1, 0), min(row_block + 2, blocks)):
                for slab in range(slabs):
                    s = where_ref[(slab * blocks + row_block) * 3 + col_block - row_block + 1]
                    total += jnp.dot(
                        oper_ref[s // slots, w, s % slots], theta_ref[w, col_block],
                        preferred_element_type=F32,
                    )
            out_ref[w, row_block] = total.astype(BF16)


def per_device(theta, trial, chol, fields, tile_info, tile_count, block_size):
    owners = lax.axis_size("blk")
    walk, norb, nocc = theta.shape
    walkers = walk * owners
    slots, gs, _ = chol.shape
    nchol = fields.shape[1]
    blocks = block_size.shape[0]
    bs = norb // blocks
    slabs = nchol // gs
    spread = slabs == 1 and walk == 1
    params = pltpu.CompilerParams(vmem_limit_bytes=LIMIT)
    theta_blocks = theta.reshape(walk, blocks, bs, nocc)

    outgoing, rows, mask, draws, where = pl.pallas_call(
        pick_kernel,
        out_shape=(
            jax.ShapeDtypeStruct((owners, walk, slots, bs, nocc), BF16),
            jax.ShapeDtypeStruct((slots, bs, nocc), BF16),
            jax.ShapeDtypeStruct((slots, bs, bs), F32),
            jax.ShapeDtypeStruct((8, nchol), F32),
            jax.ShapeDtypeStruct((slabs * blocks * 3,), jnp.int32),
        ),
        in_specs=[HBM] * 6,
        out_specs=(VMEM, VMEM, VMEM, VMEM, SMEM),
        scratch_shapes=[
            pltpu.SMEM(tile_info.shape, jnp.int32),
            pltpu.SMEM(tile_count.shape, jnp.int32),
            pltpu.SMEM(block_size.shape, jnp.int32),
            pltpu.VMEM(fields.shape, F32),
            pltpu.SemaphoreType.DMA((6,)),
        ],
        compiler_params=params,
        name="pick",
    )(*(pltpu.with_memory_space_constraint(x, pltpu.HBM)
        for x in (tile_info, tile_count, block_size, fields, theta_blocks, trial)))
    received = lax.all_to_all(outgoing, "blk", split_axis=0, concat_axis=0, tiled=True)

    part_shape = (owners, walkers + 8, gs) if spread else (slots, walkers, gs)
    part, tiles = pl.pallas_call(
        functools.partial(bias_kernel, spread),
        out_shape=(jax.ShapeDtypeStruct(part_shape, F32), jax.ShapeDtypeStruct(chol.shape, BF16)),
        in_specs=[VMEM, VMEM, VMEM, VMEM, HBM],
        out_specs=(VMEM, VMEM),
        scratch_shapes=[
            pltpu.VMEM((slots, bs * walkers, bs), F32),
            pltpu.VMEM((slots, walkers, gs), F32),
            pltpu.SemaphoreType.DMA((slots, PIECES)),
        ],
        compiler_params=params,
        name="bias",
    )(received, rows, mask, draws, pltpu.with_memory_space_constraint(chol, pltpu.HBM))

    if spread:
        bias_in = lax.all_to_all(part, "blk", split_axis=0, concat_axis=0, tiled=True)
        inputs = (bias_in.reshape(owners * (walkers + 8), gs),)
    else:
        me = lax.axis_index("blk")
        local = jnp.zeros((walkers, nchol), F32)
        for slot in range(slots):
            start = (0, tile_info[2, me * slots + slot] * gs)
            old = lax.dynamic_slice(local, start, (walkers, gs))
            local = lax.dynamic_update_slice(local, old + part[slot], start)
        inputs = (tile_info, lax.psum(local, "blk"), lax.all_gather(fields, "blk", axis=0, tiled=True))

    operators, own_bias = pl.pallas_call(
        functools.partial(operator_kernel, spread),
        out_shape=(
            jax.ShapeDtypeStruct((owners, walk, slots, bs, bs), BF16),
            jax.ShapeDtypeStruct((walk, nchol), F32),
        ),
        in_specs=([VMEM] if spread else [SMEM, VMEM, VMEM]) + [VMEM, VMEM],
        out_specs=(VMEM, VMEM),
        scratch_shapes=[
            pltpu.VMEM((walkers, nchol), F32),
            pltpu.VMEM((walkers * bs, bs), F32),
        ],
        compiler_params=params,
        name="operator",
    )(*inputs, mask, tiles)
    arrived = lax.all_to_all(operators, "blk", split_axis=0, concat_axis=0, tiled=True)

    propagated = pl.pallas_call(
        update_kernel,
        out_shape=jax.ShapeDtypeStruct(theta_blocks.shape, BF16),
        in_specs=[SMEM, VMEM, VMEM],
        out_specs=VMEM,
        compiler_params=params,
        name="update",
    )(where, theta_blocks, arrived)
    return propagated.reshape(theta.shape), own_bias


def solution(mesh):
    placed = (
        P(("grp", "blk"), None, None),
        P("grp", None),
        P(("grp", "blk"), None, None),
        P(("grp", "blk"), None),
        P("grp", None),
        P("grp"),
        P("grp"),
    )
    return jax.shard_map(
        per_device,
        mesh=mesh,
        in_specs=placed,
        out_specs=(P(("grp", "blk"), None, None), P(("grp", "blk"), None)),
        check_vma=False,
    )
```

```python
import functools

import jax
import jax.numpy as jnp
from jax import lax
from jax.experimental import pallas as pl
from jax.experimental.pallas import tpu as pltpu
from jax.sharding import PartitionSpec as P

STEP_ROOT = 0.25
PIECES = 8
F32 = jnp.float32
BF16 = jnp.bfloat16
LIMIT = 24 * 1024 * 1024
VMEM = pl.BlockSpec(memory_space=pltpu.VMEM)
SMEM = pl.BlockSpec(memory_space=pltpu.SMEM)
HBM = pl.BlockSpec(memory_space=pltpu.HBM)
NT = (((1,), (1,)), ((), ()))


def each(count, body):
    if count <= 16:
        for index in range(count):
            body(index)
    else:

        def step(index, carry):
            body(index)
            return carry

        lax.fori_loop(0, count, step, 0, unroll=8)


def pick_kernel(
    info_hbm, count_hbm, size_hbm, fields_hbm, theta_ref, trial_ref, chol_ref,
    out_ref, rows_ref, mask_ref, draws_ref, where_ref, info_ref, count_ref, size_ref, fields_ref, sems,
):
    owners, walk, slots, bs, _ = out_ref.shape
    blocks = theta_ref.shape[1]
    small = [
        pltpu.make_async_copy(source, target, sems.at[2 + n])
        for n, (source, target) in enumerate(
            [(info_hbm, info_ref), (count_hbm, count_ref), (size_hbm, size_ref), (fields_hbm, fields_ref)]
        )
    ]
    for copy in small:
        copy.start()
    small[0].wait()
    copies = []
    for o in range(owners):
        for j in range(slots):
            block = info_ref[1, o * slots + j]
            for w in range(walk):
                copies.append(pltpu.make_async_copy(theta_ref.at[w, block], out_ref.at[o, w, j], sems.at[0]))
    me = lax.axis_index("blk")
    for j in range(slots):
        block = info_ref[0, me * slots + j]
        copies.append(
            pltpu.make_async_copy(
                trial_ref.at[pl.ds(pl.multiple_of(block * bs, bs), bs), :], rows_ref.at[j], sems.at[1]
            )
        )
    for copy in copies:
        copy.start()
    for copy in small[1:]:
        copy.wait()
    live = count_ref[me]
    for j in range(slots):
        row_size = jnp.where(j < live, size_ref[info_ref[0, me * slots + j]], 0)
        col_size = size_ref[info_ref[1, me * slots + j]]
        rows = lax.broadcasted_iota(jnp.int32, (bs, bs), 0) < row_size
        cols = lax.broadcasted_iota(jnp.int32, (bs, bs), 1) < col_size
        mask_ref[j] = jnp.where(rows & cols, 1.0, 0.0)
    draws_ref[...] = jnp.broadcast_to(fields_ref[0:1, :], draws_ref.shape)
    for o in range(owners):
        for j in range(slots):

            @pl.when(j < count_ref[o])
            def _(s=o * slots + j):
                row_block = info_ref[0, s]
                side = info_ref[1, s] - row_block + 1
                where_ref[(info_ref[2, s] * blocks + row_block) * 3 + side] = jnp.int32(s)

    pltpu.make_async_copy(out_ref, out_ref, sems.at[0]).wait()
    pltpu.make_async_copy(rows_ref, rows_ref, sems.at[1]).wait()


def bias_kernel(
    spread, recv_ref, rows_ref, mask_ref, draws_ref, chol_ref, out_ref, green_ref, bias_ref
):
    owners, walk, slots, bs, _ = recv_ref.shape
    walkers = owners * walk
    for slot in range(slots):

        def one(w, slot=slot):
            block = recv_ref[w // walk, w % walk, slot]
            green = lax.dot_general(rows_ref[slot], block, NT, preferred_element_type=F32)
            green_ref[slot, pl.ds(w, bs, stride=walkers), :] = green * mask_ref[slot]

        each(walkers, one)
    per = bs // PIECES
    for slot in range(slots):
        bias = jnp.zeros((walkers, chol_ref.shape[1]), F32)
        for c in range(PIECES):
            base = c * per * walkers
            left = jnp.concatenate(
                [green_ref[slot, pl.ds(base + p * walkers, walkers), :].astype(BF16) for p in range(per)],
                axis=1,
            )
            right = chol_ref[slot, :, pl.ds(c * per * bs, per * bs)]
            bias += lax.dot_general(left, right, NT, preferred_element_type=F32)
        bias_ref[slot] = bias

    if spread:
        total = sum(bias_ref[slot] for slot in range(slots))
        for o in range(owners):
            out_ref[o, :walkers, :] = total
            out_ref[o, pl.ds(walkers, 8), :] = draws_ref[...]
    else:
        out_ref[...] = bias_ref[...]


def operator_kernel(spread, *refs):
    if spread:
        bias_ref, mask_ref, chol_ref, out_ref, own_ref, shifted_ref, oper_ref = refs
    else:
        info_ref, bias_ref, fields_ref, mask_ref, chol_ref, out_ref, own_ref, shifted_ref, oper_ref = refs
    owners, walk, slots, bs, _ = out_ref.shape
    walkers = owners * walk
    gs = chol_ref.shape[1]
    me = lax.axis_index("blk")
    if spread:
        rows = walkers + 8
        bias = sum(bias_ref[pl.ds(o * rows, walkers), :] for o in range(owners))
        fields = bias_ref[pl.ds(walkers, owners, stride=rows), :]
        shifted_ref[...] = bias
        own_ref[...] = shifted_ref[pl.ds(me, 1), :]
    else:
        bias = bias_ref[...]
        fields = fields_ref[...]
        own_ref[...] = bias_ref[pl.ds(me * walk, walk), :]
    shifted_ref[...] = fields - bias
    for slot in range(slots):
        slab = 0 if spread else pl.multiple_of(info_ref[2, me * slots + slot] * gs, gs)
        left = shifted_ref[:, pl.ds(slab, gs)].astype(BF16)
        per = bs // PIECES
        for c in range(PIECES):
            right = chol_ref[slot, :, pl.ds(c * per * bs, per * bs)]
            oper = jnp.dot(left, right, preferred_element_type=F32) * STEP_ROOT
            for p in range(per):
                oper_ref[pl.ds(c * per + p, walkers, stride=bs), :] = oper[:, p * bs : (p + 1) * bs]

        def one(w, slot=slot):
            block = oper_ref[pl.ds(w * bs, bs), :]
            out_ref[w // walk, w % walk, slot] = (block * mask_ref[slot]).astype(BF16)

        each(walkers, one)


def update_kernel(where_ref, theta_ref, oper_ref, out_ref):
    owners, walk, slots, bs, _ = oper_ref.shape
    blocks = theta_ref.shape[1]
    slabs = where_ref.shape[0] // (3 * blocks)
    for w in range(walk):
        for row_block in range(blocks):
            total = theta_ref[w, row_block].astype(F32)
            for col_block in range(max(row_block - 1, 0), min(row_block + 2, blocks)):
                for slab in range(slabs):
                    s = where_ref[(slab * blocks + row_block) * 3 + col_block - row_block + 1]
                    total += jnp.dot(
                        oper_ref[s // slots, w, s % slots], theta_ref[w, col_block],
                        preferred_element_type=F32,
                    )
            out_ref[w, row_block] = total.astype(BF16)


def per_device(theta, trial, chol, fields, tile_info, tile_count, block_size):
    owners = lax.axis_size("blk")
    walk, norb, nocc = theta.shape
    walkers = walk * owners
    slots, gs, _ = chol.shape
    nchol = fields.shape[1]
    blocks = block_size.shape[0]
    bs = norb // blocks
    slabs = nchol // gs
    spread = slabs == 1 and walk == 1
    params = pltpu.CompilerParams(vmem_limit_bytes=LIMIT)
    theta_blocks = theta.reshape(walk, blocks, bs, nocc)

    outgoing, rows, mask, draws, where = pl.pallas_call(
        pick_kernel,
        out_shape=(
            jax.ShapeDtypeStruct((owners, walk, slots, bs, nocc), BF16),
            jax.ShapeDtypeStruct((slots, bs, nocc), BF16),
            jax.ShapeDtypeStruct((slots, bs, bs), F32),
            jax.ShapeDtypeStruct((8, nchol), F32),
            jax.ShapeDtypeStruct((slabs * blocks * 3,), jnp.int32),
        ),
        in_specs=[HBM] * 7,
        out_specs=(VMEM, VMEM, VMEM, VMEM, SMEM),
        scratch_shapes=[
            pltpu.SMEM(tile_info.shape, jnp.int32),
            pltpu.SMEM(tile_count.shape, jnp.int32),
            pltpu.SMEM(block_size.shape, jnp.int32),
            pltpu.VMEM(fields.shape, F32),
            pltpu.SemaphoreType.DMA((6,)),
        ],
        compiler_params=params,
        cost_estimate=pl.CostEstimate(flops=0, bytes_accessed=4 * chol.size * 2, transcendentals=0),
        name="pick",
    )(*(pltpu.with_memory_space_constraint(x, pltpu.HBM)
        for x in (tile_info, tile_count, block_size, fields, theta_blocks, trial, chol)))
    received = lax.all_to_all(outgoing, "blk", split_axis=0, concat_axis=0, tiled=True)

    part_shape = (owners, walkers + 8, gs) if spread else (slots, walkers, gs)
    part = pl.pallas_call(
        functools.partial(bias_kernel, spread),
        out_shape=jax.ShapeDtypeStruct(part_shape, F32),
        in_specs=[VMEM] * 5,
        out_specs=VMEM,
        scratch_shapes=[
            pltpu.VMEM((slots, bs * walkers, bs), F32),
            pltpu.VMEM((slots, walkers, gs), F32),
        ],
        compiler_params=params,
        name="bias",
    )(received, rows, mask, draws, chol)

    if spread:
        bias_in = lax.all_to_all(part, "blk", split_axis=0, concat_axis=0, tiled=True)
        inputs = (bias_in.reshape(owners * (walkers + 8), gs),)
    else:
        me = lax.axis_index("blk")
        local = jnp.zeros((walkers, nchol), F32)
        for slot in range(slots):
            start = (0, tile_info[2, me * slots + slot] * gs)
            old = lax.dynamic_slice(local, start, (walkers, gs))
            local = lax.dynamic_update_slice(local, old + part[slot], start)
        inputs = (tile_info, lax.psum(local, "blk"), lax.all_gather(fields, "blk", axis=0, tiled=True))

    operators, own_bias = pl.pallas_call(
        functools.partial(operator_kernel, spread),
        out_shape=(
            jax.ShapeDtypeStruct((owners, walk, slots, bs, bs), BF16),
            jax.ShapeDtypeStruct((walk, nchol), F32),
        ),
        in_specs=([VMEM] if spread else [SMEM, VMEM, VMEM]) + [VMEM, VMEM],
        out_specs=(VMEM, VMEM),
        scratch_shapes=[
            pltpu.VMEM((walkers, nchol), F32),
            pltpu.VMEM((walkers * bs, bs), F32),
        ],
        compiler_params=params,
        name="operator",
    )(*inputs, mask, chol)
    arrived = lax.all_to_all(operators, "blk", split_axis=0, concat_axis=0, tiled=True)

    propagated = pl.pallas_call(
        update_kernel,
        out_shape=jax.ShapeDtypeStruct(theta_blocks.shape, BF16),
        in_specs=[SMEM, VMEM, VMEM],
        out_specs=VMEM,
        compiler_params=params,
        name="update",
    )(where, theta_blocks, arrived)
    return propagated.reshape(theta.shape), own_bias


def solution(mesh):
    placed = (
        P(("grp", "blk"), None, None),
        P("grp", None),
        P(("grp", "blk"), None, None),
        P(("grp", "blk"), None),
        P("grp", None),
        P("grp"),
        P("grp"),
    )
    return jax.shard_map(
        per_device,
        mesh=mesh,
        in_specs=placed,
        out_specs=(P(("grp", "blk"), None, None), P(("grp", "blk"), None)),
        check_vma=False,
    )
```

```python
import functools

import jax
import jax.numpy as jnp
from jax import lax
from jax.experimental import pallas as pl
from jax.experimental.pallas import tpu as pltpu
from jax.sharding import PartitionSpec as P

STEP_ROOT = 0.25
PIECES = 8
F32 = jnp.float32
BF16 = jnp.bfloat16
LIMIT = 24 * 1024 * 1024
VMEM = pl.BlockSpec(memory_space=pltpu.VMEM)
SMEM = pl.BlockSpec(memory_space=pltpu.SMEM)
HBM = pl.BlockSpec(memory_space=pltpu.HBM)
ANY = pl.BlockSpec(memory_space=pl.ANY)
NT = (((1,), (1,)), ((), ()))


def each(count, body):
    if count <= 16:
        for index in range(count):
            body(index)
    else:

        def step(index, carry):
            body(index)
            return carry

        lax.fori_loop(0, count, step, 0, unroll=8)


def pick_kernel(
    info_hbm, count_hbm, size_hbm, fields_hbm, theta_ref, trial_ref, chol_ref,
    out_ref, rows_ref, mask_ref, draws_ref, where_ref, info_ref, count_ref, size_ref, fields_ref, sems,
):
    owners, walk, slots, bs, _ = out_ref.shape
    blocks = theta_ref.shape[1]
    small = [
        pltpu.make_async_copy(source, target, sems.at[2 + n])
        for n, (source, target) in enumerate(
            [(info_hbm, info_ref), (count_hbm, count_ref), (size_hbm, size_ref), (fields_hbm, fields_ref)]
        )
    ]
    for copy in small:
        copy.start()
    small[0].wait()
    copies = []
    for o in range(owners):
        for j in range(slots):
            block = info_ref[1, o * slots + j]
            for w in range(walk):
                copies.append(pltpu.make_async_copy(theta_ref.at[w, block], out_ref.at[o, w, j], sems.at[0]))
    me = lax.axis_index("blk")
    for j in range(slots):
        block = info_ref[0, me * slots + j]
        copies.append(
            pltpu.make_async_copy(
                trial_ref.at[pl.ds(pl.multiple_of(block * bs, bs), bs), :], rows_ref.at[j], sems.at[1]
            )
        )
    for copy in copies:
        copy.start()
    for copy in small[1:]:
        copy.wait()
    live = count_ref[me]
    for j in range(slots):
        row_size = jnp.where(j < live, size_ref[info_ref[0, me * slots + j]], 0)
        col_size = size_ref[info_ref[1, me * slots + j]]
        rows = lax.broadcasted_iota(jnp.int32, (bs, bs), 0) < row_size
        cols = lax.broadcasted_iota(jnp.int32, (bs, bs), 1) < col_size
        mask_ref[j] = jnp.where(rows & cols, 1.0, 0.0)
    draws_ref[...] = jnp.broadcast_to(fields_ref[0:1, :], draws_ref.shape)
    for o in range(owners):
        for j in range(slots):

            @pl.when(j < count_ref[o])
            def _(s=o * slots + j):
                row_block = info_ref[0, s]
                side = info_ref[1, s] - row_block + 1
                where_ref[(info_ref[2, s] * blocks + row_block) * 3 + side] = jnp.int32(s)

    pltpu.make_async_copy(out_ref, out_ref, sems.at[0]).wait()
    pltpu.make_async_copy(rows_ref, rows_ref, sems.at[1]).wait()


def bias_kernel(
    spread, recv_ref, rows_ref, mask_ref, draws_ref, chol_ref, out_ref, green_ref, bias_ref
):
    owners, walk, slots, bs, _ = recv_ref.shape
    walkers = owners * walk
    for slot in range(slots):

        def one(w, slot=slot):
            block = recv_ref[w // walk, w % walk, slot]
            green = lax.dot_general(rows_ref[slot], block, NT, preferred_element_type=F32)
            green_ref[slot, pl.ds(w, bs, stride=walkers), :] = green * mask_ref[slot]

        each(walkers, one)
    per = bs // PIECES
    for slot in range(slots):
        bias = jnp.zeros((walkers, chol_ref.shape[1]), F32)
        for c in range(PIECES):
            base = c * per * walkers
            left = jnp.concatenate(
                [green_ref[slot, pl.ds(base + p * walkers, walkers), :].astype(BF16) for p in range(per)],
                axis=1,
            )
            right = chol_ref[slot, :, pl.ds(c * per * bs, per * bs)]
            bias += lax.dot_general(left, right, NT, preferred_element_type=F32)
        bias_ref[slot] = bias

    if spread:
        total = sum(bias_ref[slot] for slot in range(slots))
        for o in range(owners):
            out_ref[o, :walkers, :] = total
            out_ref[o, pl.ds(walkers, 8), :] = draws_ref[...]
    else:
        out_ref[...] = bias_ref[...]


def operator_kernel(spread, *refs):
    if spread:
        bias_ref, mask_ref, chol_ref, out_ref, own_ref, shifted_ref, oper_ref = refs
    else:
        info_ref, bias_ref, fields_ref, mask_ref, chol_ref, out_ref, own_ref, shifted_ref, oper_ref = refs
    owners, walk, slots, bs, _ = out_ref.shape
    walkers = owners * walk
    gs = chol_ref.shape[1]
    me = lax.axis_index("blk")
    if spread:
        rows = walkers + 8
        bias = sum(bias_ref[pl.ds(o * rows, walkers), :] for o in range(owners))
        fields = bias_ref[pl.ds(walkers, owners, stride=rows), :]
        shifted_ref[...] = bias
        own_ref[...] = shifted_ref[pl.ds(me, 1), :]
    else:
        bias = bias_ref[...]
        fields = fields_ref[...]
        own_ref[...] = bias_ref[pl.ds(me * walk, walk), :]
    shifted_ref[...] = fields - bias
    for slot in range(slots):
        slab = 0 if spread else pl.multiple_of(info_ref[2, me * slots + slot] * gs, gs)
        left = shifted_ref[:, pl.ds(slab, gs)].astype(BF16)
        per = bs // PIECES
        for c in range(PIECES):
            right = chol_ref[slot, :, pl.ds(c * per * bs, per * bs)]
            oper = jnp.dot(left, right, preferred_element_type=F32) * STEP_ROOT
            for p in range(per):
                oper_ref[pl.ds(c * per + p, walkers, stride=bs), :] = oper[:, p * bs : (p + 1) * bs]

        def one(w, slot=slot):
            block = oper_ref[pl.ds(w * bs, bs), :]
            out_ref[w // walk, w % walk, slot] = (block * mask_ref[slot]).astype(BF16)

        each(walkers, one)


def update_kernel(where_ref, theta_ref, oper_ref, out_ref):
    owners, walk, slots, bs, _ = oper_ref.shape
    blocks = theta_ref.shape[1]
    slabs = where_ref.shape[0] // (3 * blocks)
    for w in range(walk):
        for row_block in range(blocks):
            total = theta_ref[w, row_block].astype(F32)
            for col_block in range(max(row_block - 1, 0), min(row_block + 2, blocks)):
                for slab in range(slabs):
                    s = where_ref[(slab * blocks + row_block) * 3 + col_block - row_block + 1]
                    total += jnp.dot(
                        oper_ref[s // slots, w, s % slots], theta_ref[w, col_block],
                        preferred_element_type=F32,
                    )
            out_ref[w, row_block] = total.astype(BF16)


def long_axis(theta, trial, chol, fields, tile_info, tile_count, block_size):
    owners = lax.axis_size("blk")
    walk, norb, nocc = theta.shape
    walkers = walk * owners
    slots, gs, _ = chol.shape
    nchol = fields.shape[1]
    blocks = block_size.shape[0]
    bs = norb // blocks
    slabs = nchol // gs
    spread = slabs == 1 and walk == 1
    params = pltpu.CompilerParams(vmem_limit_bytes=LIMIT)
    theta_blocks = theta.reshape(walk, blocks, bs, nocc)

    outgoing, rows, mask, draws, where = pl.pallas_call(
        pick_kernel,
        out_shape=(
            jax.ShapeDtypeStruct((owners, walk, slots, bs, nocc), BF16),
            jax.ShapeDtypeStruct((slots, bs, nocc), BF16),
            jax.ShapeDtypeStruct((slots, bs, bs), F32),
            jax.ShapeDtypeStruct((8, nchol), F32),
            jax.ShapeDtypeStruct((slabs * blocks * 3,), jnp.int32),
        ),
        in_specs=[HBM] * 7,
        out_specs=(VMEM, VMEM, VMEM, VMEM, SMEM),
        scratch_shapes=[
            pltpu.SMEM(tile_info.shape, jnp.int32),
            pltpu.SMEM(tile_count.shape, jnp.int32),
            pltpu.SMEM(block_size.shape, jnp.int32),
            pltpu.VMEM(fields.shape, F32),
            pltpu.SemaphoreType.DMA((6,)),
        ],
        compiler_params=params,
        cost_estimate=pl.CostEstimate(flops=0, bytes_accessed=4 * chol.size * 2, transcendentals=0),
        name="pick",
    )(*(pltpu.with_memory_space_constraint(x, pltpu.HBM)
        for x in (tile_info, tile_count, block_size, fields, theta_blocks, trial, chol)))
    received = lax.all_to_all(outgoing, "blk", split_axis=0, concat_axis=0, tiled=True)

    part_shape = (owners, walkers + 8, gs) if spread else (slots, walkers, gs)
    part = pl.pallas_call(
        functools.partial(bias_kernel, spread),
        out_shape=jax.ShapeDtypeStruct(part_shape, F32),
        in_specs=[VMEM] * 5,
        out_specs=VMEM,
        scratch_shapes=[
            pltpu.VMEM((slots, bs * walkers, bs), F32),
            pltpu.VMEM((slots, walkers, gs), F32),
        ],
        compiler_params=params,
        name="bias",
    )(received, rows, mask, draws, chol)

    if spread:
        bias_in = lax.all_to_all(part, "blk", split_axis=0, concat_axis=0, tiled=True)
        inputs = (bias_in.reshape(owners * (walkers + 8), gs),)
    else:
        me = lax.axis_index("blk")
        local = jnp.zeros((walkers, nchol), F32)
        for slot in range(slots):
            start = (0, tile_info[2, me * slots + slot] * gs)
            old = lax.dynamic_slice(local, start, (walkers, gs))
            local = lax.dynamic_update_slice(local, old + part[slot], start)
        inputs = (tile_info, lax.psum(local, "blk"), lax.all_gather(fields, "blk", axis=0, tiled=True))

    operators, own_bias = pl.pallas_call(
        functools.partial(operator_kernel, spread),
        out_shape=(
            jax.ShapeDtypeStruct((owners, walk, slots, bs, bs), BF16),
            jax.ShapeDtypeStruct((walk, nchol), F32),
        ),
        in_specs=([VMEM] if spread else [SMEM, VMEM, VMEM]) + [VMEM, VMEM],
        out_specs=(VMEM, VMEM),
        scratch_shapes=[
            pltpu.VMEM((walkers, nchol), F32),
            pltpu.VMEM((walkers * bs, bs), F32),
        ],
        compiler_params=params,
        name="operator",
    )(*inputs, mask, chol)
    arrived = lax.all_to_all(operators, "blk", split_axis=0, concat_axis=0, tiled=True)

    propagated = pl.pallas_call(
        update_kernel,
        out_shape=jax.ShapeDtypeStruct(theta_blocks.shape, BF16),
        in_specs=[SMEM, VMEM, VMEM],
        out_specs=VMEM,
        compiler_params=params,
        name="update",
    )(where, theta_blocks, arrived)
    return propagated.reshape(theta.shape), own_bias


def pick_pair_kernel(*refs):
    info_hbm, count_hbm, size_hbm, fields_hbm, theta_ref, other_ref, trial_ref, _ = refs[:8]
    rows_ref, mask_ref, draws_ref, where_ref, cols_ref = refs[8:13]
    info_ref, count_ref, size_ref, fields_ref, sems, send_sems = refs[-6:]
    pair_refs = refs[13:-6]
    slots, bs, _ = rows_ref.shape
    owners = count_ref.shape[0]
    blocks = theta_ref.shape[1]
    small = [
        pltpu.make_async_copy(source, target, sems.at[n])
        for n, (source, target) in enumerate(
            [(info_hbm, info_ref), (count_hbm, count_ref), (size_hbm, size_ref), (fields_hbm, fields_ref)]
        )
    ]
    for copy in small:
        copy.start()
    me = lax.axis_index("blk")
    core = me % 2
    small[0].wait()
    for r, ref in enumerate(pair_refs):
        for j in range(slots):
            block = info_ref[1, (me ^ (2 * r)) * slots + j]
            pltpu.make_async_copy(theta_ref.at[0, block], ref.at[core, j], send_sems.at[r]).start()
            pltpu.make_async_copy(other_ref.at[0, block], ref.at[1 - core, j], send_sems.at[r]).start()
    first = me // (owners // 2) * (owners // 2) * slots
    for n in range(owners // 2 * slots):
        cols_ref[n] = info_ref[1, first + n]
    trial = []
    for j in range(slots):
        block = info_ref[0, me * slots + j]
        trial.append(
            pltpu.make_async_copy(
                trial_ref.at[pl.ds(pl.multiple_of(block * bs, bs), bs), :], rows_ref.at[j], sems.at[4 + j]
            )
        )
        trial[-1].start()
    for copy in small[1:]:
        copy.wait()
    live = count_ref[me]
    for j in range(slots):
        row_size = jnp.where(j < live, size_ref[info_ref[0, me * slots + j]], 0)
        col_size = size_ref[info_ref[1, me * slots + j]]
        rows = lax.broadcasted_iota(jnp.int32, (bs, bs), 0) < row_size
        cols = lax.broadcasted_iota(jnp.int32, (bs, bs), 1) < col_size
        mask_ref[j] = jnp.where(rows & cols, 1.0, 0.0)
    draws_ref[...] = jnp.broadcast_to(fields_ref[0:1, :], draws_ref.shape)
    for o in range(owners):
        for j in range(slots):

            @pl.when(j < count_ref[o])
            def _(s=o * slots + j):
                row_block = info_ref[0, s]
                where_ref[row_block * 3 + info_ref[1, s] - row_block + 1] = jnp.int32(s)

    for r, ref in enumerate(pair_refs):
        pltpu.make_async_copy(ref, ref, send_sems.at[r]).wait()
    for copy in trial:
        copy.wait()


def spread_far_kernel(cols_ref, theta_ref, _, out_ref):
    slots = out_ref.shape[1]
    for k in range(out_ref.shape[0]):
        for j in range(slots):
            out_ref[k, j] = theta_ref[0, cols_ref[k * slots + j]]


def bias_pair_kernel(step, rows_ref, mask_ref, draws_ref, chol_ref, far_ref, *refs):
    pair_refs = refs[:-3]
    out_ref, green_ref, total_ref = refs[-3:]
    half, slots, bs, nocc = far_ref.shape
    walkers = 2 * half
    me = lax.axis_index("blk")
    first = me // half * half
    for slot in range(slots):
        mask = mask_ref[slot]
        for blocks, start in [(ref[:, slot], 2 * r) for r, ref in enumerate(pair_refs)] + [(far_ref[:, slot], half)]:
            count = blocks.shape[0]
            green = lax.dot_general(
                rows_ref[slot], blocks.reshape(count * bs, nocc), NT, preferred_element_type=F32
            )
            for n in range(count):
                green_ref[slot, pl.ds(start + n, bs, stride=walkers), :] = green[:, n * bs : (n + 1) * bs] * mask
    per = bs // PIECES
    tall = jnp.zeros((chol_ref.shape[1], walkers), F32)
    wide = jnp.zeros((walkers, chol_ref.shape[1]), F32)
    for c in range(PIECES):
        for slot in range(slots):
            green = jnp.concatenate(
                [green_ref[slot, pl.ds((c * per + p) * walkers, walkers), :].astype(BF16) for p in range(per)],
                axis=1,
            )
            tile = chol_ref[slot, :, pl.ds(c * per * bs, per * bs)]
            if slot % 2:
                wide += lax.dot_general(green, tile, NT, preferred_element_type=F32)
            else:
                tall += lax.dot_general(tile, green, NT, preferred_element_type=F32)
    total = -(tall.T + wide)
    for n in range(walkers):
        walker = (me // 2 ^ (n // 2)) * 2 + n % 2 if n < half else (first + n - half) ^ step
        total_ref[pl.ds(walker, 1), :] = total[n : n + 1, :]
    total = total_ref[...]
    own = total_ref[pl.ds(me, 1), :]
    for o in range(walkers):
        out_ref[o] = total
        out_ref[o, pl.ds(me, 1), :] = jnp.where(o == me, own, own + draws_ref[0:1, :])


def operator_pair_kernel(shift_ref, fields_ref, mask_ref, chol_ref, out_ref, own_ref, total_ref, oper_ref):
    walkers, _, slots, bs, _ = out_ref.shape
    me = lax.axis_index("blk")
    total_ref[...] = sum(shift_ref[o] for o in range(walkers))
    own = total_ref[pl.ds(me, 1), :]
    own_ref[...] = -own
    total_ref[pl.ds(me, 1), :] = own + fields_ref[0:1, :]
    left = total_ref[...].astype(BF16)
    per = bs // PIECES
    for slot in range(slots):
        for c in range(PIECES):
            right = chol_ref[slot, :, pl.ds(c * per * bs, per * bs)]
            oper = jnp.dot(left, right, preferred_element_type=F32) * STEP_ROOT
            for p in range(per):
                oper_ref[slot, pl.ds(c * per + p, walkers, stride=bs), :] = oper[:, p * bs : (p + 1) * bs]
        for w in range(walkers):
            block = oper_ref[slot, pl.ds(w * bs, bs), :]
            out_ref[w, 0, slot] = (block * mask_ref[slot]).astype(BF16)


def short_axis(theta, trial, chol, fields, tile_info, tile_count, block_size):
    owners = lax.axis_size("blk")
    _, norb, nocc = theta.shape
    slots, gs, _ = chol.shape
    blocks = block_size.shape[0]
    bs = norb // blocks
    half = owners // 2
    step = half + half // 2
    near = half // 2
    params = pltpu.CompilerParams(vmem_limit_bytes=LIMIT)
    theta_blocks = theta.reshape(1, blocks, bs, nocc)

    def swap(x, step):
        return lax.ppermute(x, "blk", [(i, i ^ step) for i in range(owners)])

    def to_all(x, groups=None):
        return lax.all_to_all(x, "blk", split_axis=0, concat_axis=0, tiled=True, axis_index_groups=groups)

    def spread(pairs):
        return [pairs[0]] + [swap(pairs[r], 2 * r) for r in range(1, near)]

    hbm = functools.partial(pltpu.with_memory_space_constraint, memory_space=pltpu.HBM)
    pair_shapes = (jax.ShapeDtypeStruct((2, slots, bs, nocc), BF16),) * near
    partner = swap(theta_blocks, step)
    rows, mask, draws, where, cols, *pairs = pl.pallas_call(
        pick_pair_kernel,
        out_shape=(
            jax.ShapeDtypeStruct((slots, bs, nocc), BF16),
            jax.ShapeDtypeStruct((slots, bs, bs), F32),
            jax.ShapeDtypeStruct((8, gs), F32),
            jax.ShapeDtypeStruct((3 * blocks,), jnp.int32),
            jax.ShapeDtypeStruct((half * slots,), jnp.int32),
            *pair_shapes,
        ),
        in_specs=[HBM] * 5 + [ANY] + [HBM] * 2,
        out_specs=(VMEM, VMEM, VMEM, SMEM, SMEM) + (VMEM,) * near,
        scratch_shapes=[
            pltpu.SMEM(tile_info.shape, jnp.int32),
            pltpu.SMEM(tile_count.shape, jnp.int32),
            pltpu.SMEM(block_size.shape, jnp.int32),
            pltpu.VMEM(fields.shape, F32),
            pltpu.SemaphoreType.DMA((4 + slots,)),
            pltpu.SemaphoreType.DMA((near,)),
        ],
        compiler_params=params,
        cost_estimate=pl.CostEstimate(flops=0, bytes_accessed=8 * chol.size, transcendentals=0),
        name="pick",
    )(
        *map(hbm, (tile_info, tile_count, block_size, fields, theta_blocks)),
        swap(theta_blocks, 1),
        *map(hbm, (trial, chol)),
    )
    received = spread(pairs)
    partner, *received = lax.optimization_barrier((partner, *received))
    far = pl.pallas_call(
        spread_far_kernel,
        out_shape=jax.ShapeDtypeStruct((half, slots, bs, nocc), BF16),
        in_specs=[SMEM, VMEM, HBM],
        out_specs=VMEM,
        compiler_params=params,
        cost_estimate=pl.CostEstimate(flops=0, bytes_accessed=8 * chol.size, transcendentals=0),
        name="spread",
    )(cols, partner, hbm(chol))
    groups = [list(range(half)), list(range(half, owners))]
    far = to_all(far, groups)

    part = pl.pallas_call(
        functools.partial(bias_pair_kernel, step),
        out_shape=jax.ShapeDtypeStruct((owners, owners, gs), F32),
        in_specs=[VMEM] * (5 + near),
        out_specs=VMEM,
        scratch_shapes=[pltpu.VMEM((slots, bs * owners, bs), F32), pltpu.VMEM((owners, gs), F32)],
        compiler_params=params,
        name="bias",
    )(rows, mask, draws, chol, far, *received)

    operators, own_bias = pl.pallas_call(
        operator_pair_kernel,
        out_shape=(
            jax.ShapeDtypeStruct((owners, 1, slots, bs, bs), BF16),
            jax.ShapeDtypeStruct((1, gs), F32),
        ),
        in_specs=[VMEM] * 4,
        out_specs=(VMEM, VMEM),
        scratch_shapes=[pltpu.VMEM((owners, gs), F32), pltpu.VMEM((slots, owners * bs, bs), F32)],
        compiler_params=params,
        name="operator",
    )(to_all(part), draws, mask, chol)

    propagated = pl.pallas_call(
        update_kernel,
        out_shape=jax.ShapeDtypeStruct(theta_blocks.shape, BF16),
        in_specs=[SMEM, VMEM, VMEM],
        out_specs=VMEM,
        compiler_params=params,
        name="update",
    )(where, theta_blocks, to_all(operators))
    return propagated.reshape(theta.shape), own_bias


def per_device(theta, trial, chol, fields, tile_info, tile_count, block_size):
    short = lax.axis_size("blk") in (8, 16)
    one_slab = fields.shape[1] == chol.shape[1]
    plan = short_axis if short and one_slab and theta.shape[0] == 1 else long_axis
    return plan(theta, trial, chol, fields, tile_info, tile_count, block_size)


def solution(mesh):
    placed = (
        P(("grp", "blk"), None, None),
        P("grp", None),
        P(("grp", "blk"), None, None),
        P(("grp", "blk"), None),
        P("grp", None),
        P("grp"),
        P("grp"),
    )
    return jax.shard_map(
        per_device,
        mesh=mesh,
        in_specs=placed,
        out_specs=(P(("grp", "blk"), None, None), P(("grp", "blk"), None)),
        check_vma=False,
    )
```

```python
import functools

import jax
import jax.numpy as jnp
from jax import lax
from jax.experimental import pallas as pl
from jax.experimental.pallas import tpu as pltpu
from jax.sharding import PartitionSpec as P

STEP_ROOT = 0.25
PIECES = 8
F32 = jnp.float32
BF16 = jnp.bfloat16
LIMIT = 24 * 1024 * 1024
VMEM = pl.BlockSpec(memory_space=pltpu.VMEM)
SMEM = pl.BlockSpec(memory_space=pltpu.SMEM)
HBM = pl.BlockSpec(memory_space=pltpu.HBM)
ANY = pl.BlockSpec(memory_space=pl.ANY)
NT = (((1,), (1,)), ((), ()))


def each(count, body):
    if count <= 16:
        for index in range(count):
            body(index)
    else:

        def step(index, carry):
            body(index)
            return carry

        lax.fori_loop(0, count, step, 0, unroll=8)


def pick_kernel(
    info_hbm, count_hbm, size_hbm, fields_hbm, theta_ref, trial_ref, chol_ref,
    out_ref, rows_ref, mask_ref, draws_ref, where_ref, info_ref, count_ref, size_ref, fields_ref, sems,
):
    owners, walk, slots, bs, _ = out_ref.shape
    blocks = theta_ref.shape[1]
    small = [
        pltpu.make_async_copy(source, target, sems.at[2 + n])
        for n, (source, target) in enumerate(
            [(info_hbm, info_ref), (count_hbm, count_ref), (size_hbm, size_ref), (fields_hbm, fields_ref)]
        )
    ]
    for copy in small:
        copy.start()
    small[0].wait()
    copies = []
    for o in range(owners):
        for j in range(slots):
            block = info_ref[1, o * slots + j]
            for w in range(walk):
                copies.append(pltpu.make_async_copy(theta_ref.at[w, block], out_ref.at[o, w, j], sems.at[0]))
    me = lax.axis_index("blk")
    for j in range(slots):
        block = info_ref[0, me * slots + j]
        copies.append(
            pltpu.make_async_copy(
                trial_ref.at[pl.ds(pl.multiple_of(block * bs, bs), bs), :], rows_ref.at[j], sems.at[1]
            )
        )
    for copy in copies:
        copy.start()
    for copy in small[1:]:
        copy.wait()
    live = count_ref[me]
    for j in range(slots):
        row_size = jnp.where(j < live, size_ref[info_ref[0, me * slots + j]], 0)
        col_size = size_ref[info_ref[1, me * slots + j]]
        rows = lax.broadcasted_iota(jnp.int32, (bs, bs), 0) < row_size
        cols = lax.broadcasted_iota(jnp.int32, (bs, bs), 1) < col_size
        mask_ref[j] = jnp.where(rows & cols, 1.0, 0.0)
    draws_ref[...] = jnp.broadcast_to(fields_ref[0:1, :], draws_ref.shape)
    for o in range(owners):
        for j in range(slots):

            @pl.when(j < count_ref[o])
            def _(s=o * slots + j):
                row_block = info_ref[0, s]
                side = info_ref[1, s] - row_block + 1
                where_ref[(info_ref[2, s] * blocks + row_block) * 3 + side] = jnp.int32(s)

    pltpu.make_async_copy(out_ref, out_ref, sems.at[0]).wait()
    pltpu.make_async_copy(rows_ref, rows_ref, sems.at[1]).wait()


def bias_kernel(
    spread, recv_ref, rows_ref, mask_ref, draws_ref, chol_ref, out_ref, green_ref, bias_ref
):
    owners, walk, slots, bs, _ = recv_ref.shape
    walkers = owners * walk
    for slot in range(slots):

        def one(w, slot=slot):
            block = recv_ref[w // walk, w % walk, slot]
            green = lax.dot_general(rows_ref[slot], block, NT, preferred_element_type=F32)
            green_ref[slot, pl.ds(w, bs, stride=walkers), :] = green * mask_ref[slot]

        each(walkers, one)
    per = bs // PIECES
    for slot in range(slots):
        bias = jnp.zeros((walkers, chol_ref.shape[1]), F32)
        for c in range(PIECES):
            base = c * per * walkers
            left = jnp.concatenate(
                [green_ref[slot, pl.ds(base + p * walkers, walkers), :].astype(BF16) for p in range(per)],
                axis=1,
            )
            right = chol_ref[slot, :, pl.ds(c * per * bs, per * bs)]
            bias += lax.dot_general(left, right, NT, preferred_element_type=F32)
        bias_ref[slot] = bias

    if spread:
        total = sum(bias_ref[slot] for slot in range(slots))
        for o in range(owners):
            out_ref[o, :walkers, :] = total
            out_ref[o, pl.ds(walkers, 8), :] = draws_ref[...]
    else:
        out_ref[...] = bias_ref[...]


def operator_kernel(spread, *refs):
    if spread:
        bias_ref, mask_ref, chol_ref, out_ref, own_ref, shifted_ref, oper_ref = refs
    else:
        info_ref, bias_ref, fields_ref, mask_ref, chol_ref, out_ref, own_ref, shifted_ref, oper_ref = refs
    owners, walk, slots, bs, _ = out_ref.shape
    walkers = owners * walk
    gs = chol_ref.shape[1]
    me = lax.axis_index("blk")
    if spread:
        rows = walkers + 8
        bias = sum(bias_ref[pl.ds(o * rows, walkers), :] for o in range(owners))
        fields = bias_ref[pl.ds(walkers, owners, stride=rows), :]
        shifted_ref[...] = bias
        own_ref[...] = shifted_ref[pl.ds(me, 1), :]
    else:
        bias = bias_ref[...]
        fields = fields_ref[...]
        own_ref[...] = bias_ref[pl.ds(me * walk, walk), :]
    shifted_ref[...] = fields - bias
    for slot in range(slots):
        slab = 0 if spread else pl.multiple_of(info_ref[2, me * slots + slot] * gs, gs)
        left = shifted_ref[:, pl.ds(slab, gs)].astype(BF16)
        per = bs // PIECES
        for c in range(PIECES):
            right = chol_ref[slot, :, pl.ds(c * per * bs, per * bs)]
            oper = jnp.dot(left, right, preferred_element_type=F32) * STEP_ROOT
            for p in range(per):
                oper_ref[pl.ds(c * per + p, walkers, stride=bs), :] = oper[:, p * bs : (p + 1) * bs]

        def one(w, slot=slot):
            block = oper_ref[pl.ds(w * bs, bs), :]
            out_ref[w // walk, w % walk, slot] = (block * mask_ref[slot]).astype(BF16)

        each(walkers, one)


def update_kernel(where_ref, theta_ref, oper_ref, out_ref):
    owners, walk, slots, bs, _ = oper_ref.shape
    blocks = theta_ref.shape[1]
    slabs = where_ref.shape[0] // (3 * blocks)
    for w in range(walk):
        for row_block in range(blocks):
            total = theta_ref[w, row_block].astype(F32)
            for col_block in range(max(row_block - 1, 0), min(row_block + 2, blocks)):
                for slab in range(slabs):
                    s = where_ref[(slab * blocks + row_block) * 3 + col_block - row_block + 1]
                    total += jnp.dot(
                        oper_ref[s // slots, w, s % slots], theta_ref[w, col_block],
                        preferred_element_type=F32,
                    )
            out_ref[w, row_block] = total.astype(BF16)


def long_axis(theta, trial, chol, fields, tile_info, tile_count, block_size):
    owners = lax.axis_size("blk")
    walk, norb, nocc = theta.shape
    walkers = walk * owners
    slots, gs, _ = chol.shape
    nchol = fields.shape[1]
    blocks = block_size.shape[0]
    bs = norb // blocks
    slabs = nchol // gs
    spread = slabs == 1 and walk == 1
    params = pltpu.CompilerParams(vmem_limit_bytes=LIMIT)
    theta_blocks = theta.reshape(walk, blocks, bs, nocc)

    outgoing, rows, mask, draws, where = pl.pallas_call(
        pick_kernel,
        out_shape=(
            jax.ShapeDtypeStruct((owners, walk, slots, bs, nocc), BF16),
            jax.ShapeDtypeStruct((slots, bs, nocc), BF16),
            jax.ShapeDtypeStruct((slots, bs, bs), F32),
            jax.ShapeDtypeStruct((8, nchol), F32),
            jax.ShapeDtypeStruct((slabs * blocks * 3,), jnp.int32),
        ),
        in_specs=[HBM] * 7,
        out_specs=(VMEM, VMEM, VMEM, VMEM, SMEM),
        scratch_shapes=[
            pltpu.SMEM(tile_info.shape, jnp.int32),
            pltpu.SMEM(tile_count.shape, jnp.int32),
            pltpu.SMEM(block_size.shape, jnp.int32),
            pltpu.VMEM(fields.shape, F32),
            pltpu.SemaphoreType.DMA((6,)),
        ],
        compiler_params=params,
        cost_estimate=pl.CostEstimate(flops=0, bytes_accessed=4 * chol.size * 2, transcendentals=0),
        name="pick",
    )(*(pltpu.with_memory_space_constraint(x, pltpu.HBM)
        for x in (tile_info, tile_count, block_size, fields, theta_blocks, trial, chol)))
    received = lax.all_to_all(outgoing, "blk", split_axis=0, concat_axis=0, tiled=True)

    part_shape = (owners, walkers + 8, gs) if spread else (slots, walkers, gs)
    part = pl.pallas_call(
        functools.partial(bias_kernel, spread),
        out_shape=jax.ShapeDtypeStruct(part_shape, F32),
        in_specs=[VMEM] * 5,
        out_specs=VMEM,
        scratch_shapes=[
            pltpu.VMEM((slots, bs * walkers, bs), F32),
            pltpu.VMEM((slots, walkers, gs), F32),
        ],
        compiler_params=params,
        name="bias",
    )(received, rows, mask, draws, chol)

    if spread:
        bias_in = lax.all_to_all(part, "blk", split_axis=0, concat_axis=0, tiled=True)
        inputs = (bias_in.reshape(owners * (walkers + 8), gs),)
    else:
        me = lax.axis_index("blk")
        local = jnp.zeros((walkers, nchol), F32)
        for slot in range(slots):
            start = (0, tile_info[2, me * slots + slot] * gs)
            old = lax.dynamic_slice(local, start, (walkers, gs))
            local = lax.dynamic_update_slice(local, old + part[slot], start)
        inputs = (tile_info, lax.psum(local, "blk"), lax.all_gather(fields, "blk", axis=0, tiled=True))

    operators, own_bias = pl.pallas_call(
        functools.partial(operator_kernel, spread),
        out_shape=(
            jax.ShapeDtypeStruct((owners, walk, slots, bs, bs), BF16),
            jax.ShapeDtypeStruct((walk, nchol), F32),
        ),
        in_specs=([VMEM] if spread else [SMEM, VMEM, VMEM]) + [VMEM, VMEM],
        out_specs=(VMEM, VMEM),
        scratch_shapes=[
            pltpu.VMEM((walkers, nchol), F32),
            pltpu.VMEM((walkers * bs, bs), F32),
        ],
        compiler_params=params,
        name="operator",
    )(*inputs, mask, chol)
    arrived = lax.all_to_all(operators, "blk", split_axis=0, concat_axis=0, tiled=True)

    propagated = pl.pallas_call(
        update_kernel,
        out_shape=jax.ShapeDtypeStruct(theta_blocks.shape, BF16),
        in_specs=[SMEM, VMEM, VMEM],
        out_specs=VMEM,
        compiler_params=params,
        name="update",
    )(where, theta_blocks, arrived)
    return propagated.reshape(theta.shape), own_bias


def pick_pair_kernel(info_hbm, theta_hbm, other_ref, _, *refs):
    pair_refs = refs[:-3]
    info_ref, theta_ref, sems = refs[-3:]
    slots = pair_refs[0].shape[1]
    copies = [
        pltpu.make_async_copy(info_hbm, info_ref, sems.at[0]),
        pltpu.make_async_copy(theta_hbm, theta_ref, sems.at[1]),
    ]
    for copy in copies:
        copy.start()
    me = lax.axis_index("blk")
    core = me % 2
    for copy in copies:
        copy.wait()
    for r, ref in enumerate(pair_refs):
        for j in range(slots):
            block = info_ref[1, (me ^ (2 * r)) * slots + j]
            ref[core, j] = theta_ref[0, block]
            ref[1 - core, j] = other_ref[0, block]


def prepare_kernel(
    info_hbm, count_hbm, size_hbm, fields_hbm, trial_ref,
    rows_ref, mask_ref, draws_ref, where_ref, cols_ref, info_ref, count_ref, size_ref, fields_ref, sems,
):
    slots, bs, _ = rows_ref.shape
    owners = count_ref.shape[0]
    small = [
        pltpu.make_async_copy(source, target, sems.at[n])
        for n, (source, target) in enumerate(
            [(info_hbm, info_ref), (count_hbm, count_ref), (size_hbm, size_ref), (fields_hbm, fields_ref)]
        )
    ]
    for copy in small:
        copy.start()
    me = lax.axis_index("blk")
    for copy in small:
        copy.wait()
    trial = []
    for j in range(slots):
        block = info_ref[0, me * slots + j]
        trial.append(
            pltpu.make_async_copy(
                trial_ref.at[pl.ds(pl.multiple_of(block * bs, bs), bs), :], rows_ref.at[j], sems.at[4 + j]
            )
        )
        trial[-1].start()
    first = me // (owners // 2) * (owners // 2) * slots
    for n in range(owners // 2 * slots):
        cols_ref[n] = info_ref[1, first + n]
    live = count_ref[me]
    for j in range(slots):
        row_size = jnp.where(j < live, size_ref[info_ref[0, me * slots + j]], 0)
        col_size = size_ref[info_ref[1, me * slots + j]]
        rows = lax.broadcasted_iota(jnp.int32, (bs, bs), 0) < row_size
        cols = lax.broadcasted_iota(jnp.int32, (bs, bs), 1) < col_size
        mask_ref[j] = jnp.where(rows & cols, 1.0, 0.0)
    draws_ref[...] = jnp.broadcast_to(fields_ref[0:1, :], draws_ref.shape)
    for o in range(owners):
        for j in range(slots):

            @pl.when(j < count_ref[o])
            def _(s=o * slots + j):
                row_block = info_ref[0, s]
                where_ref[row_block * 3 + info_ref[1, s] - row_block + 1] = jnp.int32(s)

    for copy in trial:
        copy.wait()


def spread_far_kernel(cols_ref, theta_ref, _, out_ref):
    slots = out_ref.shape[1]
    for k in range(out_ref.shape[0]):
        for j in range(slots):
            out_ref[k, j] = theta_ref[0, cols_ref[k * slots + j]]


def bias_pair_kernel(step, rows_ref, mask_ref, draws_ref, chol_ref, far_ref, *refs):
    pair_refs = refs[:-3]
    out_ref, green_ref, total_ref = refs[-3:]
    half, slots, bs, nocc = far_ref.shape
    walkers = 2 * half
    me = lax.axis_index("blk")
    first = me // half * half
    pitch = walkers + 1
    for slot in range(slots):
        mask = mask_ref[slot]
        for blocks, start in [(ref[:, slot], 2 * r) for r, ref in enumerate(pair_refs)] + [(far_ref[:, slot], half)]:
            count = blocks.shape[0]
            green = lax.dot_general(
                rows_ref[slot], blocks.reshape(count * bs, nocc), NT, preferred_element_type=F32
            )
            for n in range(count):
                green_ref[slot, pl.ds(start + n, bs, stride=pitch), :] = green[:, n * bs : (n + 1) * bs] * mask
    per = bs // PIECES
    tall = jnp.zeros((chol_ref.shape[1], walkers), F32)
    wide = jnp.zeros((walkers, chol_ref.shape[1]), F32)
    for c in range(PIECES):
        for slot in range(slots):
            green = jnp.concatenate(
                [green_ref[slot, pl.ds((c * per + p) * pitch, walkers), :].astype(BF16) for p in range(per)],
                axis=1,
            )
            tile = chol_ref[slot, :, pl.ds(c * per * bs, per * bs)]
            if slot % 2:
                wide += lax.dot_general(green, tile, NT, preferred_element_type=F32)
            else:
                tall += lax.dot_general(tile, green, NT, preferred_element_type=F32)
    total = -(tall.T + wide)
    for n in range(walkers):
        walker = (me // 2 ^ (n // 2)) * 2 + n % 2 if n < half else (first + n - half) ^ step
        total_ref[pl.ds(walker, 1), :] = total[n : n + 1, :]
    total = total_ref[...]
    own = total_ref[pl.ds(me, 1), :]
    for o in range(walkers):
        out_ref[o] = total
        out_ref[o, pl.ds(me, 1), :] = jnp.where(o == me, own, own + draws_ref[0:1, :])


def operator_pair_kernel(shift_ref, fields_ref, mask_ref, chol_ref, out_ref, own_ref, total_ref, oper_ref):
    walkers, _, slots, bs, _ = out_ref.shape
    me = lax.axis_index("blk")
    total_ref[...] = sum(shift_ref[o] for o in range(walkers))
    own = total_ref[pl.ds(me, 1), :]
    own_ref[...] = -own
    total_ref[pl.ds(me, 1), :] = own + fields_ref[0:1, :]
    left = total_ref[...].astype(BF16)
    per = bs // PIECES
    pitch = bs + 8
    for slot in range(slots):
        for c in range(PIECES):
            right = chol_ref[slot, :, pl.ds(c * per * bs, per * bs)]
            oper = jnp.dot(left, right, preferred_element_type=F32) * STEP_ROOT
            for p in range(per):
                oper_ref[slot, pl.ds(c * per + p, walkers, stride=pitch), :] = oper[:, p * bs : (p + 1) * bs]
        for w in range(walkers):
            block = oper_ref[slot, pl.ds(w * pitch, bs), :]
            out_ref[w, 0, slot] = (block * mask_ref[slot]).astype(BF16)


def short_axis(theta, trial, chol, fields, tile_info, tile_count, block_size):
    owners = lax.axis_size("blk")
    _, norb, nocc = theta.shape
    slots, gs, _ = chol.shape
    blocks = block_size.shape[0]
    bs = norb // blocks
    half = owners // 2
    step = half + half // 2
    near = half // 2
    params = pltpu.CompilerParams(vmem_limit_bytes=LIMIT)
    theta_blocks = theta.reshape(1, blocks, bs, nocc)

    def swap(x, step):
        return lax.ppermute(x, "blk", [(i, i ^ step) for i in range(owners)])

    def to_all(x, groups=None):
        return lax.all_to_all(x, "blk", split_axis=0, concat_axis=0, tiled=True, axis_index_groups=groups)

    def spread(pairs):
        return [pairs[0]] + [swap(pairs[r], 2 * r) for r in range(1, near)]

    hbm = functools.partial(pltpu.with_memory_space_constraint, memory_space=pltpu.HBM)
    pair_shapes = (jax.ShapeDtypeStruct((2, slots, bs, nocc), BF16),) * near
    partner = swap(theta_blocks, step)
    load = pl.CostEstimate(flops=0, bytes_accessed=8 * chol.size, transcendentals=0)
    pairs = pl.pallas_call(
        pick_pair_kernel,
        out_shape=pair_shapes,
        in_specs=[HBM, HBM, VMEM, HBM],
        out_specs=(VMEM,) * near,
        scratch_shapes=[
            pltpu.SMEM(tile_info.shape, jnp.int32),
            pltpu.VMEM(theta_blocks.shape, BF16),
            pltpu.SemaphoreType.DMA((2,)),
        ],
        compiler_params=params,
        cost_estimate=load,
        name="pick",
    )(hbm(tile_info), hbm(theta_blocks), swap(theta_blocks, 1), hbm(chol))
    rows, mask, draws, where, cols = pl.pallas_call(
        prepare_kernel,
        out_shape=(
            jax.ShapeDtypeStruct((slots, bs, nocc), BF16),
            jax.ShapeDtypeStruct((slots, bs, bs), F32),
            jax.ShapeDtypeStruct((8, gs), F32),
            jax.ShapeDtypeStruct((3 * blocks,), jnp.int32),
            jax.ShapeDtypeStruct((half * slots,), jnp.int32),
        ),
        in_specs=[HBM] * 5,
        out_specs=(VMEM, VMEM, VMEM, SMEM, SMEM),
        scratch_shapes=[
            pltpu.SMEM(tile_info.shape, jnp.int32),
            pltpu.SMEM(tile_count.shape, jnp.int32),
            pltpu.SMEM(block_size.shape, jnp.int32),
            pltpu.VMEM(fields.shape, F32),
            pltpu.SemaphoreType.DMA((4 + slots,)),
        ],
        compiler_params=params,
        name="prepare",
    )(*map(hbm, (tile_info, tile_count, block_size, fields, trial)))
    received = spread(pairs)
    far = pl.pallas_call(
        spread_far_kernel,
        out_shape=jax.ShapeDtypeStruct((half, slots, bs, nocc), BF16),
        in_specs=[SMEM, VMEM, HBM],
        out_specs=VMEM,
        compiler_params=params,
        cost_estimate=load,
        name="spread",
    )(cols, partner, hbm(chol))
    groups = [list(range(half)), list(range(half, owners))]
    far, *received = lax.optimization_barrier((far, *received))
    far = to_all(far, groups)

    part = pl.pallas_call(
        functools.partial(bias_pair_kernel, step),
        out_shape=jax.ShapeDtypeStruct((owners, owners, gs), F32),
        in_specs=[VMEM] * (5 + near),
        out_specs=VMEM,
        scratch_shapes=[pltpu.VMEM((slots, (bs + 1) * (owners + 1), bs), F32), pltpu.VMEM((owners, gs), F32)],
        compiler_params=params,
        name="bias",
    )(rows, mask, draws, chol, far, *received)

    operators, own_bias = pl.pallas_call(
        operator_pair_kernel,
        out_shape=(
            jax.ShapeDtypeStruct((owners, 1, slots, bs, bs), BF16),
            jax.ShapeDtypeStruct((1, gs), F32),
        ),
        in_specs=[VMEM] * 4,
        out_specs=(VMEM, VMEM),
        scratch_shapes=[pltpu.VMEM((owners, gs), F32), pltpu.VMEM((slots, (owners + 1) * (bs + 8), bs), F32)],
        compiler_params=params,
        name="operator",
    )(to_all(part), draws, mask, chol)

    propagated = pl.pallas_call(
        update_kernel,
        out_shape=jax.ShapeDtypeStruct(theta_blocks.shape, BF16),
        in_specs=[SMEM, VMEM, VMEM],
        out_specs=VMEM,
        compiler_params=params,
        name="update",
    )(where, theta_blocks, to_all(operators))
    return propagated.reshape(theta.shape), own_bias


def per_device(theta, trial, chol, fields, tile_info, tile_count, block_size):
    short = lax.axis_size("blk") in (8, 16)
    one_slab = fields.shape[1] == chol.shape[1]
    plan = short_axis if short and one_slab and theta.shape[0] == 1 else long_axis
    return plan(theta, trial, chol, fields, tile_info, tile_count, block_size)


def solution(mesh):
    placed = (
        P(("grp", "blk"), None, None),
        P("grp", None),
        P(("grp", "blk"), None, None),
        P(("grp", "blk"), None),
        P("grp", None),
        P("grp"),
        P("grp"),
    )
    return jax.shard_map(
        per_device,
        mesh=mesh,
        in_specs=placed,
        out_specs=(P(("grp", "blk"), None, None), P(("grp", "blk"), None)),
        check_vma=False,
    )
```

```python
import functools

import jax
import jax.numpy as jnp
from jax import lax
from jax.experimental import pallas as pl
from jax.experimental.pallas import tpu as pltpu
from jax.sharding import PartitionSpec as P

STEP_ROOT = 0.25
PIECES = 8
F32 = jnp.float32
BF16 = jnp.bfloat16
LIMIT = 24 * 1024 * 1024
VMEM = pl.BlockSpec(memory_space=pltpu.VMEM)
SMEM = pl.BlockSpec(memory_space=pltpu.SMEM)
HBM = pl.BlockSpec(memory_space=pltpu.HBM)
ANY = pl.BlockSpec(memory_space=pl.ANY)
NT = (((1,), (1,)), ((), ()))


def each(count, body):
    if count <= 16:
        for index in range(count):
            body(index)
    else:

        def step(index, carry):
            body(index)
            return carry

        lax.fori_loop(0, count, step, 0, unroll=8)


def pick_kernel(
    info_hbm, count_hbm, size_hbm, fields_hbm, theta_ref, trial_ref, chol_ref,
    out_ref, rows_ref, mask_ref, draws_ref, where_ref, info_ref, count_ref, size_ref, fields_ref, sems,
):
    owners, walk, slots, bs, _ = out_ref.shape
    blocks = theta_ref.shape[1]
    small = [
        pltpu.make_async_copy(source, target, sems.at[2 + n])
        for n, (source, target) in enumerate(
            [(info_hbm, info_ref), (count_hbm, count_ref), (size_hbm, size_ref), (fields_hbm, fields_ref)]
        )
    ]
    for copy in small:
        copy.start()
    small[0].wait()
    copies = []
    for o in range(owners):
        for j in range(slots):
            block = info_ref[1, o * slots + j]
            for w in range(walk):
                copies.append(pltpu.make_async_copy(theta_ref.at[w, block], out_ref.at[o, w, j], sems.at[0]))
    me = lax.axis_index("blk")
    for j in range(slots):
        block = info_ref[0, me * slots + j]
        copies.append(
            pltpu.make_async_copy(
                trial_ref.at[pl.ds(pl.multiple_of(block * bs, bs), bs), :], rows_ref.at[j], sems.at[1]
            )
        )
    for copy in copies:
        copy.start()
    for copy in small[1:]:
        copy.wait()
    live = count_ref[me]
    for j in range(slots):
        row_size = jnp.where(j < live, size_ref[info_ref[0, me * slots + j]], 0)
        col_size = size_ref[info_ref[1, me * slots + j]]
        rows = lax.broadcasted_iota(jnp.int32, (bs, bs), 0) < row_size
        cols = lax.broadcasted_iota(jnp.int32, (bs, bs), 1) < col_size
        mask_ref[j] = jnp.where(rows & cols, 1.0, 0.0)
    draws_ref[...] = jnp.broadcast_to(fields_ref[0:1, :], draws_ref.shape)
    for o in range(owners):
        for j in range(slots):

            @pl.when(j < count_ref[o])
            def _(s=o * slots + j):
                row_block = info_ref[0, s]
                side = info_ref[1, s] - row_block + 1
                where_ref[(info_ref[2, s] * blocks + row_block) * 3 + side] = jnp.int32(s)

    pltpu.make_async_copy(out_ref, out_ref, sems.at[0]).wait()
    pltpu.make_async_copy(rows_ref, rows_ref, sems.at[1]).wait()


def bias_kernel(
    spread, recv_ref, rows_ref, mask_ref, draws_ref, chol_ref, out_ref, green_ref, bias_ref
):
    owners, walk, slots, bs, _ = recv_ref.shape
    walkers = owners * walk
    for slot in range(slots):

        def one(w, slot=slot):
            block = recv_ref[w // walk, w % walk, slot]
            green = lax.dot_general(rows_ref[slot], block, NT, preferred_element_type=F32)
            green_ref[slot, pl.ds(w, bs, stride=walkers), :] = green * mask_ref[slot]

        each(walkers, one)
    per = bs // PIECES
    for slot in range(slots):
        bias = jnp.zeros((walkers, chol_ref.shape[1]), F32)
        for c in range(PIECES):
            base = c * per * walkers
            left = jnp.concatenate(
                [green_ref[slot, pl.ds(base + p * walkers, walkers), :].astype(BF16) for p in range(per)],
                axis=1,
            )
            right = chol_ref[slot, :, pl.ds(c * per * bs, per * bs)]
            bias += lax.dot_general(left, right, NT, preferred_element_type=F32)
        bias_ref[slot] = bias

    if spread:
        total = sum(bias_ref[slot] for slot in range(slots))
        for o in range(owners):
            out_ref[o, :walkers, :] = total
            out_ref[o, pl.ds(walkers, 8), :] = draws_ref[...]
    else:
        out_ref[...] = bias_ref[...]


def operator_kernel(spread, *refs):
    if spread:
        bias_ref, mask_ref, chol_ref, out_ref, own_ref, shifted_ref, oper_ref = refs
    else:
        info_ref, bias_ref, fields_ref, mask_ref, chol_ref, out_ref, own_ref, shifted_ref, oper_ref = refs
    owners, walk, slots, bs, _ = out_ref.shape
    walkers = owners * walk
    gs = chol_ref.shape[1]
    me = lax.axis_index("blk")
    if spread:
        rows = walkers + 8
        bias = sum(bias_ref[pl.ds(o * rows, walkers), :] for o in range(owners))
        fields = bias_ref[pl.ds(walkers, owners, stride=rows), :]
        shifted_ref[...] = bias
        own_ref[...] = shifted_ref[pl.ds(me, 1), :]
    else:
        bias = bias_ref[...]
        fields = fields_ref[...]
        own_ref[...] = bias_ref[pl.ds(me * walk, walk), :]
    shifted_ref[...] = fields - bias
    for slot in range(slots):
        slab = 0 if spread else pl.multiple_of(info_ref[2, me * slots + slot] * gs, gs)
        left = shifted_ref[:, pl.ds(slab, gs)].astype(BF16)
        per = bs // PIECES
        for c in range(PIECES):
            right = chol_ref[slot, :, pl.ds(c * per * bs, per * bs)]
            oper = jnp.dot(left, right, preferred_element_type=F32) * STEP_ROOT
            for p in range(per):
                oper_ref[pl.ds(c * per + p, walkers, stride=bs), :] = oper[:, p * bs : (p + 1) * bs]

        def one(w, slot=slot):
            block = oper_ref[pl.ds(w * bs, bs), :]
            out_ref[w // walk, w % walk, slot] = (block * mask_ref[slot]).astype(BF16)

        each(walkers, one)


def update_kernel(where_ref, theta_ref, oper_ref, out_ref):
    owners, walk, slots, bs, _ = oper_ref.shape
    blocks = theta_ref.shape[1]
    slabs = where_ref.shape[0] // (3 * blocks)
    for w in range(walk):
        for row_block in range(blocks):
            total = theta_ref[w, row_block].astype(F32)
            for col_block in range(max(row_block - 1, 0), min(row_block + 2, blocks)):
                for slab in range(slabs):
                    s = where_ref[(slab * blocks + row_block) * 3 + col_block - row_block + 1]
                    total += jnp.dot(
                        oper_ref[s // slots, w, s % slots], theta_ref[w, col_block],
                        preferred_element_type=F32,
                    )
            out_ref[w, row_block] = total.astype(BF16)


def long_axis(theta, trial, chol, fields, tile_info, tile_count, block_size):
    owners = lax.axis_size("blk")
    walk, norb, nocc = theta.shape
    walkers = walk * owners
    slots, gs, _ = chol.shape
    nchol = fields.shape[1]
    blocks = block_size.shape[0]
    bs = norb // blocks
    slabs = nchol // gs
    spread = slabs == 1 and walk == 1
    params = pltpu.CompilerParams(vmem_limit_bytes=LIMIT)
    theta_blocks = theta.reshape(walk, blocks, bs, nocc)

    outgoing, rows, mask, draws, where = pl.pallas_call(
        pick_kernel,
        out_shape=(
            jax.ShapeDtypeStruct((owners, walk, slots, bs, nocc), BF16),
            jax.ShapeDtypeStruct((slots, bs, nocc), BF16),
            jax.ShapeDtypeStruct((slots, bs, bs), F32),
            jax.ShapeDtypeStruct((8, nchol), F32),
            jax.ShapeDtypeStruct((slabs * blocks * 3,), jnp.int32),
        ),
        in_specs=[HBM] * 7,
        out_specs=(VMEM, VMEM, VMEM, VMEM, SMEM),
        scratch_shapes=[
            pltpu.SMEM(tile_info.shape, jnp.int32),
            pltpu.SMEM(tile_count.shape, jnp.int32),
            pltpu.SMEM(block_size.shape, jnp.int32),
            pltpu.VMEM(fields.shape, F32),
            pltpu.SemaphoreType.DMA((6,)),
        ],
        compiler_params=params,
        cost_estimate=pl.CostEstimate(flops=0, bytes_accessed=4 * chol.size * 2, transcendentals=0),
        name="pick",
    )(*(pltpu.with_memory_space_constraint(x, pltpu.HBM)
        for x in (tile_info, tile_count, block_size, fields, theta_blocks, trial, chol)))
    received = lax.all_to_all(outgoing, "blk", split_axis=0, concat_axis=0, tiled=True)

    part_shape = (owners, walkers + 8, gs) if spread else (slots, walkers, gs)
    part = pl.pallas_call(
        functools.partial(bias_kernel, spread),
        out_shape=jax.ShapeDtypeStruct(part_shape, F32),
        in_specs=[VMEM] * 5,
        out_specs=VMEM,
        scratch_shapes=[
            pltpu.VMEM((slots, bs * walkers, bs), F32),
            pltpu.VMEM((slots, walkers, gs), F32),
        ],
        compiler_params=params,
        name="bias",
    )(received, rows, mask, draws, chol)

    if spread:
        bias_in = lax.all_to_all(part, "blk", split_axis=0, concat_axis=0, tiled=True)
        inputs = (bias_in.reshape(owners * (walkers + 8), gs),)
    else:
        me = lax.axis_index("blk")
        local = jnp.zeros((walkers, nchol), F32)
        for slot in range(slots):
            start = (0, tile_info[2, me * slots + slot] * gs)
            old = lax.dynamic_slice(local, start, (walkers, gs))
            local = lax.dynamic_update_slice(local, old + part[slot], start)
        inputs = (tile_info, lax.psum(local, "blk"), lax.all_gather(fields, "blk", axis=0, tiled=True))

    operators, own_bias = pl.pallas_call(
        functools.partial(operator_kernel, spread),
        out_shape=(
            jax.ShapeDtypeStruct((owners, walk, slots, bs, bs), BF16),
            jax.ShapeDtypeStruct((walk, nchol), F32),
        ),
        in_specs=([VMEM] if spread else [SMEM, VMEM, VMEM]) + [VMEM, VMEM],
        out_specs=(VMEM, VMEM),
        scratch_shapes=[
            pltpu.VMEM((walkers, nchol), F32),
            pltpu.VMEM((walkers * bs, bs), F32),
        ],
        compiler_params=params,
        name="operator",
    )(*inputs, mask, chol)
    arrived = lax.all_to_all(operators, "blk", split_axis=0, concat_axis=0, tiled=True)

    propagated = pl.pallas_call(
        update_kernel,
        out_shape=jax.ShapeDtypeStruct(theta_blocks.shape, BF16),
        in_specs=[SMEM, VMEM, VMEM],
        out_specs=VMEM,
        compiler_params=params,
        name="update",
    )(where, theta_blocks, arrived)
    return propagated.reshape(theta.shape), own_bias


def pick_pair_kernel(info_hbm, theta_hbm, other_ref, _, *refs):
    pair_refs = refs[:-3]
    info_ref, theta_ref, sems = refs[-3:]
    slots = pair_refs[0].shape[1]
    copies = [
        pltpu.make_async_copy(info_hbm, info_ref, sems.at[0]),
        pltpu.make_async_copy(theta_hbm, theta_ref, sems.at[1]),
    ]
    for copy in copies:
        copy.start()
    me = lax.axis_index("blk")
    core = me % 2
    for copy in copies:
        copy.wait()
    for r, ref in enumerate(pair_refs):
        for j in range(slots):
            block = info_ref[1, (me ^ (2 * r)) * slots + j]
            ref[core, j] = theta_ref[0, block]
            ref[1 - core, j] = other_ref[0, block]


def prepare_kernel(
    place, near_ring, info_hbm, count_hbm, size_hbm, fields_hbm, trial_ref,
    rows_ref, mask_ref, draws_ref, where_ref, cols_ref, info_ref, count_ref, size_ref, fields_ref, sems,
):
    slots, bs, _ = rows_ref.shape
    owners = count_ref.shape[0]
    small = [
        pltpu.make_async_copy(source, target, sems.at[n])
        for n, (source, target) in enumerate(
            [(info_hbm, info_ref), (count_hbm, count_ref), (size_hbm, size_ref), (fields_hbm, fields_ref)]
        )
    ]
    for copy in small:
        copy.start()
    me = lax.axis_index("blk")
    for copy in small:
        copy.wait()
    trial = []
    for j in range(slots):
        block = info_ref[0, me * slots + j]
        trial.append(
            pltpu.make_async_copy(
                trial_ref.at[pl.ds(pl.multiple_of(block * bs, bs), bs), :], rows_ref.at[j], sems.at[4 + j]
            )
        )
        trial[-1].start()
    first = me // len(near_ring) * len(near_ring)
    for n, k in enumerate(near_ring):
        for j in range(slots):
            cols_ref[n * slots + j] = info_ref[1, (first + k) * slots + j]
    live = count_ref[me]
    for j in range(slots):
        row_size = jnp.where(j < live, size_ref[info_ref[0, me * slots + j]], 0)
        col_size = size_ref[info_ref[1, me * slots + j]]
        rows = lax.broadcasted_iota(jnp.int32, (bs, bs), 0) < row_size
        cols = lax.broadcasted_iota(jnp.int32, (bs, bs), 1) < col_size
        mask_ref[j] = jnp.where(rows & cols, 1.0, 0.0)
    draws_ref[...] = jnp.broadcast_to(fields_ref[0:1, :], draws_ref.shape)
    for o in range(owners):
        for j in range(slots):

            @pl.when(j < count_ref[o])
            def _(s=o * slots + j, n=place[o] * slots + j):
                row_block = info_ref[0, s]
                where_ref[row_block * 3 + info_ref[1, s] - row_block + 1] = jnp.int32(n)

    for copy in trial:
        copy.wait()


def spread_far_kernel(cols_ref, theta_ref, _, out_ref):
    slots = out_ref.shape[1]
    for k in range(out_ref.shape[0]):
        for j in range(slots):
            out_ref[k, j] = theta_ref[0, cols_ref[k * slots + j]]


def bias_pair_kernel(step, ring, near_ring, rows_ref, mask_ref, draws_ref, chol_ref, far_ref, *refs):
    pair_refs = refs[:-3]
    out_ref, green_ref, total_ref = refs[-3:]
    half, slots, bs, nocc = far_ref.shape
    walkers = 2 * half
    me = lax.axis_index("blk")
    first = me // half * half
    pitch = walkers + 1
    for slot in range(slots):
        mask = mask_ref[slot]
        for blocks, start in [(ref[:, slot], 2 * r) for r, ref in enumerate(pair_refs)] + [(far_ref[:, slot], half)]:
            count = blocks.shape[0]
            green = lax.dot_general(
                rows_ref[slot], blocks.reshape(count * bs, nocc), NT, preferred_element_type=F32
            )
            for n in range(count):
                green_ref[slot, pl.ds(start + n, bs, stride=pitch), :] = green[:, n * bs : (n + 1) * bs] * mask
    per = bs // PIECES
    tall = jnp.zeros((chol_ref.shape[1], walkers), F32)
    wide = jnp.zeros((walkers, chol_ref.shape[1]), F32)
    for c in range(PIECES):
        for slot in range(slots):
            green = jnp.concatenate(
                [green_ref[slot, pl.ds((c * per + p) * pitch, walkers), :].astype(BF16) for p in range(per)],
                axis=1,
            )
            tile = chol_ref[slot, :, pl.ds(c * per * bs, per * bs)]
            if slot % 2:
                wide += lax.dot_general(green, tile, NT, preferred_element_type=F32)
            else:
                tall += lax.dot_general(tile, green, NT, preferred_element_type=F32)
    total = -(tall.T + wide)
    for n in range(walkers):
        walker = (me // 2 ^ (n // 2)) * 2 + n % 2 if n < half else (first + near_ring[n - half]) ^ step
        total_ref[pl.ds(walker, 1), :] = total[n : n + 1, :]
    total = total_ref[...]
    own = total_ref[pl.ds(me, 1), :]
    for n, o in enumerate(ring):
        out_ref[n] = total
        out_ref[n, pl.ds(me, 1), :] = jnp.where(o == me, own, own + draws_ref[0:1, :])


def operator_pair_kernel(place, shift_ref, fields_ref, mask_ref, chol_ref, out_ref, own_ref, total_ref, oper_ref):
    walkers, _, slots, bs, _ = out_ref.shape
    me = lax.axis_index("blk")
    total_ref[...] = sum(shift_ref[o] for o in range(walkers))
    own = total_ref[pl.ds(me, 1), :]
    own_ref[...] = -own
    total_ref[pl.ds(me, 1), :] = own + fields_ref[0:1, :]
    left = total_ref[...].astype(BF16)
    per = bs // PIECES
    pitch = bs + 8
    for slot in range(slots):
        for c in range(PIECES):
            right = chol_ref[slot, :, pl.ds(c * per * bs, per * bs)]
            oper = jnp.dot(left, right, preferred_element_type=F32) * STEP_ROOT
            for p in range(per):
                oper_ref[slot, pl.ds(c * per + p, walkers, stride=pitch), :] = oper[:, p * bs : (p + 1) * bs]
        for w in range(walkers):
            block = oper_ref[slot, pl.ds(w * pitch, bs), :]
            out_ref[place[w], 0, slot] = (block * mask_ref[slot]).astype(BF16)


def short_axis(theta, trial, chol, fields, tile_info, tile_count, block_size):
    owners = lax.axis_size("blk")
    _, norb, nocc = theta.shape
    slots, gs, _ = chol.shape
    blocks = block_size.shape[0]
    bs = norb // blocks
    half = owners // 2
    step = half + half // 2
    near = half // 2
    chips = [*range(1, half, 2), *range(0, half, 2)[::-1]]
    ring = [2 * chip + core for chip in chips for core in (1, 0)]
    place = [ring.index(o) for o in range(owners)]
    near_ring = [2 * chip + core for chip in range(near) for core in (1, 0)]
    params = pltpu.CompilerParams(vmem_limit_bytes=LIMIT)
    theta_blocks = theta.reshape(1, blocks, bs, nocc)

    def swap(x, step):
        return lax.ppermute(x, "blk", [(i, i ^ step) for i in range(owners)])

    def to_all(x, groups=None):
        return lax.all_to_all(x, "blk", split_axis=0, concat_axis=0, tiled=True, axis_index_groups=groups)

    def spread(pairs):
        return [pairs[0]] + [swap(pairs[r], 2 * r) for r in range(1, near)]

    hbm = functools.partial(pltpu.with_memory_space_constraint, memory_space=pltpu.HBM)
    pair_shapes = (jax.ShapeDtypeStruct((2, slots, bs, nocc), BF16),) * near
    partner = swap(theta_blocks, step)
    load = pl.CostEstimate(flops=0, bytes_accessed=8 * chol.size, transcendentals=0)
    pairs = pl.pallas_call(
        pick_pair_kernel,
        out_shape=pair_shapes,
        in_specs=[HBM, HBM, VMEM, HBM],
        out_specs=(VMEM,) * near,
        scratch_shapes=[
            pltpu.SMEM(tile_info.shape, jnp.int32),
            pltpu.VMEM(theta_blocks.shape, BF16),
            pltpu.SemaphoreType.DMA((2,)),
        ],
        compiler_params=params,
        cost_estimate=load,
        name="pick",
    )(hbm(tile_info), hbm(theta_blocks), swap(theta_blocks, 1), hbm(chol))
    rows, mask, draws, where, cols = pl.pallas_call(
        functools.partial(prepare_kernel, place, near_ring),
        out_shape=(
            jax.ShapeDtypeStruct((slots, bs, nocc), BF16),
            jax.ShapeDtypeStruct((slots, bs, bs), F32),
            jax.ShapeDtypeStruct((8, gs), F32),
            jax.ShapeDtypeStruct((3 * blocks,), jnp.int32),
            jax.ShapeDtypeStruct((half * slots,), jnp.int32),
        ),
        in_specs=[HBM] * 5,
        out_specs=(VMEM, VMEM, VMEM, SMEM, SMEM),
        scratch_shapes=[
            pltpu.SMEM(tile_info.shape, jnp.int32),
            pltpu.SMEM(tile_count.shape, jnp.int32),
            pltpu.SMEM(block_size.shape, jnp.int32),
            pltpu.VMEM(fields.shape, F32),
            pltpu.SemaphoreType.DMA((4 + slots,)),
        ],
        compiler_params=params,
        name="prepare",
    )(*map(hbm, (tile_info, tile_count, block_size, fields, trial)))
    received = spread(pairs)
    far = pl.pallas_call(
        spread_far_kernel,
        out_shape=jax.ShapeDtypeStruct((half, slots, bs, nocc), BF16),
        in_specs=[SMEM, VMEM, HBM],
        out_specs=VMEM,
        compiler_params=params,
        cost_estimate=load,
        name="spread",
    )(cols, partner, hbm(chol))
    groups = [near_ring, [half + k for k in near_ring]]
    far, *received = lax.optimization_barrier((far, *received))
    far = to_all(far, groups)

    part = pl.pallas_call(
        functools.partial(bias_pair_kernel, step, ring, near_ring),
        out_shape=jax.ShapeDtypeStruct((owners, owners, gs), F32),
        in_specs=[VMEM] * (5 + near),
        out_specs=VMEM,
        scratch_shapes=[pltpu.VMEM((slots, (bs + 1) * (owners + 1), bs), F32), pltpu.VMEM((owners, gs), F32)],
        compiler_params=params,
        name="bias",
    )(rows, mask, draws, chol, far, *received)

    operators, own_bias = pl.pallas_call(
        functools.partial(operator_pair_kernel, place),
        out_shape=(
            jax.ShapeDtypeStruct((owners, 1, slots, bs, bs), BF16),
            jax.ShapeDtypeStruct((1, gs), F32),
        ),
        in_specs=[VMEM] * 4,
        out_specs=(VMEM, VMEM),
        scratch_shapes=[pltpu.VMEM((owners, gs), F32), pltpu.VMEM((slots, (owners + 1) * (bs + 8), bs), F32)],
        compiler_params=params,
        name="operator",
    )(to_all(part, [ring]), draws, mask, chol)

    propagated = pl.pallas_call(
        update_kernel,
        out_shape=jax.ShapeDtypeStruct(theta_blocks.shape, BF16),
        in_specs=[SMEM, VMEM, VMEM],
        out_specs=VMEM,
        compiler_params=params,
        name="update",
    )(where, theta_blocks, to_all(operators, [ring]))
    return propagated.reshape(theta.shape), own_bias


def per_device(theta, trial, chol, fields, tile_info, tile_count, block_size):
    short = lax.axis_size("blk") in (8, 16)
    one_slab = fields.shape[1] == chol.shape[1]
    plan = short_axis if short and one_slab and theta.shape[0] == 1 else long_axis
    return plan(theta, trial, chol, fields, tile_info, tile_count, block_size)


def solution(mesh):
    placed = (
        P(("grp", "blk"), None, None),
        P("grp", None),
        P(("grp", "blk"), None, None),
        P(("grp", "blk"), None),
        P("grp", None),
        P("grp"),
        P("grp"),
    )
    return jax.shard_map(
        per_device,
        mesh=mesh,
        in_specs=placed,
        out_specs=(P(("grp", "blk"), None, None), P(("grp", "blk"), None)),
        check_vma=False,
    )
```

```python
import functools

import jax
import jax.numpy as jnp
from jax import lax
from jax.experimental import pallas as pl
from jax.experimental.pallas import tpu as pltpu
from jax.sharding import PartitionSpec as P

STEP_ROOT = 0.25
PIECES = 8
F32 = jnp.float32
BF16 = jnp.bfloat16
LIMIT = 24 * 1024 * 1024
VMEM = pl.BlockSpec(memory_space=pltpu.VMEM)
SMEM = pl.BlockSpec(memory_space=pltpu.SMEM)
HBM = pl.BlockSpec(memory_space=pltpu.HBM)
ANY = pl.BlockSpec(memory_space=pl.ANY)
NT = (((1,), (1,)), ((), ()))


def each(count, body):
    if count <= 16:
        for index in range(count):
            body(index)
    else:

        def step(index, carry):
            body(index)
            return carry

        lax.fori_loop(0, count, step, 0, unroll=8)


def pick_kernel(
    info_hbm, count_hbm, size_hbm, fields_hbm, theta_ref, trial_ref, chol_ref,
    out_ref, rows_ref, mask_ref, draws_ref, where_ref, info_ref, count_ref, size_ref, fields_ref, sems,
):
    owners, walk, slots, bs, _ = out_ref.shape
    blocks = theta_ref.shape[1]
    small = [
        pltpu.make_async_copy(source, target, sems.at[2 + n])
        for n, (source, target) in enumerate(
            [(info_hbm, info_ref), (count_hbm, count_ref), (size_hbm, size_ref), (fields_hbm, fields_ref)]
        )
    ]
    for copy in small:
        copy.start()
    small[0].wait()
    copies = []
    for o in range(owners):
        for j in range(slots):
            block = info_ref[1, o * slots + j]
            for w in range(walk):
                copies.append(pltpu.make_async_copy(theta_ref.at[w, block], out_ref.at[o, w, j], sems.at[0]))
    me = lax.axis_index("blk")
    for j in range(slots):
        block = info_ref[0, me * slots + j]
        copies.append(
            pltpu.make_async_copy(
                trial_ref.at[pl.ds(pl.multiple_of(block * bs, bs), bs), :], rows_ref.at[j], sems.at[1]
            )
        )
    for copy in copies:
        copy.start()
    for copy in small[1:]:
        copy.wait()
    live = count_ref[me]
    for j in range(slots):
        row_size = jnp.where(j < live, size_ref[info_ref[0, me * slots + j]], 0)
        col_size = size_ref[info_ref[1, me * slots + j]]
        rows = lax.broadcasted_iota(jnp.int32, (bs, bs), 0) < row_size
        cols = lax.broadcasted_iota(jnp.int32, (bs, bs), 1) < col_size
        mask_ref[j] = jnp.where(rows & cols, 1.0, 0.0)
    draws_ref[...] = jnp.broadcast_to(fields_ref[0:1, :], draws_ref.shape)
    for o in range(owners):
        for j in range(slots):

            @pl.when(j < count_ref[o])
            def _(s=o * slots + j):
                row_block = info_ref[0, s]
                side = info_ref[1, s] - row_block + 1
                where_ref[(info_ref[2, s] * blocks + row_block) * 3 + side] = jnp.int32(s)

    pltpu.make_async_copy(out_ref, out_ref, sems.at[0]).wait()
    pltpu.make_async_copy(rows_ref, rows_ref, sems.at[1]).wait()


def bias_kernel(
    spread, recv_ref, rows_ref, mask_ref, draws_ref, chol_ref, out_ref, green_ref, bias_ref
):
    owners, walk, slots, bs, _ = recv_ref.shape
    walkers = owners * walk
    for slot in range(slots):

        def one(w, slot=slot):
            block = recv_ref[w // walk, w % walk, slot]
            green = lax.dot_general(rows_ref[slot], block, NT, preferred_element_type=F32)
            green_ref[slot, pl.ds(w, bs, stride=walkers), :] = green * mask_ref[slot]

        each(walkers, one)
    per = bs // PIECES
    for slot in range(slots):
        bias = jnp.zeros((walkers, chol_ref.shape[1]), F32)
        for c in range(PIECES):
            base = c * per * walkers
            left = jnp.concatenate(
                [green_ref[slot, pl.ds(base + p * walkers, walkers), :].astype(BF16) for p in range(per)],
                axis=1,
            )
            right = chol_ref[slot, :, pl.ds(c * per * bs, per * bs)]
            bias += lax.dot_general(left, right, NT, preferred_element_type=F32)
        bias_ref[slot] = bias

    if spread:
        total = sum(bias_ref[slot] for slot in range(slots))
        for o in range(owners):
            out_ref[o, :walkers, :] = total
            out_ref[o, pl.ds(walkers, 8), :] = draws_ref[...]
    else:
        out_ref[...] = bias_ref[...]


def operator_kernel(spread, *refs):
    if spread:
        bias_ref, mask_ref, chol_ref, out_ref, own_ref, shifted_ref, oper_ref = refs
    else:
        info_ref, bias_ref, fields_ref, mask_ref, chol_ref, out_ref, own_ref, shifted_ref, oper_ref = refs
    owners, walk, slots, bs, _ = out_ref.shape
    walkers = owners * walk
    gs = chol_ref.shape[1]
    me = lax.axis_index("blk")
    if spread:
        rows = walkers + 8
        bias = sum(bias_ref[pl.ds(o * rows, walkers), :] for o in range(owners))
        fields = bias_ref[pl.ds(walkers, owners, stride=rows), :]
        shifted_ref[...] = bias
        own_ref[...] = shifted_ref[pl.ds(me, 1), :]
    else:
        bias = bias_ref[...]
        fields = fields_ref[...]
        own_ref[...] = bias_ref[pl.ds(me * walk, walk), :]
    shifted_ref[...] = fields - bias
    for slot in range(slots):
        slab = 0 if spread else pl.multiple_of(info_ref[2, me * slots + slot] * gs, gs)
        left = shifted_ref[:, pl.ds(slab, gs)].astype(BF16)
        per = bs // PIECES
        for c in range(PIECES):
            right = chol_ref[slot, :, pl.ds(c * per * bs, per * bs)]
            oper = jnp.dot(left, right, preferred_element_type=F32) * STEP_ROOT
            for p in range(per):
                oper_ref[pl.ds(c * per + p, walkers, stride=bs), :] = oper[:, p * bs : (p + 1) * bs]

        def one(w, slot=slot):
            block = oper_ref[pl.ds(w * bs, bs), :]
            out_ref[w // walk, w % walk, slot] = (block * mask_ref[slot]).astype(BF16)

        each(walkers, one)


def update_kernel(where_ref, theta_ref, oper_ref, out_ref):
    owners, walk, slots, bs, _ = oper_ref.shape
    blocks = theta_ref.shape[1]
    slabs = where_ref.shape[0] // (3 * blocks)
    for w in range(walk):
        for row_block in range(blocks):
            total = theta_ref[w, row_block].astype(F32)
            for col_block in range(max(row_block - 1, 0), min(row_block + 2, blocks)):
                for slab in range(slabs):
                    s = where_ref[(slab * blocks + row_block) * 3 + col_block - row_block + 1]
                    total += jnp.dot(
                        oper_ref[s // slots, w, s % slots], theta_ref[w, col_block],
                        preferred_element_type=F32,
                    )
            out_ref[w, row_block] = total.astype(BF16)


def long_axis(theta, trial, chol, fields, tile_info, tile_count, block_size):
    owners = lax.axis_size("blk")
    walk, norb, nocc = theta.shape
    walkers = walk * owners
    slots, gs, _ = chol.shape
    nchol = fields.shape[1]
    blocks = block_size.shape[0]
    bs = norb // blocks
    slabs = nchol // gs
    spread = slabs == 1 and walk == 1
    params = pltpu.CompilerParams(vmem_limit_bytes=LIMIT)
    theta_blocks = theta.reshape(walk, blocks, bs, nocc)

    outgoing, rows, mask, draws, where = pl.pallas_call(
        pick_kernel,
        out_shape=(
            jax.ShapeDtypeStruct((owners, walk, slots, bs, nocc), BF16),
            jax.ShapeDtypeStruct((slots, bs, nocc), BF16),
            jax.ShapeDtypeStruct((slots, bs, bs), F32),
            jax.ShapeDtypeStruct((8, nchol), F32),
            jax.ShapeDtypeStruct((slabs * blocks * 3,), jnp.int32),
        ),
        in_specs=[HBM] * 7,
        out_specs=(VMEM, VMEM, VMEM, VMEM, SMEM),
        scratch_shapes=[
            pltpu.SMEM(tile_info.shape, jnp.int32),
            pltpu.SMEM(tile_count.shape, jnp.int32),
            pltpu.SMEM(block_size.shape, jnp.int32),
            pltpu.VMEM(fields.shape, F32),
            pltpu.SemaphoreType.DMA((6,)),
        ],
        compiler_params=params,
        cost_estimate=pl.CostEstimate(flops=0, bytes_accessed=4 * chol.size * 2, transcendentals=0),
        name="pick",
    )(*(pltpu.with_memory_space_constraint(x, pltpu.HBM)
        for x in (tile_info, tile_count, block_size, fields, theta_blocks, trial, chol)))
    received = lax.all_to_all(outgoing, "blk", split_axis=0, concat_axis=0, tiled=True)

    part_shape = (owners, walkers + 8, gs) if spread else (slots, walkers, gs)
    part = pl.pallas_call(
        functools.partial(bias_kernel, spread),
        out_shape=jax.ShapeDtypeStruct(part_shape, F32),
        in_specs=[VMEM] * 5,
        out_specs=VMEM,
        scratch_shapes=[
            pltpu.VMEM((slots, bs * walkers, bs), F32),
            pltpu.VMEM((slots, walkers, gs), F32),
        ],
        compiler_params=params,
        name="bias",
    )(received, rows, mask, draws, chol)

    if spread:
        bias_in = lax.all_to_all(part, "blk", split_axis=0, concat_axis=0, tiled=True)
        inputs = (bias_in.reshape(owners * (walkers + 8), gs),)
    else:
        me = lax.axis_index("blk")
        local = jnp.zeros((walkers, nchol), F32)
        for slot in range(slots):
            start = (0, tile_info[2, me * slots + slot] * gs)
            old = lax.dynamic_slice(local, start, (walkers, gs))
            local = lax.dynamic_update_slice(local, old + part[slot], start)
        inputs = (tile_info, lax.psum(local, "blk"), lax.all_gather(fields, "blk", axis=0, tiled=True))

    operators, own_bias = pl.pallas_call(
        functools.partial(operator_kernel, spread),
        out_shape=(
            jax.ShapeDtypeStruct((owners, walk, slots, bs, bs), BF16),
            jax.ShapeDtypeStruct((walk, nchol), F32),
        ),
        in_specs=([VMEM] if spread else [SMEM, VMEM, VMEM]) + [VMEM, VMEM],
        out_specs=(VMEM, VMEM),
        scratch_shapes=[
            pltpu.VMEM((walkers, nchol), F32),
            pltpu.VMEM((walkers * bs, bs), F32),
        ],
        compiler_params=params,
        name="operator",
    )(*inputs, mask, chol)
    arrived = lax.all_to_all(operators, "blk", split_axis=0, concat_axis=0, tiled=True)

    propagated = pl.pallas_call(
        update_kernel,
        out_shape=jax.ShapeDtypeStruct(theta_blocks.shape, BF16),
        in_specs=[SMEM, VMEM, VMEM],
        out_specs=VMEM,
        compiler_params=params,
        name="update",
    )(where, theta_blocks, arrived)
    return propagated.reshape(theta.shape), own_bias


def pick_pair_kernel(info_hbm, theta_hbm, other_ref, _, *refs):
    pair_refs = refs[:-3]
    info_ref, theta_ref, sems = refs[-3:]
    slots = pair_refs[0].shape[1]
    copies = [
        pltpu.make_async_copy(info_hbm, info_ref, sems.at[0]),
        pltpu.make_async_copy(theta_hbm, theta_ref, sems.at[1]),
    ]
    for copy in copies:
        copy.start()
    me = lax.axis_index("blk")
    core = me % 2
    for copy in copies:
        copy.wait()
    for r, ref in enumerate(pair_refs):
        for j in range(slots):
            block = info_ref[1, (me ^ (2 * r)) * slots + j]
            ref[core, j] = theta_ref[0, block]
            ref[1 - core, j] = other_ref[0, block]


def prepare_kernel(
    place, near_ring, info_hbm, count_hbm, size_hbm, fields_hbm, trial_ref, _,
    rows_ref, mask_ref, draws_ref, where_ref, cols_ref, info_ref, count_ref, size_ref, fields_ref, sems,
):
    slots, bs, _ = rows_ref.shape
    owners = count_ref.shape[0]
    small = [
        pltpu.make_async_copy(source, target, sems.at[n])
        for n, (source, target) in enumerate(
            [(info_hbm, info_ref), (count_hbm, count_ref), (size_hbm, size_ref), (fields_hbm, fields_ref)]
        )
    ]
    for copy in small:
        copy.start()
    me = lax.axis_index("blk")
    for copy in small:
        copy.wait()
    trial = []
    for j in range(slots):
        block = info_ref[0, me * slots + j]
        trial.append(
            pltpu.make_async_copy(
                trial_ref.at[pl.ds(pl.multiple_of(block * bs, bs), bs), :], rows_ref.at[j], sems.at[4 + j]
            )
        )
        trial[-1].start()
    first = me // len(near_ring) * len(near_ring)
    for n, k in enumerate(near_ring):
        for j in range(slots):
            cols_ref[n * slots + j] = info_ref[1, (first + k) * slots + j]
    live = count_ref[me]
    for j in range(slots):
        row_size = jnp.where(j < live, size_ref[info_ref[0, me * slots + j]], 0)
        col_size = size_ref[info_ref[1, me * slots + j]]
        rows = lax.broadcasted_iota(jnp.int32, (bs, bs), 0) < row_size
        cols = lax.broadcasted_iota(jnp.int32, (bs, bs), 1) < col_size
        mask_ref[j] = jnp.where(rows & cols, 1.0, 0.0)
    draws_ref[...] = jnp.broadcast_to(fields_ref[0:1, :], draws_ref.shape)
    for o in range(owners):
        for j in range(slots):

            @pl.when(j < count_ref[o])
            def _(s=o * slots + j, n=place[o] * slots + j):
                row_block = info_ref[0, s]
                where_ref[row_block * 3 + info_ref[1, s] - row_block + 1] = jnp.int32(n)

    for copy in trial:
        copy.wait()


def spread_far_kernel(cols_ref, theta_ref, _, out_ref):
    slots = out_ref.shape[1]
    for k in range(out_ref.shape[0]):
        for j in range(slots):
            out_ref[k, j] = theta_ref[0, cols_ref[k * slots + j]]


def bias_pair_kernel(step, ring, near_ring, rows_ref, mask_ref, draws_ref, chol_ref, far_ref, *refs):
    pair_refs = refs[:-3]
    out_ref, green_ref, total_ref = refs[-3:]
    half, slots, bs, nocc = far_ref.shape
    walkers = 2 * half
    me = lax.axis_index("blk")
    first = me // half * half
    pitch = walkers + 1
    for slot in range(slots):
        mask = mask_ref[slot]
        for blocks, start in [(ref[:, slot], 2 * r) for r, ref in enumerate(pair_refs)] + [(far_ref[:, slot], half)]:
            count = blocks.shape[0]
            green = lax.dot_general(
                rows_ref[slot], blocks.reshape(count * bs, nocc), NT, preferred_element_type=F32
            )
            for n in range(count):
                green_ref[slot, pl.ds(start + n, bs, stride=pitch), :] = green[:, n * bs : (n + 1) * bs] * mask
    per = bs // PIECES
    tall = jnp.zeros((chol_ref.shape[1], walkers), F32)
    wide = jnp.zeros((walkers, chol_ref.shape[1]), F32)
    for c in range(PIECES):
        for slot in range(slots):
            green = jnp.concatenate(
                [green_ref[slot, pl.ds((c * per + p) * pitch, walkers), :].astype(BF16) for p in range(per)],
                axis=1,
            )
            tile = chol_ref[slot, :, pl.ds(c * per * bs, per * bs)]
            if slot % 2:
                wide += lax.dot_general(green, tile, NT, preferred_element_type=F32)
            else:
                tall += lax.dot_general(tile, green, NT, preferred_element_type=F32)
    total = -(tall.T + wide)
    for n in range(walkers):
        walker = (me // 2 ^ (n // 2)) * 2 + n % 2 if n < half else (first + near_ring[n - half]) ^ step
        total_ref[pl.ds(walker, 1), :] = total[n : n + 1, :]
    total = total_ref[...]
    own = total_ref[pl.ds(me, 1), :]
    for n, o in enumerate(ring):
        out_ref[n] = total
        out_ref[n, pl.ds(me, 1), :] = jnp.where(o == me, own, own + draws_ref[0:1, :])


def operator_pair_kernel(place, shift_ref, fields_ref, mask_ref, chol_ref, out_ref, own_ref, total_ref, oper_ref):
    walkers, _, slots, bs, _ = out_ref.shape
    me = lax.axis_index("blk")
    total_ref[...] = sum(shift_ref[o] for o in range(walkers))
    own = total_ref[pl.ds(me, 1), :]
    own_ref[...] = -own
    total_ref[pl.ds(me, 1), :] = own + fields_ref[0:1, :]
    left = total_ref[...].astype(BF16)
    per = bs // PIECES
    pitch = bs + 8
    for slot in range(slots):
        for c in range(PIECES):
            right = chol_ref[slot, :, pl.ds(c * per * bs, per * bs)]
            oper = jnp.dot(left, right, preferred_element_type=F32) * STEP_ROOT
            for p in range(per):
                oper_ref[slot, pl.ds(c * per + p, walkers, stride=pitch), :] = oper[:, p * bs : (p + 1) * bs]
        for w in range(walkers):
            block = oper_ref[slot, pl.ds(w * pitch, bs), :]
            out_ref[place[w], 0, slot] = (block * mask_ref[slot]).astype(BF16)


def short_axis(theta, trial, chol, fields, tile_info, tile_count, block_size):
    owners = lax.axis_size("blk")
    _, norb, nocc = theta.shape
    slots, gs, _ = chol.shape
    blocks = block_size.shape[0]
    bs = norb // blocks
    half = owners // 2
    step = half + half // 2
    near = half // 2
    chips = [*range(1, half, 2), *range(0, half, 2)[::-1]]
    ring = [2 * chip + core for chip in chips for core in (1, 0)]
    place = [ring.index(o) for o in range(owners)]
    near_ring = [2 * chip + core for chip in range(near) for core in (1, 0)]
    params = pltpu.CompilerParams(vmem_limit_bytes=LIMIT)
    theta_blocks = theta.reshape(1, blocks, bs, nocc)

    def swap(x, step):
        return lax.ppermute(x, "blk", [(i, i ^ step) for i in range(owners)])

    def to_all(x, groups=None):
        return lax.all_to_all(x, "blk", split_axis=0, concat_axis=0, tiled=True, axis_index_groups=groups)

    def spread(pairs):
        return [pairs[0]] + [swap(pairs[r], 2 * r) for r in range(1, near)]

    hbm = functools.partial(pltpu.with_memory_space_constraint, memory_space=pltpu.HBM)
    pair_shapes = (jax.ShapeDtypeStruct((2, slots, bs, nocc), BF16),) * near
    partner = swap(theta_blocks, step)
    load = pl.CostEstimate(flops=0, bytes_accessed=8 * chol.size, transcendentals=0)
    pick = pl.pallas_call(
        pick_pair_kernel,
        out_shape=pair_shapes,
        in_specs=[HBM, HBM, VMEM, HBM],
        out_specs=(VMEM,) * near,
        scratch_shapes=[
            pltpu.SMEM(tile_info.shape, jnp.int32),
            pltpu.VMEM(theta_blocks.shape, BF16),
            pltpu.SemaphoreType.DMA((2,)),
        ],
        compiler_params=params,
        cost_estimate=load,
        name="pick",
    )
    pairs = lax.cond(
        lax.axis_index("blk") < owners,
        lambda x: pick(hbm(tile_info), hbm(x), swap(x, 1), hbm(chol)),
        lambda x: pick(hbm(tile_info), hbm(x), swap(swap(swap(x, 1), 1), 1), hbm(chol)),
        theta_blocks,
    )
    rows, mask, draws, where, cols = pl.pallas_call(
        functools.partial(prepare_kernel, place, near_ring),
        out_shape=(
            jax.ShapeDtypeStruct((slots, bs, nocc), BF16),
            jax.ShapeDtypeStruct((slots, bs, bs), F32),
            jax.ShapeDtypeStruct((8, gs), F32),
            jax.ShapeDtypeStruct((3 * blocks,), jnp.int32),
            jax.ShapeDtypeStruct((half * slots,), jnp.int32),
        ),
        in_specs=[HBM] * 6,
        out_specs=(VMEM, VMEM, VMEM, SMEM, SMEM),
        scratch_shapes=[
            pltpu.SMEM(tile_info.shape, jnp.int32),
            pltpu.SMEM(tile_count.shape, jnp.int32),
            pltpu.SMEM(block_size.shape, jnp.int32),
            pltpu.VMEM(fields.shape, F32),
            pltpu.SemaphoreType.DMA((4 + slots,)),
        ],
        compiler_params=params,
        cost_estimate=load,
        name="prepare",
    )(*map(hbm, (tile_info, tile_count, block_size, fields, trial, chol)))
    received = spread(pairs)
    far = pl.pallas_call(
        spread_far_kernel,
        out_shape=jax.ShapeDtypeStruct((half, slots, bs, nocc), BF16),
        in_specs=[SMEM, VMEM, HBM],
        out_specs=VMEM,
        compiler_params=params,
        cost_estimate=load,
        name="spread",
    )(cols, partner, hbm(chol))
    groups = [near_ring, [half + k for k in near_ring]]
    far, *received = lax.optimization_barrier((far, *received))
    far = to_all(far, groups)

    part = pl.pallas_call(
        functools.partial(bias_pair_kernel, step, ring, near_ring),
        out_shape=jax.ShapeDtypeStruct((owners, owners, gs), F32),
        in_specs=[VMEM] * (5 + near),
        out_specs=VMEM,
        scratch_shapes=[pltpu.VMEM((slots, (bs + 1) * (owners + 1), bs), F32), pltpu.VMEM((owners, gs), F32)],
        compiler_params=params,
        name="bias",
    )(rows, mask, draws, chol, far, *received)

    operators, own_bias = pl.pallas_call(
        functools.partial(operator_pair_kernel, place),
        out_shape=(
            jax.ShapeDtypeStruct((owners, 1, slots, bs, bs), BF16),
            jax.ShapeDtypeStruct((1, gs), F32),
        ),
        in_specs=[VMEM] * 4,
        out_specs=(VMEM, VMEM),
        scratch_shapes=[pltpu.VMEM((owners, gs), F32), pltpu.VMEM((slots, (owners + 1) * (bs + 8), bs), F32)],
        compiler_params=params,
        name="operator",
    )(to_all(part, [ring]), draws, mask, chol)

    propagated = pl.pallas_call(
        update_kernel,
        out_shape=jax.ShapeDtypeStruct(theta_blocks.shape, BF16),
        in_specs=[SMEM, VMEM, VMEM],
        out_specs=VMEM,
        compiler_params=params,
        name="update",
    )(where, theta_blocks, to_all(operators, [ring]))
    return propagated.reshape(theta.shape), own_bias


def per_device(theta, trial, chol, fields, tile_info, tile_count, block_size):
    short = lax.axis_size("blk") in (8, 16)
    one_slab = fields.shape[1] == chol.shape[1]
    plan = short_axis if short and one_slab and theta.shape[0] == 1 else long_axis
    return plan(theta, trial, chol, fields, tile_info, tile_count, block_size)


def solution(mesh):
    placed = (
        P(("grp", "blk"), None, None),
        P("grp", None),
        P(("grp", "blk"), None, None),
        P(("grp", "blk"), None),
        P("grp", None),
        P("grp"),
        P("grp"),
    )
    return jax.shard_map(
        per_device,
        mesh=mesh,
        in_specs=placed,
        out_specs=(P(("grp", "blk"), None, None), P(("grp", "blk"), None)),
        check_vma=False,
    )
```

```python
import functools

import jax
import jax.numpy as jnp
from jax import lax
from jax.experimental import pallas as pl
from jax.experimental.pallas import tpu as pltpu
from jax.sharding import PartitionSpec as P

STEP_ROOT = 0.25
PIECES = 8
F32 = jnp.float32
BF16 = jnp.bfloat16
LIMIT = 24 * 1024 * 1024
VMEM = pl.BlockSpec(memory_space=pltpu.VMEM)
SMEM = pl.BlockSpec(memory_space=pltpu.SMEM)
HBM = pl.BlockSpec(memory_space=pltpu.HBM)
ANY = pl.BlockSpec(memory_space=pl.ANY)
NT = (((1,), (1,)), ((), ()))


def each(count, body):
    if count <= 16:
        for index in range(count):
            body(index)
    else:

        def step(index, carry):
            body(index)
            return carry

        lax.fori_loop(0, count, step, 0, unroll=8)


def pick_kernel(
    info_hbm, count_hbm, size_hbm, fields_hbm, theta_ref, trial_ref, chol_ref,
    out_ref, rows_ref, mask_ref, draws_ref, where_ref, info_ref, count_ref, size_ref, fields_ref, sems,
):
    owners, walk, slots, bs, _ = out_ref.shape
    blocks = theta_ref.shape[1]
    small = [
        pltpu.make_async_copy(source, target, sems.at[2 + n])
        for n, (source, target) in enumerate(
            [(info_hbm, info_ref), (count_hbm, count_ref), (size_hbm, size_ref), (fields_hbm, fields_ref)]
        )
    ]
    for copy in small:
        copy.start()
    small[0].wait()
    copies = []
    for o in range(owners):
        for j in range(slots):
            block = info_ref[1, o * slots + j]
            for w in range(walk):
                copies.append(pltpu.make_async_copy(theta_ref.at[w, block], out_ref.at[o, w, j], sems.at[0]))
    me = lax.axis_index("blk")
    for j in range(slots):
        block = info_ref[0, me * slots + j]
        copies.append(
            pltpu.make_async_copy(
                trial_ref.at[pl.ds(pl.multiple_of(block * bs, bs), bs), :], rows_ref.at[j], sems.at[1]
            )
        )
    for copy in copies:
        copy.start()
    for copy in small[1:]:
        copy.wait()
    live = count_ref[me]
    for j in range(slots):
        row_size = jnp.where(j < live, size_ref[info_ref[0, me * slots + j]], 0)
        col_size = size_ref[info_ref[1, me * slots + j]]
        rows = lax.broadcasted_iota(jnp.int32, (bs, bs), 0) < row_size
        cols = lax.broadcasted_iota(jnp.int32, (bs, bs), 1) < col_size
        mask_ref[j] = jnp.where(rows & cols, 1.0, 0.0)
    draws_ref[...] = jnp.broadcast_to(fields_ref[0:1, :], draws_ref.shape)
    for o in range(owners):
        for j in range(slots):

            @pl.when(j < count_ref[o])
            def _(s=o * slots + j):
                row_block = info_ref[0, s]
                side = info_ref[1, s] - row_block + 1
                where_ref[(info_ref[2, s] * blocks + row_block) * 3 + side] = jnp.int32(s)

    pltpu.make_async_copy(out_ref, out_ref, sems.at[0]).wait()
    pltpu.make_async_copy(rows_ref, rows_ref, sems.at[1]).wait()


def bias_kernel(
    spread, recv_ref, rows_ref, mask_ref, draws_ref, chol_ref, out_ref, green_ref, bias_ref
):
    owners, walk, slots, bs, _ = recv_ref.shape
    walkers = owners * walk
    for slot in range(slots):

        def one(w, slot=slot):
            block = recv_ref[w // walk, w % walk, slot]
            green = lax.dot_general(rows_ref[slot], block, NT, preferred_element_type=F32)
            green_ref[slot, pl.ds(w, bs, stride=walkers), :] = green * mask_ref[slot]

        each(walkers, one)
    per = bs // PIECES
    for slot in range(slots):
        bias = jnp.zeros((walkers, chol_ref.shape[1]), F32)
        for c in range(PIECES):
            base = c * per * walkers
            left = jnp.concatenate(
                [green_ref[slot, pl.ds(base + p * walkers, walkers), :].astype(BF16) for p in range(per)],
                axis=1,
            )
            right = chol_ref[slot, :, pl.ds(c * per * bs, per * bs)]
            bias += lax.dot_general(left, right, NT, preferred_element_type=F32)
        bias_ref[slot] = bias

    if spread:
        total = sum(bias_ref[slot] for slot in range(slots))
        for o in range(owners):
            out_ref[o, :walkers, :] = total
            out_ref[o, pl.ds(walkers, 8), :] = draws_ref[...]
    else:
        out_ref[...] = bias_ref[...]


def operator_kernel(spread, *refs):
    if spread:
        bias_ref, mask_ref, chol_ref, out_ref, own_ref, shifted_ref, oper_ref = refs
    else:
        info_ref, bias_ref, fields_ref, mask_ref, chol_ref, out_ref, own_ref, shifted_ref, oper_ref = refs
    owners, walk, slots, bs, _ = out_ref.shape
    walkers = owners * walk
    gs = chol_ref.shape[1]
    me = lax.axis_index("blk")
    if spread:
        rows = walkers + 8
        bias = sum(bias_ref[pl.ds(o * rows, walkers), :] for o in range(owners))
        fields = bias_ref[pl.ds(walkers, owners, stride=rows), :]
        shifted_ref[...] = bias
        own_ref[...] = shifted_ref[pl.ds(me, 1), :]
    else:
        bias = bias_ref[...]
        fields = fields_ref[...]
        own_ref[...] = bias_ref[pl.ds(me * walk, walk), :]
    shifted_ref[...] = fields - bias
    for slot in range(slots):
        slab = 0 if spread else pl.multiple_of(info_ref[2, me * slots + slot] * gs, gs)
        left = shifted_ref[:, pl.ds(slab, gs)].astype(BF16)
        per = bs // PIECES
        for c in range(PIECES):
            right = chol_ref[slot, :, pl.ds(c * per * bs, per * bs)]
            oper = jnp.dot(left, right, preferred_element_type=F32) * STEP_ROOT
            for p in range(per):
                oper_ref[pl.ds(c * per + p, walkers, stride=bs), :] = oper[:, p * bs : (p + 1) * bs]

        def one(w, slot=slot):
            block = oper_ref[pl.ds(w * bs, bs), :]
            out_ref[w // walk, w % walk, slot] = (block * mask_ref[slot]).astype(BF16)

        each(walkers, one)


def update_kernel(where_ref, theta_ref, oper_ref, out_ref):
    owners, walk, slots, bs, _ = oper_ref.shape
    blocks = theta_ref.shape[1]
    slabs = where_ref.shape[0] // (3 * blocks)
    for w in range(walk):
        for row_block in range(blocks):
            total = theta_ref[w, row_block].astype(F32)
            for col_block in range(max(row_block - 1, 0), min(row_block + 2, blocks)):
                for slab in range(slabs):
                    s = where_ref[(slab * blocks + row_block) * 3 + col_block - row_block + 1]
                    total += jnp.dot(
                        oper_ref[s // slots, w, s % slots], theta_ref[w, col_block],
                        preferred_element_type=F32,
                    )
            out_ref[w, row_block] = total.astype(BF16)


def long_axis(theta, trial, chol, fields, tile_info, tile_count, block_size):
    owners = lax.axis_size("blk")
    walk, norb, nocc = theta.shape
    walkers = walk * owners
    slots, gs, _ = chol.shape
    nchol = fields.shape[1]
    blocks = block_size.shape[0]
    bs = norb // blocks
    slabs = nchol // gs
    spread = slabs == 1 and walk == 1
    params = pltpu.CompilerParams(vmem_limit_bytes=LIMIT)
    theta_blocks = theta.reshape(walk, blocks, bs, nocc)

    outgoing, rows, mask, draws, where = pl.pallas_call(
        pick_kernel,
        out_shape=(
            jax.ShapeDtypeStruct((owners, walk, slots, bs, nocc), BF16),
            jax.ShapeDtypeStruct((slots, bs, nocc), BF16),
            jax.ShapeDtypeStruct((slots, bs, bs), F32),
            jax.ShapeDtypeStruct((8, nchol), F32),
            jax.ShapeDtypeStruct((slabs * blocks * 3,), jnp.int32),
        ),
        in_specs=[HBM] * 7,
        out_specs=(VMEM, VMEM, VMEM, VMEM, SMEM),
        scratch_shapes=[
            pltpu.SMEM(tile_info.shape, jnp.int32),
            pltpu.SMEM(tile_count.shape, jnp.int32),
            pltpu.SMEM(block_size.shape, jnp.int32),
            pltpu.VMEM(fields.shape, F32),
            pltpu.SemaphoreType.DMA((6,)),
        ],
        compiler_params=params,
        cost_estimate=pl.CostEstimate(flops=0, bytes_accessed=4 * chol.size * 2, transcendentals=0),
        name="pick",
    )(*(pltpu.with_memory_space_constraint(x, pltpu.HBM)
        for x in (tile_info, tile_count, block_size, fields, theta_blocks, trial, chol)))
    received = lax.all_to_all(outgoing, "blk", split_axis=0, concat_axis=0, tiled=True)

    part_shape = (owners, walkers + 8, gs) if spread else (slots, walkers, gs)
    part = pl.pallas_call(
        functools.partial(bias_kernel, spread),
        out_shape=jax.ShapeDtypeStruct(part_shape, F32),
        in_specs=[VMEM] * 5,
        out_specs=VMEM,
        scratch_shapes=[
            pltpu.VMEM((slots, bs * walkers, bs), F32),
            pltpu.VMEM((slots, walkers, gs), F32),
        ],
        compiler_params=params,
        name="bias",
    )(received, rows, mask, draws, chol)

    if spread:
        bias_in = lax.all_to_all(part, "blk", split_axis=0, concat_axis=0, tiled=True)
        inputs = (bias_in.reshape(owners * (walkers + 8), gs),)
    else:
        me = lax.axis_index("blk")
        local = jnp.zeros((walkers, nchol), F32)
        for slot in range(slots):
            start = (0, tile_info[2, me * slots + slot] * gs)
            old = lax.dynamic_slice(local, start, (walkers, gs))
            local = lax.dynamic_update_slice(local, old + part[slot], start)
        inputs = (tile_info, lax.psum(local, "blk"), lax.all_gather(fields, "blk", axis=0, tiled=True))

    operators, own_bias = pl.pallas_call(
        functools.partial(operator_kernel, spread),
        out_shape=(
            jax.ShapeDtypeStruct((owners, walk, slots, bs, bs), BF16),
            jax.ShapeDtypeStruct((walk, nchol), F32),
        ),
        in_specs=([VMEM] if spread else [SMEM, VMEM, VMEM]) + [VMEM, VMEM],
        out_specs=(VMEM, VMEM),
        scratch_shapes=[
            pltpu.VMEM((walkers, nchol), F32),
            pltpu.VMEM((walkers * bs, bs), F32),
        ],
        compiler_params=params,
        name="operator",
    )(*inputs, mask, chol)
    arrived = lax.all_to_all(operators, "blk", split_axis=0, concat_axis=0, tiled=True)

    propagated = pl.pallas_call(
        update_kernel,
        out_shape=jax.ShapeDtypeStruct(theta_blocks.shape, BF16),
        in_specs=[SMEM, VMEM, VMEM],
        out_specs=VMEM,
        compiler_params=params,
        name="update",
    )(where, theta_blocks, arrived)
    return propagated.reshape(theta.shape), own_bias


def pick_pair_kernel(info_hbm, theta_hbm, other_ref, _, *refs):
    pair_refs = refs[:-3]
    info_ref, theta_ref, sems = refs[-3:]
    slots = pair_refs[0].shape[1]
    copies = [
        pltpu.make_async_copy(info_hbm, info_ref, sems.at[0]),
        pltpu.make_async_copy(theta_hbm, theta_ref, sems.at[1]),
    ]
    for copy in copies:
        copy.start()
    me = lax.axis_index("blk")
    core = me % 2
    for copy in copies:
        copy.wait()
    for r, ref in enumerate(pair_refs):
        for j in range(slots):
            block = info_ref[1, (me ^ (2 * r)) * slots + j]
            ref[core, j] = theta_ref[0, block]
            ref[1 - core, j] = other_ref[0, block]


def prepare_kernel(
    place, near_ring, info_hbm, count_hbm, size_hbm, fields_hbm, trial_ref, _,
    rows_ref, mask_ref, draws_ref, where_ref, cols_ref, info_ref, count_ref, size_ref, fields_ref, sems,
):
    slots, bs, _ = rows_ref.shape
    owners = count_ref.shape[0]
    small = [
        pltpu.make_async_copy(source, target, sems.at[n])
        for n, (source, target) in enumerate(
            [(info_hbm, info_ref), (count_hbm, count_ref), (size_hbm, size_ref), (fields_hbm, fields_ref)]
        )
    ]
    for copy in small:
        copy.start()
    me = lax.axis_index("blk")
    for copy in small:
        copy.wait()
    trial = []
    for j in range(slots):
        block = info_ref[0, me * slots + j]
        trial.append(
            pltpu.make_async_copy(
                trial_ref.at[pl.ds(pl.multiple_of(block * bs, bs), bs), :], rows_ref.at[j], sems.at[4 + j]
            )
        )
        trial[-1].start()
    first = me // len(near_ring) * len(near_ring)
    for n, k in enumerate(near_ring):
        for j in range(slots):
            cols_ref[n * slots + j] = info_ref[1, (first + k) * slots + j]
    live = count_ref[me]
    for j in range(slots):
        row_size = jnp.where(j < live, size_ref[info_ref[0, me * slots + j]], 0)
        col_size = size_ref[info_ref[1, me * slots + j]]
        rows = lax.broadcasted_iota(jnp.int32, (bs, bs), 0) < row_size
        cols = lax.broadcasted_iota(jnp.int32, (bs, bs), 1) < col_size
        mask_ref[j] = jnp.where(rows & cols, 1.0, 0.0)
    draws_ref[...] = jnp.broadcast_to(fields_ref[0:1, :], draws_ref.shape)
    for o in range(owners):
        for j in range(slots):

            @pl.when(j < count_ref[o])
            def _(s=o * slots + j, n=place[o] * slots + j):
                row_block = info_ref[0, s]
                where_ref[row_block * 3 + info_ref[1, s] - row_block + 1] = jnp.int32(n)

    for copy in trial:
        copy.wait()


def spread_far_kernel(cols_ref, theta_ref, _, out_ref):
    slots = out_ref.shape[1]
    for k in range(out_ref.shape[0]):
        for j in range(slots):
            out_ref[k, j] = theta_ref[0, cols_ref[k * slots + j]]


def bias_pair_kernel(step, ring, near_ring, rows_ref, mask_ref, draws_ref, chol_ref, far_ref, *refs):
    pair_refs = refs[:-3]
    out_ref, green_ref, total_ref = refs[-3:]
    half, slots, bs, nocc = far_ref.shape
    walkers = 2 * half
    me = lax.axis_index("blk")
    first = me // half * half
    pitch = walkers + 1
    for slot in range(slots):
        mask = mask_ref[slot]
        for blocks, start in [(ref[:, slot], 2 * r) for r, ref in enumerate(pair_refs)] + [(far_ref[:, slot], half)]:
            count = blocks.shape[0]
            green = lax.dot_general(
                rows_ref[slot], blocks.reshape(count * bs, nocc), NT, preferred_element_type=F32
            )
            for n in range(count):
                green_ref[slot, pl.ds(start + n, bs, stride=pitch), :] = green[:, n * bs : (n + 1) * bs] * mask
    per = bs // PIECES
    tall = jnp.zeros((chol_ref.shape[1], walkers), F32)
    wide = jnp.zeros((walkers, chol_ref.shape[1]), F32)
    for c in range(PIECES):
        for slot in range(slots):
            green = jnp.concatenate(
                [green_ref[slot, pl.ds((c * per + p) * pitch, walkers), :].astype(BF16) for p in range(per)],
                axis=1,
            )
            tile = chol_ref[slot, :, pl.ds(c * per * bs, per * bs)]
            if slot % 2:
                wide += lax.dot_general(green, tile, NT, preferred_element_type=F32)
            else:
                tall += lax.dot_general(tile, green, NT, preferred_element_type=F32)
    total = -(tall.T + wide)
    for n in range(walkers):
        walker = (me // 2 ^ (n // 2)) * 2 + n % 2 if n < half else (first + near_ring[n - half]) ^ step
        total_ref[pl.ds(walker, 1), :] = total[n : n + 1, :]
    total = total_ref[...]
    own = total_ref[pl.ds(me, 1), :]
    for n, o in enumerate(ring):
        out_ref[n] = total
        out_ref[n, pl.ds(me, 1), :] = jnp.where(o == me, own, own + draws_ref[0:1, :])


def operator_pair_kernel(place, shift_ref, fields_ref, mask_ref, chol_ref, out_ref, own_ref, total_ref, oper_ref):
    walkers, _, slots, bs, _ = out_ref.shape
    me = lax.axis_index("blk")
    total_ref[...] = sum(shift_ref[o] for o in range(walkers))
    own = total_ref[pl.ds(me, 1), :]
    own_ref[...] = jnp.broadcast_to(-own, own_ref.shape)
    total_ref[pl.ds(me, 1), :] = own + fields_ref[0:1, :]
    left = total_ref[...].astype(BF16)
    per = bs // PIECES
    pitch = bs + 8
    for slot in range(slots):
        for c in range(PIECES):
            right = chol_ref[slot, :, pl.ds(c * per * bs, per * bs)]
            oper = jnp.dot(left, right, preferred_element_type=F32) * STEP_ROOT
            for p in range(per):
                oper_ref[slot, pl.ds(c * per + p, walkers, stride=pitch), :] = oper[:, p * bs : (p + 1) * bs]
        for w in range(walkers):
            block = oper_ref[slot, pl.ds(w * pitch, bs), :]
            out_ref[place[w], 0, slot] = (block * mask_ref[slot]).astype(BF16)


def update_pair_kernel(where_ref, theta_ref, oper_ref, bias_ref, out_ref, own_ref):
    own_ref[...] = bias_ref[0:1, :]
    update_kernel(where_ref, theta_ref, oper_ref, out_ref)


def short_axis(theta, trial, chol, fields, tile_info, tile_count, block_size):
    owners = lax.axis_size("blk")
    _, norb, nocc = theta.shape
    slots, gs, _ = chol.shape
    blocks = block_size.shape[0]
    bs = norb // blocks
    half = owners // 2
    step = half + half // 2
    near = half // 2
    chips = [*range(1, half, 2), *range(0, half, 2)[::-1]]
    ring = [2 * chip + core for chip in chips for core in (1, 0)]
    place = [ring.index(o) for o in range(owners)]
    near_ring = [2 * chip + core for chip in range(near) for core in (1, 0)]
    params = pltpu.CompilerParams(vmem_limit_bytes=LIMIT)
    theta_blocks = theta.reshape(1, blocks, bs, nocc)

    def swap(x, step):
        return lax.ppermute(x, "blk", [(i, i ^ step) for i in range(owners)])

    def to_all(x, groups=None):
        return lax.all_to_all(x, "blk", split_axis=0, concat_axis=0, tiled=True, axis_index_groups=groups)

    def spread(pairs):
        return [pairs[0]] + [swap(pairs[r], 2 * r) for r in range(1, near)]

    hbm = functools.partial(pltpu.with_memory_space_constraint, memory_space=pltpu.HBM)
    pair_shapes = (jax.ShapeDtypeStruct((2, slots, bs, nocc), BF16),) * near
    partner = swap(theta_blocks, step)
    load = pl.CostEstimate(flops=0, bytes_accessed=8 * chol.size, transcendentals=0)
    pick = pl.pallas_call(
        pick_pair_kernel,
        out_shape=pair_shapes,
        in_specs=[HBM, HBM, VMEM, HBM],
        out_specs=(VMEM,) * near,
        scratch_shapes=[
            pltpu.SMEM(tile_info.shape, jnp.int32),
            pltpu.VMEM(theta_blocks.shape, BF16),
            pltpu.SemaphoreType.DMA((2,)),
        ],
        compiler_params=params,
        cost_estimate=load,
        name="pick",
    )
    pairs = lax.cond(
        lax.axis_index("blk") < owners,
        lambda x: pick(hbm(tile_info), hbm(x), swap(x, 1), hbm(chol)),
        lambda x: pick(hbm(tile_info), hbm(x), swap(swap(swap(x, 1), 1), 1), hbm(chol)),
        theta_blocks,
    )
    rows, mask, draws, where, cols = pl.pallas_call(
        functools.partial(prepare_kernel, place, near_ring),
        out_shape=(
            jax.ShapeDtypeStruct((slots, bs, nocc), BF16),
            jax.ShapeDtypeStruct((slots, bs, bs), F32),
            jax.ShapeDtypeStruct((8, gs), F32),
            jax.ShapeDtypeStruct((3 * blocks,), jnp.int32),
            jax.ShapeDtypeStruct((half * slots,), jnp.int32),
        ),
        in_specs=[HBM] * 6,
        out_specs=(VMEM, VMEM, VMEM, SMEM, SMEM),
        scratch_shapes=[
            pltpu.SMEM(tile_info.shape, jnp.int32),
            pltpu.SMEM(tile_count.shape, jnp.int32),
            pltpu.SMEM(block_size.shape, jnp.int32),
            pltpu.VMEM(fields.shape, F32),
            pltpu.SemaphoreType.DMA((4 + slots,)),
        ],
        compiler_params=params,
        cost_estimate=load,
        name="prepare",
    )(*map(hbm, (tile_info, tile_count, block_size, fields, trial, chol)))
    received = spread(pairs)
    far = pl.pallas_call(
        spread_far_kernel,
        out_shape=jax.ShapeDtypeStruct((half, slots, bs, nocc), BF16),
        in_specs=[SMEM, VMEM, HBM],
        out_specs=VMEM,
        compiler_params=params,
        cost_estimate=load,
        name="spread",
    )(cols, partner, hbm(chol))
    groups = [near_ring, [half + k for k in near_ring]]
    far, *received = lax.optimization_barrier((far, *received))
    far = to_all(far, groups)

    part = pl.pallas_call(
        functools.partial(bias_pair_kernel, step, ring, near_ring),
        out_shape=jax.ShapeDtypeStruct((owners, owners, gs), F32),
        in_specs=[VMEM] * (5 + near),
        out_specs=VMEM,
        scratch_shapes=[pltpu.VMEM((slots, (bs + 1) * (owners + 1), bs), F32), pltpu.VMEM((owners, gs), F32)],
        compiler_params=params,
        name="bias",
    )(rows, mask, draws, chol, far, *received)

    operators, own_bias = pl.pallas_call(
        functools.partial(operator_pair_kernel, place),
        out_shape=(
            jax.ShapeDtypeStruct((owners, 1, slots, bs, bs), BF16),
            jax.ShapeDtypeStruct((8, gs), F32),
        ),
        in_specs=[VMEM] * 4,
        out_specs=(VMEM, VMEM),
        scratch_shapes=[pltpu.VMEM((owners, gs), F32), pltpu.VMEM((slots, (owners + 1) * (bs + 8), bs), F32)],
        compiler_params=params,
        name="operator",
    )(to_all(part, [ring]), draws, mask, chol)

    propagated, own_bias = pl.pallas_call(
        update_pair_kernel,
        out_shape=(jax.ShapeDtypeStruct(theta_blocks.shape, BF16), jax.ShapeDtypeStruct((1, gs), F32)),
        in_specs=[SMEM, VMEM, VMEM, VMEM],
        out_specs=(VMEM, VMEM),
        compiler_params=params,
        name="update",
    )(where, theta_blocks, to_all(operators, [ring]), own_bias)
    return propagated.reshape(theta.shape), own_bias


def per_device(theta, trial, chol, fields, tile_info, tile_count, block_size):
    short = lax.axis_size("blk") in (8, 16)
    one_slab = fields.shape[1] == chol.shape[1]
    plan = short_axis if short and one_slab and theta.shape[0] == 1 else long_axis
    return plan(theta, trial, chol, fields, tile_info, tile_count, block_size)


def solution(mesh):
    placed = (
        P(("grp", "blk"), None, None),
        P("grp", None),
        P(("grp", "blk"), None, None),
        P(("grp", "blk"), None),
        P("grp", None),
        P("grp"),
        P("grp"),
    )
    return jax.shard_map(
        per_device,
        mesh=mesh,
        in_specs=placed,
        out_specs=(P(("grp", "blk"), None, None), P(("grp", "blk"), None)),
        check_vma=False,
    )
```

```python
import functools

import jax
import jax.numpy as jnp
from jax import lax
from jax.experimental import pallas as pl
from jax.experimental.pallas import tpu as pltpu
from jax.sharding import PartitionSpec as P

STEP_ROOT = 0.25
PIECES = 8
F32 = jnp.float32
BF16 = jnp.bfloat16
LIMIT = 24 * 1024 * 1024
VMEM = pl.BlockSpec(memory_space=pltpu.VMEM)
SMEM = pl.BlockSpec(memory_space=pltpu.SMEM)
HBM = pl.BlockSpec(memory_space=pltpu.HBM)
ANY = pl.BlockSpec(memory_space=pl.ANY)
NT = (((1,), (1,)), ((), ()))


def each(count, body):
    if count <= 16:
        for index in range(count):
            body(index)
    else:

        def step(index, carry):
            body(index)
            return carry

        lax.fori_loop(0, count, step, 0, unroll=8)


def pick_kernel(
    info_hbm, count_hbm, size_hbm, fields_hbm, theta_ref, trial_ref, chol_ref,
    out_ref, rows_ref, mask_ref, draws_ref, where_ref, info_ref, count_ref, size_ref, fields_ref, sems,
):
    owners, walk, slots, bs, _ = out_ref.shape
    blocks = theta_ref.shape[1]
    small = [
        pltpu.make_async_copy(source, target, sems.at[2 + n])
        for n, (source, target) in enumerate(
            [(info_hbm, info_ref), (count_hbm, count_ref), (size_hbm, size_ref), (fields_hbm, fields_ref)]
        )
    ]
    for copy in small:
        copy.start()
    small[0].wait()
    copies = []
    for o in range(owners):
        for j in range(slots):
            block = info_ref[1, o * slots + j]
            for w in range(walk):
                copies.append(pltpu.make_async_copy(theta_ref.at[w, block], out_ref.at[o, w, j], sems.at[0]))
    me = lax.axis_index("blk")
    for j in range(slots):
        block = info_ref[0, me * slots + j]
        copies.append(
            pltpu.make_async_copy(
                trial_ref.at[pl.ds(pl.multiple_of(block * bs, bs), bs), :], rows_ref.at[j], sems.at[1]
            )
        )
    for copy in copies:
        copy.start()
    for copy in small[1:]:
        copy.wait()
    live = count_ref[me]
    for j in range(slots):
        row_size = jnp.where(j < live, size_ref[info_ref[0, me * slots + j]], 0)
        col_size = size_ref[info_ref[1, me * slots + j]]
        rows = lax.broadcasted_iota(jnp.int32, (bs, bs), 0) < row_size
        cols = lax.broadcasted_iota(jnp.int32, (bs, bs), 1) < col_size
        mask_ref[j] = jnp.where(rows & cols, 1.0, 0.0)
    draws_ref[...] = jnp.broadcast_to(fields_ref[0:1, :], draws_ref.shape)
    for o in range(owners):
        for j in range(slots):

            @pl.when(j < count_ref[o])
            def _(s=o * slots + j):
                row_block = info_ref[0, s]
                side = info_ref[1, s] - row_block + 1
                where_ref[(info_ref[2, s] * blocks + row_block) * 3 + side] = jnp.int32(s)

    pltpu.make_async_copy(out_ref, out_ref, sems.at[0]).wait()
    pltpu.make_async_copy(rows_ref, rows_ref, sems.at[1]).wait()


def bias_kernel(
    spread, recv_ref, rows_ref, mask_ref, draws_ref, chol_ref, out_ref, green_ref, bias_ref
):
    owners, walk, slots, bs, _ = recv_ref.shape
    walkers = owners * walk
    for slot in range(slots):

        def one(w, slot=slot):
            block = recv_ref[w // walk, w % walk, slot]
            green = lax.dot_general(rows_ref[slot], block, NT, preferred_element_type=F32)
            green_ref[slot, pl.ds(w, bs, stride=walkers), :] = green * mask_ref[slot]

        each(walkers, one)
    per = bs // PIECES
    for slot in range(slots):
        bias = jnp.zeros((walkers, chol_ref.shape[1]), F32)
        for c in range(PIECES):
            base = c * per * walkers
            left = jnp.concatenate(
                [green_ref[slot, pl.ds(base + p * walkers, walkers), :].astype(BF16) for p in range(per)],
                axis=1,
            )
            right = chol_ref[slot, :, pl.ds(c * per * bs, per * bs)]
            bias += lax.dot_general(left, right, NT, preferred_element_type=F32)
        bias_ref[slot] = bias

    if spread:
        total = sum(bias_ref[slot] for slot in range(slots))
        for o in range(owners):
            out_ref[o, :walkers, :] = total
            out_ref[o, pl.ds(walkers, 8), :] = draws_ref[...]
    else:
        out_ref[...] = bias_ref[...]


def operator_kernel(spread, *refs):
    if spread:
        bias_ref, mask_ref, chol_ref, out_ref, own_ref, shifted_ref, oper_ref = refs
    else:
        info_ref, bias_ref, fields_ref, mask_ref, chol_ref, out_ref, own_ref, shifted_ref, oper_ref = refs
    owners, walk, slots, bs, _ = out_ref.shape
    walkers = owners * walk
    gs = chol_ref.shape[1]
    me = lax.axis_index("blk")
    if spread:
        rows = walkers + 8
        bias = sum(bias_ref[pl.ds(o * rows, walkers), :] for o in range(owners))
        fields = bias_ref[pl.ds(walkers, owners, stride=rows), :]
        shifted_ref[...] = bias
        own_ref[...] = shifted_ref[pl.ds(me, 1), :]
    else:
        bias = bias_ref[...]
        fields = fields_ref[...]
        own_ref[...] = bias_ref[pl.ds(me * walk, walk), :]
    shifted_ref[...] = fields - bias
    for slot in range(slots):
        slab = 0 if spread else pl.multiple_of(info_ref[2, me * slots + slot] * gs, gs)
        left = shifted_ref[:, pl.ds(slab, gs)].astype(BF16)
        per = bs // PIECES
        for c in range(PIECES):
            right = chol_ref[slot, :, pl.ds(c * per * bs, per * bs)]
            oper = jnp.dot(left, right, preferred_element_type=F32) * STEP_ROOT
            for p in range(per):
                oper_ref[pl.ds(c * per + p, walkers, stride=bs), :] = oper[:, p * bs : (p + 1) * bs]

        def one(w, slot=slot):
            block = oper_ref[pl.ds(w * bs, bs), :]
            out_ref[w // walk, w % walk, slot] = (block * mask_ref[slot]).astype(BF16)

        each(walkers, one)


def update_kernel(where_ref, theta_ref, oper_ref, out_ref):
    owners, walk, slots, bs, _ = oper_ref.shape
    blocks = theta_ref.shape[1]
    slabs = where_ref.shape[0] // (3 * blocks)
    for w in range(walk):
        for row_block in range(blocks):
            total = theta_ref[w, row_block].astype(F32)
            for col_block in range(max(row_block - 1, 0), min(row_block + 2, blocks)):
                for slab in range(slabs):
                    s = where_ref[(slab * blocks + row_block) * 3 + col_block - row_block + 1]
                    total += jnp.dot(
                        oper_ref[s // slots, w, s % slots], theta_ref[w, col_block],
                        preferred_element_type=F32,
                    )
            out_ref[w, row_block] = total.astype(BF16)


def long_axis(theta, trial, chol, fields, tile_info, tile_count, block_size):
    owners = lax.axis_size("blk")
    walk, norb, nocc = theta.shape
    walkers = walk * owners
    slots, gs, _ = chol.shape
    nchol = fields.shape[1]
    blocks = block_size.shape[0]
    bs = norb // blocks
    slabs = nchol // gs
    spread = slabs == 1 and walk == 1
    params = pltpu.CompilerParams(vmem_limit_bytes=LIMIT)
    theta_blocks = theta.reshape(walk, blocks, bs, nocc)

    outgoing, rows, mask, draws, where = pl.pallas_call(
        pick_kernel,
        out_shape=(
            jax.ShapeDtypeStruct((owners, walk, slots, bs, nocc), BF16),
            jax.ShapeDtypeStruct((slots, bs, nocc), BF16),
            jax.ShapeDtypeStruct((slots, bs, bs), F32),
            jax.ShapeDtypeStruct((8, nchol), F32),
            jax.ShapeDtypeStruct((slabs * blocks * 3,), jnp.int32),
        ),
        in_specs=[HBM] * 7,
        out_specs=(VMEM, VMEM, VMEM, VMEM, SMEM),
        scratch_shapes=[
            pltpu.SMEM(tile_info.shape, jnp.int32),
            pltpu.SMEM(tile_count.shape, jnp.int32),
            pltpu.SMEM(block_size.shape, jnp.int32),
            pltpu.VMEM(fields.shape, F32),
            pltpu.SemaphoreType.DMA((6,)),
        ],
        compiler_params=params,
        cost_estimate=pl.CostEstimate(flops=0, bytes_accessed=4 * chol.size * 2, transcendentals=0),
        name="pick",
    )(*(pltpu.with_memory_space_constraint(x, pltpu.HBM)
        for x in (tile_info, tile_count, block_size, fields, theta_blocks, trial, chol)))
    received = lax.all_to_all(outgoing, "blk", split_axis=0, concat_axis=0, tiled=True)

    part_shape = (owners, walkers + 8, gs) if spread else (slots, walkers, gs)
    part = pl.pallas_call(
        functools.partial(bias_kernel, spread),
        out_shape=jax.ShapeDtypeStruct(part_shape, F32),
        in_specs=[VMEM] * 5,
        out_specs=VMEM,
        scratch_shapes=[
            pltpu.VMEM((slots, bs * walkers, bs), F32),
            pltpu.VMEM((slots, walkers, gs), F32),
        ],
        compiler_params=params,
        name="bias",
    )(received, rows, mask, draws, chol)

    if spread:
        bias_in = lax.all_to_all(part, "blk", split_axis=0, concat_axis=0, tiled=True)
        inputs = (bias_in.reshape(owners * (walkers + 8), gs),)
    else:
        me = lax.axis_index("blk")
        local = jnp.zeros((walkers, nchol), F32)
        for slot in range(slots):
            start = (0, tile_info[2, me * slots + slot] * gs)
            old = lax.dynamic_slice(local, start, (walkers, gs))
            local = lax.dynamic_update_slice(local, old + part[slot], start)
        inputs = (tile_info, lax.psum(local, "blk"), lax.all_gather(fields, "blk", axis=0, tiled=True))

    operators, own_bias = pl.pallas_call(
        functools.partial(operator_kernel, spread),
        out_shape=(
            jax.ShapeDtypeStruct((owners, walk, slots, bs, bs), BF16),
            jax.ShapeDtypeStruct((walk, nchol), F32),
        ),
        in_specs=([VMEM] if spread else [SMEM, VMEM, VMEM]) + [VMEM, VMEM],
        out_specs=(VMEM, VMEM),
        scratch_shapes=[
            pltpu.VMEM((walkers, nchol), F32),
            pltpu.VMEM((walkers * bs, bs), F32),
        ],
        compiler_params=params,
        name="operator",
    )(*inputs, mask, chol)
    arrived = lax.all_to_all(operators, "blk", split_axis=0, concat_axis=0, tiled=True)

    propagated = pl.pallas_call(
        update_kernel,
        out_shape=jax.ShapeDtypeStruct(theta_blocks.shape, BF16),
        in_specs=[SMEM, VMEM, VMEM],
        out_specs=VMEM,
        compiler_params=params,
        name="update",
    )(where, theta_blocks, arrived)
    return propagated.reshape(theta.shape), own_bias


def pick_pair_kernel(info_hbm, theta_hbm, other_ref, _, *refs):
    pair_refs = refs[:-3]
    info_ref, theta_ref, sems = refs[-3:]
    slots = pair_refs[0].shape[1]
    copies = [
        pltpu.make_async_copy(info_hbm, info_ref, sems.at[0]),
        pltpu.make_async_copy(theta_hbm, theta_ref, sems.at[1]),
    ]
    for copy in copies:
        copy.start()
    me = lax.axis_index("blk")
    core = me % 2
    for copy in copies:
        copy.wait()
    for r, ref in enumerate(pair_refs):
        for j in range(slots):
            block = info_ref[1, (me ^ (2 * r)) * slots + j]
            ref[core, j] = theta_ref[0, block]
            ref[1 - core, j] = other_ref[0, block]


def prepare_kernel(
    place, near_ring, info_hbm, count_hbm, size_hbm, fields_hbm, trial_ref, _,
    rows_ref, mask_ref, draws_ref, where_ref, cols_ref, info_ref, count_ref, size_ref, fields_ref, sems,
):
    slots, bs, _ = rows_ref.shape
    owners = count_ref.shape[0]
    small = [
        pltpu.make_async_copy(source, target, sems.at[n])
        for n, (source, target) in enumerate(
            [(info_hbm, info_ref), (count_hbm, count_ref), (size_hbm, size_ref), (fields_hbm, fields_ref)]
        )
    ]
    for copy in small:
        copy.start()
    me = lax.axis_index("blk")
    for copy in small:
        copy.wait()
    trial = []
    for j in range(slots):
        block = info_ref[0, me * slots + j]
        trial.append(
            pltpu.make_async_copy(
                trial_ref.at[pl.ds(pl.multiple_of(block * bs, bs), bs), :], rows_ref.at[j], sems.at[4 + j]
            )
        )
        trial[-1].start()
    first = me // len(near_ring) * len(near_ring)
    for n, k in enumerate(near_ring):
        for j in range(slots):
            cols_ref[n * slots + j] = info_ref[1, (first + k) * slots + j]
    live = count_ref[me]
    for j in range(slots):
        row_size = jnp.where(j < live, size_ref[info_ref[0, me * slots + j]], 0)
        col_size = size_ref[info_ref[1, me * slots + j]]
        rows = lax.broadcasted_iota(jnp.int32, (bs, bs), 0) < row_size
        cols = lax.broadcasted_iota(jnp.int32, (bs, bs), 1) < col_size
        mask_ref[j] = jnp.where(rows & cols, 1.0, 0.0)
    draws_ref[...] = jnp.broadcast_to(fields_ref[0:1, :], draws_ref.shape)
    for o in range(owners):
        for j in range(slots):

            @pl.when(j < count_ref[o])
            def _(s=o * slots + j, n=place[o] * slots + j):
                row_block = info_ref[0, s]
                where_ref[row_block * 3 + info_ref[1, s] - row_block + 1] = jnp.int32(n)

    for copy in trial:
        copy.wait()


def spread_far_kernel(cols_ref, theta_ref, _, out_ref):
    slots = out_ref.shape[1]
    for k in range(out_ref.shape[0]):
        for j in range(slots):
            out_ref[k, j] = theta_ref[0, cols_ref[k * slots + j]]


def bias_pair_kernel(step, ring, near_ring, rows_ref, mask_ref, draws_ref, chol_ref, far_ref, *refs):
    pair_refs = refs[:-3]
    out_ref, green_ref, total_ref = refs[-3:]
    half, slots, bs, nocc = far_ref.shape
    walkers = 2 * half
    me = lax.axis_index("blk")
    first = me // half * half
    pitch = walkers + 1
    for slot in range(slots):
        mask = mask_ref[slot]
        for blocks, start in [(ref[:, slot], 2 * r) for r, ref in enumerate(pair_refs)] + [(far_ref[:, slot], half)]:
            count = blocks.shape[0]
            green = lax.dot_general(
                rows_ref[slot], blocks.reshape(count * bs, nocc), NT, preferred_element_type=F32
            )
            for n in range(count):
                green_ref[slot, pl.ds(start + n, bs, stride=pitch), :] = green[:, n * bs : (n + 1) * bs] * mask
    per = bs // PIECES
    tall = jnp.zeros((chol_ref.shape[1], walkers), F32)
    wide = jnp.zeros((walkers, chol_ref.shape[1]), F32)
    for c in range(PIECES):
        for slot in range(slots):
            green = jnp.concatenate(
                [green_ref[slot, pl.ds((c * per + p) * pitch, walkers), :].astype(BF16) for p in range(per)],
                axis=1,
            )
            tile = chol_ref[slot, :, pl.ds(c * per * bs, per * bs)]
            if slot % 2:
                wide += lax.dot_general(green, tile, NT, preferred_element_type=F32)
            else:
                tall += lax.dot_general(tile, green, NT, preferred_element_type=F32)
    total = -(tall.T + wide)
    for n in range(walkers):
        walker = (me // 2 ^ (n // 2)) * 2 + n % 2 if n < half else (first + near_ring[n - half]) ^ step
        total_ref[pl.ds(walker, 1), :] = total[n : n + 1, :]
    total = total_ref[...]
    own = total_ref[pl.ds(me, 1), :]
    for n, o in enumerate(ring):
        out_ref[n] = total
        out_ref[n, pl.ds(me, 1), :] = jnp.where(o == me, own, own + draws_ref[0:1, :])


def operator_pair_kernel(place, shift_ref, fields_ref, mask_ref, chol_ref, out_ref, own_ref, total_ref, oper_ref):
    walkers, _, slots, bs, _ = out_ref.shape
    me = lax.axis_index("blk")
    total_ref[...] = sum(shift_ref[o] for o in range(walkers))
    own = total_ref[pl.ds(me, 1), :]
    own_ref[...] = jnp.broadcast_to(-own, own_ref.shape)
    total_ref[pl.ds(me, 1), :] = own + fields_ref[0:1, :]
    left = total_ref[...].astype(BF16)
    per = bs // PIECES
    pitch = bs + 8
    for slot in range(slots):
        for c in range(PIECES):
            right = chol_ref[slot, :, pl.ds(c * per * bs, per * bs)]
            oper = jnp.dot(left, right, preferred_element_type=F32) * STEP_ROOT
            for p in range(per):
                oper_ref[slot, pl.ds(c * per + p, walkers, stride=pitch), :] = oper[:, p * bs : (p + 1) * bs]
        for w in range(walkers):
            block = oper_ref[slot, pl.ds(w * pitch, bs), :]
            out_ref[place[w], 0, slot] = (block * mask_ref[slot]).astype(BF16)


def update_pair_kernel(where_ref, theta_ref, oper_ref, bias_ref, out_ref, own_ref):
    own_ref[...] = bias_ref[0:1, :]
    update_kernel(where_ref, theta_ref, oper_ref, out_ref)


def short_axis(theta, trial, chol, fields, tile_info, tile_count, block_size):
    owners = lax.axis_size("blk")
    _, norb, nocc = theta.shape
    slots, gs, _ = chol.shape
    blocks = block_size.shape[0]
    bs = norb // blocks
    half = owners // 2
    step = half + half // 2
    near = half // 2
    chips = [*range(1, half, 2), *range(0, half, 2)[::-1]]
    ring = [2 * chip + core for chip in chips for core in (1, 0)]
    back = [o for n in range(half) for o in (2 * chips[n] + 1, 2 * chips[(n + near) % half])]
    place = [back.index(o) for o in range(owners)]
    near_ring = [2 * chip + core for chip in range(near) for core in (1, 0)]
    params = pltpu.CompilerParams(vmem_limit_bytes=LIMIT)
    theta_blocks = theta.reshape(1, blocks, bs, nocc)

    def swap(x, step):
        return lax.ppermute(x, "blk", [(i, i ^ step) for i in range(owners)])

    def to_all(x, groups=None):
        return lax.all_to_all(x, "blk", split_axis=0, concat_axis=0, tiled=True, axis_index_groups=groups)

    def spread(pairs):
        return [pairs[0]] + [swap(pairs[r], 2 * r) for r in range(1, near)]

    hbm = functools.partial(pltpu.with_memory_space_constraint, memory_space=pltpu.HBM)
    pair_shapes = (jax.ShapeDtypeStruct((2, slots, bs, nocc), BF16),) * near
    partner = swap(theta_blocks, step)
    load = pl.CostEstimate(flops=0, bytes_accessed=8 * chol.size, transcendentals=0)
    pick = pl.pallas_call(
        pick_pair_kernel,
        out_shape=pair_shapes,
        in_specs=[HBM, HBM, VMEM, HBM],
        out_specs=(VMEM,) * near,
        scratch_shapes=[
            pltpu.SMEM(tile_info.shape, jnp.int32),
            pltpu.VMEM(theta_blocks.shape, BF16),
            pltpu.SemaphoreType.DMA((2,)),
        ],
        compiler_params=params,
        cost_estimate=load,
        name="pick",
    )
    pairs = lax.cond(
        lax.axis_index("blk") < owners,
        lambda x: pick(hbm(tile_info), hbm(x), swap(x, 1), hbm(chol)),
        lambda x: pick(hbm(tile_info), hbm(x), swap(swap(swap(x, 1), 1), 1), hbm(chol)),
        theta_blocks,
    )
    rows, mask, draws, where, cols = pl.pallas_call(
        functools.partial(prepare_kernel, place, near_ring),
        out_shape=(
            jax.ShapeDtypeStruct((slots, bs, nocc), BF16),
            jax.ShapeDtypeStruct((slots, bs, bs), F32),
            jax.ShapeDtypeStruct((8, gs), F32),
            jax.ShapeDtypeStruct((3 * blocks,), jnp.int32),
            jax.ShapeDtypeStruct((half * slots,), jnp.int32),
        ),
        in_specs=[HBM] * 6,
        out_specs=(VMEM, VMEM, VMEM, SMEM, SMEM),
        scratch_shapes=[
            pltpu.SMEM(tile_info.shape, jnp.int32),
            pltpu.SMEM(tile_count.shape, jnp.int32),
            pltpu.SMEM(block_size.shape, jnp.int32),
            pltpu.VMEM(fields.shape, F32),
            pltpu.SemaphoreType.DMA((4 + slots,)),
        ],
        compiler_params=params,
        cost_estimate=load,
        name="prepare",
    )(*map(hbm, (tile_info, tile_count, block_size, fields, trial, chol)))
    received = spread(pairs)
    far = pl.pallas_call(
        spread_far_kernel,
        out_shape=jax.ShapeDtypeStruct((half, slots, bs, nocc), BF16),
        in_specs=[SMEM, VMEM, HBM],
        out_specs=VMEM,
        compiler_params=params,
        cost_estimate=load,
        name="spread",
    )(cols, partner, hbm(chol))
    groups = [near_ring, [half + k for k in near_ring]]
    far, *received = lax.optimization_barrier((far, *received))
    far = to_all(far, groups)

    part = pl.pallas_call(
        functools.partial(bias_pair_kernel, step, ring, near_ring),
        out_shape=jax.ShapeDtypeStruct((owners, owners, gs), F32),
        in_specs=[VMEM] * (5 + near),
        out_specs=VMEM,
        scratch_shapes=[pltpu.VMEM((slots, (bs + 1) * (owners + 1), bs), F32), pltpu.VMEM((owners, gs), F32)],
        compiler_params=params,
        name="bias",
    )(rows, mask, draws, chol, far, *received)

    operators, own_bias = pl.pallas_call(
        functools.partial(operator_pair_kernel, place),
        out_shape=(
            jax.ShapeDtypeStruct((owners, 1, slots, bs, bs), BF16),
            jax.ShapeDtypeStruct((8, gs), F32),
        ),
        in_specs=[VMEM] * 4,
        out_specs=(VMEM, VMEM),
        scratch_shapes=[pltpu.VMEM((owners, gs), F32), pltpu.VMEM((slots, (owners + 1) * (bs + 8), bs), F32)],
        compiler_params=params,
        name="operator",
    )(to_all(part, [ring]), draws, mask, chol)

    propagated, own_bias = pl.pallas_call(
        update_pair_kernel,
        out_shape=(jax.ShapeDtypeStruct(theta_blocks.shape, BF16), jax.ShapeDtypeStruct((1, gs), F32)),
        in_specs=[SMEM, VMEM, VMEM, VMEM],
        out_specs=(VMEM, VMEM),
        compiler_params=params,
        name="update",
    )(where, theta_blocks, to_all(operators, [back]), own_bias)
    return propagated.reshape(theta.shape), own_bias


def per_device(theta, trial, chol, fields, tile_info, tile_count, block_size):
    short = lax.axis_size("blk") in (8, 16)
    one_slab = fields.shape[1] == chol.shape[1]
    plan = short_axis if short and one_slab and theta.shape[0] == 1 else long_axis
    return plan(theta, trial, chol, fields, tile_info, tile_count, block_size)


def solution(mesh):
    placed = (
        P(("grp", "blk"), None, None),
        P("grp", None),
        P(("grp", "blk"), None, None),
        P(("grp", "blk"), None),
        P("grp", None),
        P("grp"),
        P("grp"),
    )
    return jax.shard_map(
        per_device,
        mesh=mesh,
        in_specs=placed,
        out_specs=(P(("grp", "blk"), None, None), P(("grp", "blk"), None)),
        check_vma=False,
    )
```

```python
import functools

import jax
import jax.numpy as jnp
from jax import lax
from jax.experimental import pallas as pl
from jax.experimental.pallas import tpu as pltpu
from jax.sharding import PartitionSpec as P

STEP_ROOT = 0.25
PIECES = 8
F32 = jnp.float32
BF16 = jnp.bfloat16
LIMIT = 24 * 1024 * 1024
VMEM = pl.BlockSpec(memory_space=pltpu.VMEM)
SMEM = pl.BlockSpec(memory_space=pltpu.SMEM)
HBM = pl.BlockSpec(memory_space=pltpu.HBM)
ANY = pl.BlockSpec(memory_space=pl.ANY)
NT = (((1,), (1,)), ((), ()))


def each(count, body):
    if count <= 16:
        for index in range(count):
            body(index)
    else:

        def step(index, carry):
            body(index)
            return carry

        lax.fori_loop(0, count, step, 0, unroll=8)


def pick_kernel(
    info_hbm, count_hbm, size_hbm, fields_hbm, theta_ref, trial_ref, chol_ref,
    out_ref, rows_ref, mask_ref, draws_ref, where_ref, info_ref, count_ref, size_ref, fields_ref, sems,
):
    owners, walk, slots, bs, _ = out_ref.shape
    blocks = theta_ref.shape[1]
    small = [
        pltpu.make_async_copy(source, target, sems.at[2 + n])
        for n, (source, target) in enumerate(
            [(info_hbm, info_ref), (count_hbm, count_ref), (size_hbm, size_ref), (fields_hbm, fields_ref)]
        )
    ]
    for copy in small:
        copy.start()
    small[0].wait()
    copies = []
    for o in range(owners):
        for j in range(slots):
            block = info_ref[1, o * slots + j]
            for w in range(walk):
                copies.append(pltpu.make_async_copy(theta_ref.at[w, block], out_ref.at[o, w, j], sems.at[0]))
    me = lax.axis_index("blk")
    for j in range(slots):
        block = info_ref[0, me * slots + j]
        copies.append(
            pltpu.make_async_copy(
                trial_ref.at[pl.ds(pl.multiple_of(block * bs, bs), bs), :], rows_ref.at[j], sems.at[1]
            )
        )
    for copy in copies:
        copy.start()
    for copy in small[1:]:
        copy.wait()
    live = count_ref[me]
    for j in range(slots):
        row_size = jnp.where(j < live, size_ref[info_ref[0, me * slots + j]], 0)
        col_size = size_ref[info_ref[1, me * slots + j]]
        rows = lax.broadcasted_iota(jnp.int32, (bs, bs), 0) < row_size
        cols = lax.broadcasted_iota(jnp.int32, (bs, bs), 1) < col_size
        mask_ref[j] = jnp.where(rows & cols, 1.0, 0.0)
    draws_ref[...] = jnp.broadcast_to(fields_ref[0:1, :], draws_ref.shape)
    for o in range(owners):
        for j in range(slots):

            @pl.when(j < count_ref[o])
            def _(s=o * slots + j):
                row_block = info_ref[0, s]
                side = info_ref[1, s] - row_block + 1
                where_ref[(info_ref[2, s] * blocks + row_block) * 3 + side] = jnp.int32(s)

    pltpu.make_async_copy(out_ref, out_ref, sems.at[0]).wait()
    pltpu.make_async_copy(rows_ref, rows_ref, sems.at[1]).wait()


def bias_kernel(
    spread, recv_ref, rows_ref, mask_ref, draws_ref, chol_ref, out_ref, green_ref, bias_ref
):
    owners, walk, slots, bs, _ = recv_ref.shape
    walkers = owners * walk
    for slot in range(slots):

        def one(w, slot=slot):
            block = recv_ref[w // walk, w % walk, slot]
            green = lax.dot_general(rows_ref[slot], block, NT, preferred_element_type=F32)
            green_ref[slot, pl.ds(w, bs, stride=walkers), :] = green * mask_ref[slot]

        each(walkers, one)
    per = bs // PIECES
    for slot in range(slots):
        bias = jnp.zeros((walkers, chol_ref.shape[1]), F32)
        for c in range(PIECES):
            base = c * per * walkers
            left = jnp.concatenate(
                [green_ref[slot, pl.ds(base + p * walkers, walkers), :].astype(BF16) for p in range(per)],
                axis=1,
            )
            right = chol_ref[slot, :, pl.ds(c * per * bs, per * bs)]
            bias += lax.dot_general(left, right, NT, preferred_element_type=F32)
        bias_ref[slot] = bias

    if spread:
        total = sum(bias_ref[slot] for slot in range(slots))
        for o in range(owners):
            out_ref[o, :walkers, :] = total
            out_ref[o, pl.ds(walkers, 8), :] = draws_ref[...]
    else:
        out_ref[...] = bias_ref[...]


def operator_kernel(spread, *refs):
    if spread:
        bias_ref, mask_ref, chol_ref, out_ref, own_ref, shifted_ref, oper_ref = refs
    else:
        info_ref, bias_ref, fields_ref, mask_ref, chol_ref, out_ref, own_ref, shifted_ref, oper_ref = refs
    owners, walk, slots, bs, _ = out_ref.shape
    walkers = owners * walk
    gs = chol_ref.shape[1]
    me = lax.axis_index("blk")
    if spread:
        rows = walkers + 8
        bias = sum(bias_ref[pl.ds(o * rows, walkers), :] for o in range(owners))
        fields = bias_ref[pl.ds(walkers, owners, stride=rows), :]
        shifted_ref[...] = bias
        own_ref[...] = shifted_ref[pl.ds(me, 1), :]
    else:
        bias = bias_ref[...]
        fields = fields_ref[...]
        own_ref[...] = bias_ref[pl.ds(me * walk, walk), :]
    shifted_ref[...] = fields - bias
    for slot in range(slots):
        slab = 0 if spread else pl.multiple_of(info_ref[2, me * slots + slot] * gs, gs)
        left = shifted_ref[:, pl.ds(slab, gs)].astype(BF16)
        per = bs // PIECES
        for c in range(PIECES):
            right = chol_ref[slot, :, pl.ds(c * per * bs, per * bs)]
            oper = jnp.dot(left, right, preferred_element_type=F32) * STEP_ROOT
            for p in range(per):
                oper_ref[pl.ds(c * per + p, walkers, stride=bs), :] = oper[:, p * bs : (p + 1) * bs]

        def one(w, slot=slot):
            block = oper_ref[pl.ds(w * bs, bs), :]
            out_ref[w // walk, w % walk, slot] = (block * mask_ref[slot]).astype(BF16)

        each(walkers, one)


def update_kernel(where_ref, theta_ref, oper_ref, out_ref):
    owners, walk, slots, bs, _ = oper_ref.shape
    blocks = theta_ref.shape[1]
    slabs = where_ref.shape[0] // (3 * blocks)
    for w in range(walk):
        for row_block in range(blocks):
            total = theta_ref[w, row_block].astype(F32)
            for col_block in range(max(row_block - 1, 0), min(row_block + 2, blocks)):
                for slab in range(slabs):
                    s = where_ref[(slab * blocks + row_block) * 3 + col_block - row_block + 1]
                    total += jnp.dot(
                        oper_ref[s // slots, w, s % slots], theta_ref[w, col_block],
                        preferred_element_type=F32,
                    )
            out_ref[w, row_block] = total.astype(BF16)


def long_axis(theta, trial, chol, fields, tile_info, tile_count, block_size):
    owners = lax.axis_size("blk")
    walk, norb, nocc = theta.shape
    walkers = walk * owners
    slots, gs, _ = chol.shape
    nchol = fields.shape[1]
    blocks = block_size.shape[0]
    bs = norb // blocks
    slabs = nchol // gs
    spread = slabs == 1 and walk == 1
    params = pltpu.CompilerParams(vmem_limit_bytes=LIMIT)
    theta_blocks = theta.reshape(walk, blocks, bs, nocc)

    outgoing, rows, mask, draws, where = pl.pallas_call(
        pick_kernel,
        out_shape=(
            jax.ShapeDtypeStruct((owners, walk, slots, bs, nocc), BF16),
            jax.ShapeDtypeStruct((slots, bs, nocc), BF16),
            jax.ShapeDtypeStruct((slots, bs, bs), F32),
            jax.ShapeDtypeStruct((8, nchol), F32),
            jax.ShapeDtypeStruct((slabs * blocks * 3,), jnp.int32),
        ),
        in_specs=[HBM] * 7,
        out_specs=(VMEM, VMEM, VMEM, VMEM, SMEM),
        scratch_shapes=[
            pltpu.SMEM(tile_info.shape, jnp.int32),
            pltpu.SMEM(tile_count.shape, jnp.int32),
            pltpu.SMEM(block_size.shape, jnp.int32),
            pltpu.VMEM(fields.shape, F32),
            pltpu.SemaphoreType.DMA((6,)),
        ],
        compiler_params=params,
        cost_estimate=pl.CostEstimate(flops=0, bytes_accessed=4 * chol.size * 2, transcendentals=0),
        name="pick",
    )(*(pltpu.with_memory_space_constraint(x, pltpu.HBM)
        for x in (tile_info, tile_count, block_size, fields, theta_blocks, trial, chol)))
    received = lax.all_to_all(outgoing, "blk", split_axis=0, concat_axis=0, tiled=True)

    part_shape = (owners, walkers + 8, gs) if spread else (slots, walkers, gs)
    part = pl.pallas_call(
        functools.partial(bias_kernel, spread),
        out_shape=jax.ShapeDtypeStruct(part_shape, F32),
        in_specs=[VMEM] * 5,
        out_specs=VMEM,
        scratch_shapes=[
            pltpu.VMEM((slots, bs * walkers, bs), F32),
            pltpu.VMEM((slots, walkers, gs), F32),
        ],
        compiler_params=params,
        name="bias",
    )(received, rows, mask, draws, chol)

    if spread:
        bias_in = lax.all_to_all(part, "blk", split_axis=0, concat_axis=0, tiled=True)
        inputs = (bias_in.reshape(owners * (walkers + 8), gs),)
    else:
        me = lax.axis_index("blk")
        local = jnp.zeros((walkers, nchol), F32)
        for slot in range(slots):
            start = (0, tile_info[2, me * slots + slot] * gs)
            old = lax.dynamic_slice(local, start, (walkers, gs))
            local = lax.dynamic_update_slice(local, old + part[slot], start)
        inputs = (tile_info, lax.psum(local, "blk"), lax.all_gather(fields, "blk", axis=0, tiled=True))

    operators, own_bias = pl.pallas_call(
        functools.partial(operator_kernel, spread),
        out_shape=(
            jax.ShapeDtypeStruct((owners, walk, slots, bs, bs), BF16),
            jax.ShapeDtypeStruct((walk, nchol), F32),
        ),
        in_specs=([VMEM] if spread else [SMEM, VMEM, VMEM]) + [VMEM, VMEM],
        out_specs=(VMEM, VMEM),
        scratch_shapes=[
            pltpu.VMEM((walkers, nchol), F32),
            pltpu.VMEM((walkers * bs, bs), F32),
        ],
        compiler_params=params,
        name="operator",
    )(*inputs, mask, chol)
    arrived = lax.all_to_all(operators, "blk", split_axis=0, concat_axis=0, tiled=True)

    propagated = pl.pallas_call(
        update_kernel,
        out_shape=jax.ShapeDtypeStruct(theta_blocks.shape, BF16),
        in_specs=[SMEM, VMEM, VMEM],
        out_specs=VMEM,
        compiler_params=params,
        name="update",
    )(where, theta_blocks, arrived)
    return propagated.reshape(theta.shape), own_bias


def pick_pair_kernel(info_hbm, theta_hbm, other_ref, _, *refs):
    pair_refs = refs[:-3]
    info_ref, theta_ref, sems = refs[-3:]
    slots = pair_refs[0].shape[1]
    copies = [
        pltpu.make_async_copy(info_hbm, info_ref, sems.at[0]),
        pltpu.make_async_copy(theta_hbm, theta_ref, sems.at[1]),
    ]
    for copy in copies:
        copy.start()
    me = lax.axis_index("blk")
    core = me % 2
    for copy in copies:
        copy.wait()
    for r, ref in enumerate(pair_refs):
        for j in range(slots):
            block = info_ref[1, (me ^ (2 * r)) * slots + j]
            ref[core, j] = theta_ref[0, block]
            ref[1 - core, j] = other_ref[0, block]


def prepare_kernel(
    place, near_ring, info_hbm, count_hbm, size_hbm, fields_hbm, trial_ref, _,
    rows_ref, mask_ref, draws_ref, where_ref, cols_ref, info_ref, count_ref, size_ref, fields_ref, sems,
):
    slots, bs, _ = rows_ref.shape
    owners = count_ref.shape[0]
    small = [
        pltpu.make_async_copy(source, target, sems.at[n])
        for n, (source, target) in enumerate(
            [(info_hbm, info_ref), (count_hbm, count_ref), (size_hbm, size_ref), (fields_hbm, fields_ref)]
        )
    ]
    for copy in small:
        copy.start()
    me = lax.axis_index("blk")
    for copy in small:
        copy.wait()
    trial = []
    for j in range(slots):
        block = info_ref[0, me * slots + j]
        trial.append(
            pltpu.make_async_copy(
                trial_ref.at[pl.ds(pl.multiple_of(block * bs, bs), bs), :], rows_ref.at[j], sems.at[4 + j]
            )
        )
        trial[-1].start()
    first = me // len(near_ring) * len(near_ring)
    for n, k in enumerate(near_ring):
        for j in range(slots):
            cols_ref[n * slots + j] = info_ref[1, (first + k) * slots + j]
    live = count_ref[me]
    for j in range(slots):
        row_size = jnp.where(j < live, size_ref[info_ref[0, me * slots + j]], 0)
        col_size = size_ref[info_ref[1, me * slots + j]]
        rows = lax.broadcasted_iota(jnp.int32, (bs, bs), 0) < row_size
        cols = lax.broadcasted_iota(jnp.int32, (bs, bs), 1) < col_size
        mask_ref[j] = jnp.where(rows & cols, 1.0, 0.0)
    draws_ref[...] = jnp.broadcast_to(fields_ref[0:1, :], draws_ref.shape)
    for o in range(owners):
        for j in range(slots):

            @pl.when(j < count_ref[o])
            def _(s=o * slots + j, n=place[o] * slots + j):
                row_block = info_ref[0, s]
                where_ref[row_block * 3 + info_ref[1, s] - row_block + 1] = jnp.int32(n)

    for copy in trial:
        copy.wait()


def spread_far_kernel(cols_ref, theta_ref, _, out_ref):
    slots = out_ref.shape[1]
    for k in range(out_ref.shape[0]):
        for j in range(slots):
            out_ref[k, j] = theta_ref[0, cols_ref[k * slots + j]]


def bias_pair_kernel(step, ring, near_ring, rows_ref, mask_ref, draws_ref, chol_ref, far_ref, *refs):
    pair_refs = refs[:-3]
    out_ref, green_ref, total_ref = refs[-3:]
    half, slots, bs, nocc = far_ref.shape
    walkers = 2 * half
    me = lax.axis_index("blk")
    first = me // half * half
    pitch = walkers + 1
    for slot in range(slots):
        mask = mask_ref[slot]
        for blocks, start in [(ref[:, slot], 2 * r) for r, ref in enumerate(pair_refs)] + [(far_ref[:, slot], half)]:
            count = blocks.shape[0]
            green = lax.dot_general(
                rows_ref[slot], blocks.reshape(count * bs, nocc), NT, preferred_element_type=F32
            )
            for n in range(count):
                green_ref[slot, pl.ds(start + n, bs, stride=pitch), :] = green[:, n * bs : (n + 1) * bs] * mask
    per = bs // PIECES
    tall = jnp.zeros((chol_ref.shape[1], walkers), F32)
    wide = jnp.zeros((walkers, chol_ref.shape[1]), F32)
    for c in range(PIECES):
        for slot in range(slots):
            green = jnp.concatenate(
                [green_ref[slot, pl.ds((c * per + p) * pitch, walkers), :].astype(BF16) for p in range(per)],
                axis=1,
            )
            tile = chol_ref[slot, :, pl.ds(c * per * bs, per * bs)]
            if slot % 2:
                wide += lax.dot_general(green, tile, NT, preferred_element_type=F32)
            else:
                tall += lax.dot_general(tile, green, NT, preferred_element_type=F32)
    total = -(tall.T + wide)
    for n in range(walkers):
        walker = (me // 2 ^ (n // 2)) * 2 + n % 2 if n < half else (first + near_ring[n - half]) ^ step
        total_ref[pl.ds(walker, 1), :] = total[n : n + 1, :]
    total = total_ref[...]
    own = total_ref[pl.ds(me, 1), :]
    for n, o in enumerate(ring):
        out_ref[n] = total
        out_ref[n, pl.ds(me, 1), :] = jnp.where(o == me, own, own + draws_ref[0:1, :])


def operator_pair_kernel(place, shift_ref, fields_ref, mask_ref, chol_ref, out_ref, own_ref, total_ref, oper_ref):
    walkers, _, slots, bs, _ = out_ref.shape
    me = lax.axis_index("blk")
    total_ref[...] = sum(shift_ref[o] for o in range(walkers))
    own = total_ref[pl.ds(me, 1), :]
    own_ref[...] = jnp.broadcast_to(-own, own_ref.shape)
    total_ref[pl.ds(me, 1), :] = own + fields_ref[0:1, :]
    left = (total_ref[...] * STEP_ROOT).astype(BF16)
    per = bs // PIECES
    pitch = bs + 8
    for slot in range(slots):
        for c in range(PIECES):
            right = chol_ref[slot, :, pl.ds(c * per * bs, per * bs)]
            oper = jnp.dot(left, right, preferred_element_type=F32)
            for p in range(per):
                oper_ref[slot, pl.ds(c * per + p, walkers, stride=pitch), :] = oper[:, p * bs : (p + 1) * bs]
        for w in range(walkers):
            block = oper_ref[slot, pl.ds(w * pitch, bs), :]
            out_ref[place[w], 0, slot] = (block * mask_ref[slot]).astype(BF16)


def update_pair_kernel(where_ref, theta_ref, oper_ref, bias_ref, out_ref, own_ref):
    own_ref[...] = bias_ref[0:1, :]
    update_kernel(where_ref, theta_ref, oper_ref, out_ref)


def short_axis(theta, trial, chol, fields, tile_info, tile_count, block_size):
    owners = lax.axis_size("blk")
    _, norb, nocc = theta.shape
    slots, gs, _ = chol.shape
    blocks = block_size.shape[0]
    bs = norb // blocks
    half = owners // 2
    step = half + half // 2
    near = half // 2
    chips = [*range(1, half, 2), *range(0, half, 2)[::-1]]
    ring = [2 * chip + core for chip in chips for core in (1, 0)]
    back = [o for n in range(half) for o in (2 * chips[n] + 1, 2 * chips[(n + near) % half])]
    place = [back.index(o) for o in range(owners)]
    near_ring = [2 * chip + core for chip in range(near) for core in (1, 0)]
    params = pltpu.CompilerParams(vmem_limit_bytes=LIMIT)
    theta_blocks = theta.reshape(1, blocks, bs, nocc)

    def swap(x, step):
        return lax.ppermute(x, "blk", [(i, i ^ step) for i in range(owners)])

    def to_all(x, groups=None):
        return lax.all_to_all(x, "blk", split_axis=0, concat_axis=0, tiled=True, axis_index_groups=groups)

    def spread(pairs):
        return [pairs[0]] + [swap(pairs[r], 2 * r) for r in range(1, near)]

    hbm = functools.partial(pltpu.with_memory_space_constraint, memory_space=pltpu.HBM)
    pair_shapes = (jax.ShapeDtypeStruct((2, slots, bs, nocc), BF16),) * near
    partner = swap(theta_blocks, step)
    load = pl.CostEstimate(flops=0, bytes_accessed=8 * chol.size, transcendentals=0)
    pick = pl.pallas_call(
        pick_pair_kernel,
        out_shape=pair_shapes,
        in_specs=[HBM, HBM, VMEM, HBM],
        out_specs=(VMEM,) * near,
        scratch_shapes=[
            pltpu.SMEM(tile_info.shape, jnp.int32),
            pltpu.VMEM(theta_blocks.shape, BF16),
            pltpu.SemaphoreType.DMA((2,)),
        ],
        compiler_params=params,
        cost_estimate=load,
        name="pick",
    )
    pairs = lax.cond(
        lax.axis_index("blk") < owners,
        lambda x: pick(hbm(tile_info), hbm(x), swap(x, 1), hbm(chol)),
        lambda x: pick(hbm(tile_info), hbm(x), swap(swap(swap(x, 1), 1), 1), hbm(chol)),
        theta_blocks,
    )
    rows, mask, draws, where, cols = pl.pallas_call(
        functools.partial(prepare_kernel, place, near_ring),
        out_shape=(
            jax.ShapeDtypeStruct((slots, bs, nocc), BF16),
            jax.ShapeDtypeStruct((slots, bs, bs), F32),
            jax.ShapeDtypeStruct((8, gs), F32),
            jax.ShapeDtypeStruct((3 * blocks,), jnp.int32),
            jax.ShapeDtypeStruct((half * slots,), jnp.int32),
        ),
        in_specs=[HBM] * 6,
        out_specs=(VMEM, VMEM, VMEM, SMEM, SMEM),
        scratch_shapes=[
            pltpu.SMEM(tile_info.shape, jnp.int32),
            pltpu.SMEM(tile_count.shape, jnp.int32),
            pltpu.SMEM(block_size.shape, jnp.int32),
            pltpu.VMEM(fields.shape, F32),
            pltpu.SemaphoreType.DMA((4 + slots,)),
        ],
        compiler_params=params,
        cost_estimate=load,
        name="prepare",
    )(*map(hbm, (tile_info, tile_count, block_size, fields, trial, chol)))
    received = spread(pairs)
    far = pl.pallas_call(
        spread_far_kernel,
        out_shape=jax.ShapeDtypeStruct((half, slots, bs, nocc), BF16),
        in_specs=[SMEM, VMEM, HBM],
        out_specs=VMEM,
        compiler_params=params,
        cost_estimate=load,
        name="spread",
    )(cols, partner, hbm(chol))
    groups = [near_ring, [half + k for k in near_ring]]
    far, *received = lax.optimization_barrier((far, *received))
    far = to_all(far, groups)

    part = pl.pallas_call(
        functools.partial(bias_pair_kernel, step, ring, near_ring),
        out_shape=jax.ShapeDtypeStruct((owners, owners, gs), F32),
        in_specs=[VMEM] * (5 + near),
        out_specs=VMEM,
        scratch_shapes=[pltpu.VMEM((slots, (bs + 1) * (owners + 1), bs), F32), pltpu.VMEM((owners, gs), F32)],
        compiler_params=params,
        name="bias",
    )(rows, mask, draws, chol, far, *received)

    operators, own_bias = pl.pallas_call(
        functools.partial(operator_pair_kernel, place),
        out_shape=(
            jax.ShapeDtypeStruct((owners, 1, slots, bs, bs), BF16),
            jax.ShapeDtypeStruct((8, gs), F32),
        ),
        in_specs=[VMEM] * 4,
        out_specs=(VMEM, VMEM),
        scratch_shapes=[pltpu.VMEM((owners, gs), F32), pltpu.VMEM((slots, (owners + 1) * (bs + 8), bs), F32)],
        compiler_params=params,
        name="operator",
    )(to_all(part, [ring]), draws, mask, chol)

    propagated, own_bias = pl.pallas_call(
        update_pair_kernel,
        out_shape=(jax.ShapeDtypeStruct(theta_blocks.shape, BF16), jax.ShapeDtypeStruct((1, gs), F32)),
        in_specs=[SMEM, VMEM, VMEM, VMEM],
        out_specs=(VMEM, VMEM),
        compiler_params=params,
        name="update",
    )(where, theta_blocks, to_all(operators, [back]), own_bias)
    return propagated.reshape(theta.shape), own_bias


def per_device(theta, trial, chol, fields, tile_info, tile_count, block_size):
    short = lax.axis_size("blk") in (8, 16)
    one_slab = fields.shape[1] == chol.shape[1]
    plan = short_axis if short and one_slab and theta.shape[0] == 1 else long_axis
    return plan(theta, trial, chol, fields, tile_info, tile_count, block_size)


def solution(mesh):
    placed = (
        P(("grp", "blk"), None, None),
        P("grp", None),
        P(("grp", "blk"), None, None),
        P(("grp", "blk"), None),
        P("grp", None),
        P("grp"),
        P("grp"),
    )
    return jax.shard_map(
        per_device,
        mesh=mesh,
        in_specs=placed,
        out_specs=(P(("grp", "blk"), None, None), P(("grp", "blk"), None)),
        check_vma=False,
    )
```
